32 devices in a mesh: group: 8 (over z, x), fsdp: 4 (over y, core).
Axes of the slice: x: 2, y: 2, z: 4, core: 2. Of those that a mesh axis runs over, the one named last changes fastest.
Arguments:
- tokens: bfloat16 [2, 8, 1024, 2048], P(None, 'group', 'fsdp'), may hold values from -6 to 6
- segment_ids: int32 [2, 8, 1024], P(None, 'group', 'fsdp'), may hold values from 0 to 1023, as said below
- cotangent: bfloat16 [2, 8, 1024, 2048], P(None, 'group', 'fsdp'), may hold values from -6 to 6
- norm_gain: bfloat16 [2048], P('fsdp'), may hold values from 0.099609375 to 1.8984375
- in_weight: bfloat16 [2048, 8512], P('fsdp'), may hold values from -0.125 to 0.125
- conv_weight: bfloat16 [4, 4352], P(None, 'fsdp'), may hold values from -3 to 3
- conv_bias: bfloat16 [4352], P('fsdp'), may hold values from -3 to 3
- dt_bias: bfloat16 [64], P('fsdp'), may hold values from -5 to -2
- a_log: bfloat16 [64], P('fsdp'), may hold values from -4 to 1
- skip_d: bfloat16 [64], P('fsdp'), may hold values from 0.5 to 2
- inner_gain: bfloat16 [4096], P('fsdp'), may hold values from 0.099609375 to 1.8984375
- out_weight: bfloat16 [4096, 2048], P('fsdp'), may hold values from -0.09375 to 0.09375
Outputs:
- mixed: bfloat16 [2, 8, 1024, 2048], P(None, 'group', 'fsdp')
- grad_tokens: bfloat16 [2, 8, 1024, 2048], P(None, 'group', 'fsdp')
- grad_norm_gain: float32 [2048], P('fsdp')
- grad_in_weight: float32 [2048, 8512], P('fsdp')
- grad_conv_weight: float32 [4, 4352], P(None, 'fsdp')
- grad_conv_bias: float32 [4352], P('fsdp')
- grad_dt_bias: float32 [64], P('fsdp')
- grad_a_log: float32 [64], P('fsdp')
- grad_skip_d: float32 [64], P('fsdp')
- grad_inner_gain: float32 [4096], P('fsdp')
- grad_out_weight: float32 [4096, 2048], P('fsdp')
The draws below stay inside these ranges and needn't reach their ends.
Inputs may be any that keep to these rules, and one draw needn't show every extreme that they name: Within each sequence segment_ids never falls and equals the position of its document's first token; documents hold 200 to 2000 tokens except a sequence's last two, which may be shorter; of the 2 sequences at each index along the second dimension, one drawn from the seed is a single document.
All inputs are finite; a program needn't handle non-finite values.
Results may differ from the reference program's by a relative error of at most 0.0084.
Values may be sent and summed in bfloat16 or wider, within the bound.
No kernel may reach another device: no remote copies, remote signals or barrier semaphores. Data moves between devices by JAX's collectives and lax.ppermute only.
A program may use at most 448 MiB of HBM per device.

```python
from functools import partial
import jax
import jax.numpy as jnp
from jax import lax

D = 2048
INNER = 4096
HEADS = 64
HEADDIM = 64
STATE = 128
CONV = 4
SPAN = 256
SEQ = 1024
MICRO = 2
DOC_MIN = 200
DOC_MAX = 2000
SEQS = 8
XBC = 4352
PROJ = 8512


def draw_segment_ids(key, part):
    key = jax.random.fold_in(key, 7)
    length_key, whole_key = jax.random.split(key)
    doc_count = SEQ // DOC_MIN + 1
    lengths = jax.random.randint(length_key, (MICRO, SEQS, doc_count), DOC_MIN, DOC_MAX + 1)
    starts = jnp.cumsum(lengths, axis=-1) - lengths
    positions = jnp.arange(SEQ, dtype=jnp.int32)
    begun = starts[:, :, None, :] <= positions[None, None, :, None]
    labels = jnp.max(jnp.where(begun, starts[:, :, None, :], 0), axis=-1)
    labels = jnp.where(positions[None, None, :] == SEQ - 1, SEQ - 1, labels)
    chosen = jax.random.randint(whole_key, (SEQS,), 0, MICRO)
    single = jnp.arange(MICRO)[:, None] == chosen[None, :]
    return jnp.where(single[:, :, None], 0, labels).astype(jnp.int32)


def block_levels(own_key, dims, cuts, smallest, largest):
    level = 1.0
    for dim, blocks in cuts:
        draws = jax.random.uniform(jax.random.fold_in(jax.random.fold_in(own_key, 6), dim), (blocks,), jnp.float32, smallest / len(cuts), largest / len(cuts))
        level = level * jnp.repeat(jnp.exp(draws), dims[dim] // blocks).reshape((-1,) + (1,) * (len(dims) - 1 - dim))
    return level


def gaussian(rng, dims, scale, limit, cuts=(), kind=jnp.bfloat16):
    array = scale * jax.random.normal(rng, dims, jnp.float32)
    if cuts:
        array = array * block_levels(rng, dims, cuts, -0.22, 0.18)
    return jnp.clip(array, -limit, limit).astype(kind)


def setup_inputs(seed: int = 0) -> dict:
    arg_keys = jax.random.split(jax.random.key(seed), 13)
    tokens = gaussian(arg_keys[0], (MICRO, SEQS, SEQ, D), 1.0, 6.0, ((1, 8), (2, 4)))
    segment_ids = draw_segment_ids(jax.random.fold_in(arg_keys[12], 71), 0)
    cotangent = gaussian(arg_keys[2], (MICRO, SEQS, SEQ, D), 1.0, 6.0, ((1, 8), (2, 4)))
    norm_gain = jnp.clip(1.0 + 0.18 * jax.random.normal(arg_keys[3], (D,), jnp.float32), 0.099609375, 1.8984375).astype(jnp.bfloat16)
    in_weight = gaussian(arg_keys[4], (D, PROJ), D ** -0.5, 0.125, ((0, 4),))
    conv_weight = gaussian(arg_keys[5], (CONV, XBC), CONV ** -0.5, 3.0, ((1, 4),))
    conv_bias = gaussian(arg_keys[6], (XBC,), 0.5, 3.0, ((0, 4),))
    dt_bias = jnp.clip(-5.0 + 3.0 * jax.random.uniform(arg_keys[7], (HEADS,), jnp.float32) ** block_levels(arg_keys[7], (HEADS,), ((0, 4),), -0.2, 0.2), -5.0, -2.0).astype(jnp.bfloat16)
    a_log = jnp.clip(-4.0 + 5.0 * jax.random.uniform(arg_keys[8], (HEADS,), jnp.float32) ** block_levels(arg_keys[8], (HEADS,), ((0, 4),), -0.2, 0.2), -4.0, 1.0).astype(jnp.bfloat16)
    skip_d = jnp.clip(0.5 + 1.5 * jax.random.uniform(arg_keys[9], (HEADS,), jnp.float32) ** block_levels(arg_keys[9], (HEADS,), ((0, 4),), -0.2, 0.2), 0.5, 2.0).astype(jnp.bfloat16)
    inner_gain = jnp.clip(1.0 + 0.18 * jax.random.normal(arg_keys[10], (INNER,), jnp.float32), 0.099609375, 1.8984375).astype(jnp.bfloat16)
    out_weight = gaussian(arg_keys[11], (INNER, D), INNER ** -0.5, 0.09375, ((0, 4),))
    return dict(tokens=tokens, segment_ids=segment_ids, cotangent=cotangent, norm_gain=norm_gain, in_weight=in_weight, conv_weight=conv_weight, conv_bias=conv_bias, dt_bias=dt_bias, a_log=a_log, skip_d=skip_d, inner_gain=inner_gain, out_weight=out_weight)


EPSILON = 1e-05
HIGHEST = lax.Precision.HIGHEST

@jax.custom_vjp
def low(v):
    return lax.optimization_barrier(v.astype(jnp.bfloat16)).astype(jnp.float32)

@jax.custom_vjp
def low_back(v):
    return v

def low_keep(v):
    return (low(v), None)

def low_pass(kept, grad):
    return (grad,)

def back_keep(v):
    return (v, None)

def back_low(kept, grad):
    return (low(grad),)
low.defvjp(low_keep, low_pass)
low_back.defvjp(back_keep, back_low)

def rms_scale(values, gain):
    return values * lax.rsqrt(lax.optimization_barrier(jnp.mean(values * values, axis=-1, keepdims=True)) + EPSILON) * gain

def ssd_block(a_rate, skip_gain, carry_state, block):
    x_heads, b_input, c_output, step_size, seg_ids, positions = block
    span_start = positions[0]
    log_decay = step_size * a_rate[None, :]
    running = jnp.cumsum(log_decay, axis=0)
    by_head = running.T
    causal = positions[None, :] <= positions[:, None]
    linked = (seg_ids[:, None] == seg_ids[None, :]) & causal
    spread = by_head[:, :, None] - by_head[:, None, :]
    kernel = jnp.where(linked[None], jnp.exp(jnp.where(linked[None], spread, 0.0)), 0.0)
    gram_matrix = jnp.dot(c_output, b_input.T, precision=HIGHEST)
    mixing = gram_matrix[None] * kernel * step_size.T[:, None, :]
    inside = jnp.einsum('hts,shp->thp', mixing, x_heads, precision=HIGHEST)
    inflow = jnp.exp(running) * (seg_ids < span_start)[:, None]
    carried = jnp.einsum('tn,hpn->thp', c_output, carry_state, precision=HIGHEST) * inflow[:, :, None]
    block_out = inside + carried + skip_gain[None, :, None] * x_heads
    outflow = jnp.exp(running[-1][None, :] - running) * (seg_ids == seg_ids[-1])[:, None] * step_size
    fresh = jnp.einsum('shp,sn->hpn', x_heads * outflow[:, :, None], b_input, precision=HIGHEST)
    passing = jnp.exp(running[-1]) * (seg_ids[-1] < span_start)
    return (passing[:, None, None] * carry_state + fresh, block_out)

def layer_sequence(tok_rows, seg_ids, norm_gain, in_weight, conv_weight, conv_bias, dt_bias, a_log, skip_d, inner_gain, out_weight):
    normed_in = low(rms_scale(tok_rows, norm_gain))
    projected = low_back(jnp.dot(normed_in, in_weight, precision=HIGHEST))
    gate_branch = projected[:, :INNER]
    conv_in = low(projected[:, INNER:INNER + XBC])
    dt_raw = projected[:, INNER + XBC:]
    positions = jnp.arange(SEQ).astype(jnp.int32)
    padded = jnp.concatenate([jnp.zeros((CONV - 1, XBC), conv_in.dtype), conv_in], axis=0)
    conv_sum = conv_bias[None, :] + jnp.zeros_like(conv_in)
    for offset in range(CONV):
        visible = seg_ids <= positions - (CONV - 1) + offset
        conv_sum = conv_sum + conv_weight[offset][None, :] * padded[offset:offset + SEQ] * visible[:, None]
    activated = low(jax.nn.silu(conv_sum))
    x_heads = activated[:, :INNER].reshape(SEQ, HEADS, HEADDIM)
    b_input = activated[:, INNER:INNER + STATE]
    c_output = activated[:, INNER + STATE:]
    step_size = jax.nn.softplus(dt_raw + dt_bias[None, :])
    a_rate = -jnp.exp(a_log)
    blocks = SEQ // SPAN
    pieces = (x_heads.reshape(blocks, SPAN, HEADS, HEADDIM), b_input.reshape(blocks, SPAN, STATE), c_output.reshape(blocks, SPAN, STATE), step_size.reshape(blocks, SPAN, HEADS), seg_ids.reshape(blocks, SPAN), positions.reshape(blocks, SPAN))
    initial = jnp.zeros((HEADS, HEADDIM, STATE), x_heads.dtype)
    _, outputs = lax.scan(jax.checkpoint(partial(ssd_block, a_rate, skip_d)), initial, pieces)
    ssm_out = outputs.reshape(SEQ, INNER)
    gated_out = low_back(low(rms_scale(ssm_out * jax.nn.silu(gate_branch), inner_gain)))
    return tok_rows + jnp.dot(gated_out, out_weight, precision=HIGHEST)

def reference(tokens, segment_ids, cotangent, norm_gain, in_weight, conv_weight, conv_bias, dt_bias, a_log, skip_d, inner_gain, out_weight):
    weights = tuple((weight_arg.astype(jnp.float32) for weight_arg in (norm_gain, in_weight, conv_weight, conv_bias, dt_bias, a_log, skip_d, inner_gain, out_weight)))
    seq_count = MICRO * SEQS
    tok_rows = tokens.astype(jnp.float32).reshape(seq_count, SEQ, D)
    seg_rows = segment_ids.reshape(seq_count, SEQ)
    cot_rows = cotangent.astype(jnp.float32).reshape(seq_count, SEQ, D)

    def forward(inputs, *params):

        def per_sequence(seq_pair):
            return layer_sequence(seq_pair[0], seq_pair[1], *params)
        return lax.map(jax.checkpoint(per_sequence), (inputs, seg_rows))
    mixed_out, pullback = jax.vjp(forward, tok_rows, *weights)
    gradients = pullback(cot_rows)
    return (mixed_out.reshape(MICRO, SEQS, SEQ, D).astype(jnp.bfloat16), gradients[0].reshape(MICRO, SEQS, SEQ, D).astype(jnp.bfloat16), gradients[1], gradients[2], gradients[3], gradients[4], gradients[5], gradients[6], gradients[7], gradients[8], gradients[9])
```

```python
from functools import partial

import jax
import jax.numpy as jnp
from jax import lax
from jax.experimental import pallas as pl
from jax.experimental.pallas import tpu as pltpu
from jax.sharding import PartitionSpec as P

INNER = 4096
HEADS = 64
HEADDIM = 64
STATE = 128
CONV = 4
XBC = 4352
LANES = 128
EPSILON = 1e-05
FAR = -1e30
HIGHEST = lax.Precision.HIGHEST
VMEM = 48 * 1024 * 1024
F32 = jnp.float32
BF16 = jnp.bfloat16


def swap(value, axis, bit):
    count = lax.axis_size(axis)
    return lax.ppermute(value, axis, [(i, i ^ bit) for i in range(count)])


def bits_of(count):
    return [1 << k for k in reversed(range(count.bit_length() - 1))]


def gathered(piece):
    held = {0: piece}
    for bit in bits_of(lax.axis_size("fsdp")):
        for r, part in list(held.items()):
            held[r ^ bit] = swap(part, "fsdp", bit)
    return [held[r] for r in range(len(held))]


def swap_shared(value, bit):
    if bit == 1:
        return swap(value, "fsdp", bit)
    half = value.shape[1] // 2
    side = lax.axis_index("group") & 1
    mine = swap(lax.dynamic_slice_in_dim(value, side * half, half, 1), "fsdp", bit)
    other = swap(mine, "group", 1)
    return jnp.concatenate(
        [jnp.where(side == 0, mine, other), jnp.where(side == 0, other, mine)], axis=1
    )


def traded_shared(blocks):
    held = {r: {0: block} for r, block in enumerate(blocks)}
    for bit in bits_of(len(blocks)):
        going = [r for r in sorted(held) if r & bit]
        sources = sorted(held[going[0]])
        stacked = jnp.stack([held[r][s] for r in going for s in sources])
        got = swap_shared(stacked, bit)
        place = 0
        for r in going:
            for s in sources:
                held[r ^ bit][s ^ bit] = got[place]
                place += 1
            del held[r]
    return [held[0][s] for s in sorted(held[0])]


def traded(blocks):
    held = {r: {0: block} for r, block in enumerate(blocks)}
    for bit in bits_of(len(blocks)):
        going = [r for r in sorted(held) if r & bit]
        sources = sorted(held[going[0]])
        got = swap(jnp.stack([held[r][s] for r in going for s in sources]), "fsdp", bit)
        place = 0
        for r in going:
            for s in sources:
                held[r ^ bit][s ^ bit] = got[place]
                place += 1
            del held[r]
    return [held[0][s] for s in sorted(held[0])]


def scattered(value):
    count = value.shape[0]
    bit = 1
    while bit < count:
        pairs = value.reshape((value.shape[0] // 2, 2) + value.shape[1:])
        got = swap(pairs[:, 1].astype(BF16), "fsdp", bit)
        value = pairs[:, 0].astype(F32) + got.astype(F32)
        bit *= 2
    return value[0]


def absolute(blocks):
    own = lax.axis_index("fsdp")
    stacked = jnp.stack(blocks)
    return [
        lax.dynamic_index_in_dim(stacked, own ^ i, 0, keepdims=False) for i in range(len(blocks))
    ]


def summed(value, axis):
    for bit in bits_of(lax.axis_size(axis)):
        value = value + swap(value, axis, bit)
    return value


def lines():
    count = lax.axis_size("group")
    return [list(range(side, count, 2)) for side in (0, 1)]


def group_scatter(value):
    side = lax.axis_index("group") & 1
    away = lax.dynamic_index_in_dim(value, 1 - side, 0, keepdims=False).astype(BF16)
    keep = lax.dynamic_index_in_dim(value, side, 0, keepdims=False)
    half = (keep.astype(F32) + swap(away, "group", 1).astype(F32)).astype(BF16)
    return lax.psum_scatter(
        half, "group", scatter_dimension=0, tiled=False, axis_index_groups=lines()
    )


def group_gather(part):
    side = lax.axis_index("group") & 1
    half = lax.all_gather(part, "group", axis=0, tiled=False, axis_index_groups=lines())
    other = swap(half, "group", 1)
    return jnp.stack([jnp.where(side == 0, half, other), jnp.where(side == 0, other, half)])


def dot(a, b, contract=((1,), (0,)), precision=None):
    return lax.dot_general(a, b, (contract, ((), ())), precision=precision, preferred_element_type=F32)


def steps(dt_ref, head_ref, tri):
    raw = dt_ref[...] + head_ref[0:1, :]
    size = jnp.maximum(raw, 0.0) + jnp.log1p(jnp.exp(-jnp.abs(raw)))
    log_decay = size * head_ref[1:2, :]
    running = dot(tri, log_decay, precision=HIGHEST)
    return raw, size, log_decay, running


def forward_kernel(
    chunk,
    own_ref,
    pre_ref,
    gate_ref,
    dt_ref,
    back_ref,
    col_ref,
    row_ref,
    taps_ref,
    head_ref,
    skip_ref,
    gain_ref,
    act_ref,
    slope_ref,
    out_ref,
    gained_ref,
    enter_ref,
    stat_ref,
    state,
    window,
):
    where = pl.program_id(1)
    inner = gate_ref.shape[1]
    channels = pre_ref.shape[1]

    @pl.when(where == 0)
    def _():
        state[...] = jnp.zeros_like(state)
        window[0:8, :] = jnp.zeros((8, channels), F32)

    window[8:, :] = pre_ref[...].astype(F32)
    for at in range(0, channels, LANES):
        lanes = slice(at, at + LANES)
        total = taps_ref[4:5, lanes] + taps_ref[3:4, lanes] * window[8 : 8 + chunk, lanes]
        for back in range(1, CONV):
            total += taps_ref[3 - back : 4 - back, lanes] * (
                window[8 - back : 8 - back + chunk, lanes] * col_ref[:, back : back + 1]
            )
        sig = jax.nn.sigmoid(total)
        act_ref[:, lanes] = (total * sig).astype(BF16)
        slope_ref[:, lanes] = (sig * (1.0 + total * (1.0 - sig))).astype(BF16)
    window[0:8, :] = window[chunk : chunk + 8, :]

    start = (where * chunk).astype(F32)
    seg_col = col_ref[:, 0:1]
    seg_row = row_ref[...]
    seg_last = seg_row[:, chunk - 1 : chunk]
    down = lax.broadcasted_iota(jnp.int32, (chunk, chunk), 0)
    across = lax.broadcasted_iota(jnp.int32, (chunk, chunk), 1)
    tri = (across <= down).astype(F32)
    _, size, _, running = steps(dt_ref, head_ref, tri)
    running_t = running.T
    size_t = size.T
    b_input = act_ref[:, inner : inner + STATE]
    c_output = act_ref[:, inner + STATE :]
    gram = dot(c_output, b_input, ((1,), (1,)))
    veil = jnp.where((seg_col == seg_row) & (across <= down), 0.0, FAR)
    crossing = (seg_col < start).astype(F32)
    ending = (seg_col == seg_last).astype(F32)
    passing = (seg_last < start).astype(F32)
    last = running[chunk - 1 : chunk, :]
    low = lax.broadcasted_iota(jnp.int32, (chunk, LANES), 1) < HEADDIM
    low_row = low[0:1, :]
    squares = jnp.zeros((chunk, LANES), F32)
    products = jnp.zeros((chunk, LANES), F32)
    for pair in range(inner // LANES):
        lanes = slice(pair * LANES, (pair + 1) * LANES)
        heads = (2 * pair, 2 * pair + 1)
        x_low = act_ref[:, lanes]
        x_pair = x_low.astype(F32)
        masked = (jnp.where(low, x_pair, 0.0), jnp.where(low, 0.0, x_pair))
        run = [running[:, h : h + 1] for h in heads]
        inside = jnp.zeros((chunk, LANES), F32)
        for k, h in enumerate(heads):
            mixing = jnp.exp(run[k] - running_t[h : h + 1, :] + veil) * gram * size_t[h : h + 1, :]
            inside += dot(mixing.astype(BF16), masked[k].astype(BF16))
        run_pair = jnp.where(low, run[0], run[1])
        size_pair = jnp.where(low, size[:, heads[0] : heads[0] + 1], size[:, heads[1] : heads[1] + 1])
        last_pair = jnp.where(
            low_row, last[:, heads[0] : heads[0] + 1], last[:, heads[1] : heads[1] + 1]
        )
        entering = state[:, lanes]
        entering_low = entering.astype(BF16)
        enter_ref[:, lanes] = entering_low
        ssm = (
            inside
            + dot(c_output, entering_low) * (jnp.exp(run_pair) * crossing)
            + skip_ref[:, lanes] * x_pair
        )
        outflow = jnp.exp(last_pair - run_pair) * ending * size_pair
        fresh = dot(b_input, (x_pair * outflow).astype(BF16), ((0,), (0,)))
        state[:, lanes] = (jnp.exp(last_pair) * passing) * entering + fresh
        gate = gate_ref[:, lanes]
        gated = ssm * (gate * jax.nn.sigmoid(gate))
        gained = gated * gain_ref[:, lanes]
        out_ref[:, lanes] = ssm
        gained_ref[:, lanes] = gained.astype(BF16)
        squares += gated * gated
        products += gained * back_ref[:, lanes].astype(F32)
    stat_ref[0:1, :] = jnp.sum(squares.T, axis=0, keepdims=True)
    stat_ref[1:2, :] = jnp.sum(products.T, axis=0, keepdims=True)
    stat_ref[2:8, :] = jnp.zeros((6, chunk), F32)


def gate_kernel(
    chunk,
    own_ref,
    out_ref,
    gate_ref,
    back_ref,
    stat_ref,
    gain_ref,
    grad_ssm_ref,
    grad_gate_ref,
    gated_ref,
    grad_gain_ref,
):
    inner = gate_ref.shape[1]

    @pl.when((pl.program_id(0) == 0) & (pl.program_id(1) == 0))
    def _():
        grad_gain_ref[...] = jnp.zeros_like(grad_gain_ref)

    scale = lax.rsqrt(stat_ref[0:1, :] * (1.0 / INNER) + EPSILON)
    shift = scale * scale * scale * stat_ref[1:2, :] * (1.0 / INNER)
    scale = jnp.broadcast_to(scale, (LANES, chunk)).T
    shift = jnp.broadcast_to(shift, (LANES, chunk)).T
    for at in range(0, inner, LANES):
        lanes = slice(at, at + LANES)
        ssm = out_ref[:, lanes]
        gate = gate_ref[:, lanes]
        back = back_ref[:, lanes].astype(F32)
        sig = jax.nn.sigmoid(gate)
        silu = gate * sig
        gated = ssm * silu
        scaled = gated * scale
        gain = gain_ref[:, lanes]
        grad_gated = scale * (gain * back) - gated * shift
        grad_ssm_ref[:, lanes] = (grad_gated * silu).astype(BF16)
        grad_gate_ref[:, lanes] = (
            grad_gated * ssm * (sig * (1.0 + gate * (1.0 - sig)))
        ).astype(BF16)
        gated_ref[:, lanes] = (scaled * gain).astype(BF16)
        grad_gain_ref[0:1, lanes] += jnp.sum(scaled * back, axis=0, keepdims=True)


def backward_kernel(
    chunk,
    own_ref,
    act_ref,
    slope_ref,
    pre_ref,
    dt_ref,
    grad_ref,
    enter_ref,
    col_ref,
    row_ref,
    taps_ref,
    head_ref,
    skip_ref,
    grad_pre_ref,
    grad_dt_ref,
    grad_taps_ref,
    grad_skip_ref,
    grad_head_ref,
    leaving,
    window,
    grad_act,
    row_sums,
):
    count = pl.num_programs(1)
    where = count - 1 - pl.program_id(1)
    inner = grad_ref.shape[1]
    channels = pre_ref.shape[1]

    @pl.when(pl.program_id(1) == 0)
    def _():
        leaving[...] = jnp.zeros_like(leaving)
        window[chunk:, :] = jnp.zeros((8, channels), F32)

    @pl.when((pl.program_id(0) == 0) & (pl.program_id(1) == 0))
    def _():
        grad_taps_ref[...] = jnp.zeros_like(grad_taps_ref)
        grad_skip_ref[...] = jnp.zeros_like(grad_skip_ref)
        grad_head_ref[...] = jnp.zeros_like(grad_head_ref)
        row_sums[...] = jnp.zeros_like(row_sums)

    start = (where * chunk).astype(F32)
    seg_col = col_ref[:, 0:1]
    seg_row = row_ref[...]
    seg_last = seg_row[:, chunk - 1 : chunk]
    down = lax.broadcasted_iota(jnp.int32, (chunk, chunk), 0)
    across = lax.broadcasted_iota(jnp.int32, (chunk, chunk), 1)
    tri = (across <= down).astype(F32)
    raw, size, log_decay, running = steps(dt_ref, head_ref, tri)
    running_t = running.T
    b_input = act_ref[:, inner : inner + STATE]
    c_output = act_ref[:, inner + STATE :]
    gram = dot(b_input, c_output, ((1,), (1,)))
    veil = jnp.where((seg_col == seg_row) & (down <= across), 0.0, FAR)
    crossing = (seg_col < start).astype(F32)
    ending = (seg_col == seg_last).astype(F32)
    passing = (seg_last < start).astype(F32)
    last = running[chunk - 1 : chunk, :]
    lane = lax.broadcasted_iota(jnp.int32, (chunk, LANES), 1)
    low = lane < HEADDIM
    low_row = low[0:1, :]
    lane_row = lane[0:1, :]
    grad_gram = jnp.zeros((chunk, chunk), F32)
    grad_b = jnp.zeros((chunk, STATE), F32)
    grad_c = jnp.zeros((chunk, STATE), F32)
    size_grad = jnp.zeros((chunk, LANES), F32)
    carry_grad = jnp.zeros((chunk, LANES), F32)
    total_grad = jnp.zeros((1, LANES), F32)
    for pair in range(inner // LANES):
        lanes = slice(pair * LANES, (pair + 1) * LANES)
        heads = (2 * pair, 2 * pair + 1)
        x_pair = act_ref[:, lanes].astype(F32)
        grad_low = grad_ref[:, lanes]
        grad = grad_low.astype(F32)
        halves = (low, jnp.logical_not(low))
        run = [running[:, h : h + 1] for h in heads]
        sizes = [size[:, h : h + 1] for h in heads]
        run_pair = jnp.where(low, run[0], run[1])
        size_pair = jnp.where(low, sizes[0], sizes[1])
        last_pair = jnp.where(
            low_row, last[:, heads[0] : heads[0] + 1], last[:, heads[1] : heads[1] + 1]
        )
        entering = enter_ref[:, lanes]
        left = leaving[:, lanes]
        left_low = left.astype(BF16)
        inflow = jnp.exp(run_pair) * crossing
        outflow = jnp.exp(last_pair - run_pair) * ending
        into = grad * inflow
        into_low = into.astype(BF16)
        carried = into * dot(c_output, entering)
        fresh_back = dot(b_input, left_low) * outflow
        flown = x_pair * fresh_back
        whole = jnp.exp(last_pair) * passing
        kept = whole * jnp.sum(left * entering.astype(F32), axis=0, keepdims=True)
        kept += jnp.sum(flown * size_pair, axis=0, keepdims=True)
        leaving[:, lanes] = whole * left + dot(c_output, into_low, ((0,), (0,)))
        grad_c += dot(into_low, entering, ((1,), (1,)))
        grad_b += dot((x_pair * outflow * size_pair).astype(BF16), left_low, ((1,), (1,)))
        grad_x = fresh_back * size_pair + skip_ref[:, lanes] * grad
        for k, h in enumerate(heads):
            mine = halves[k]
            decay = jnp.exp(running_t[h : h + 1, :] - run[k] + veil)
            weight = decay * gram
            back = dot(jnp.where(mine, x_pair, 0.0).astype(BF16), grad_low, ((1,), (1,)))
            grad_x += dot(
                (weight * sizes[k]).astype(BF16), jnp.where(mine, grad, 0.0).astype(BF16)
            )
            grad_gram += back * decay * sizes[k]
            straight = back * weight
            row_sums[h : h + 1, :] = jnp.sum(straight * sizes[k], axis=0, keepdims=True)
            size_here = jnp.sum(straight, axis=1, keepdims=True) + jnp.sum(
                jnp.where(mine, flown, 0.0), axis=1, keepdims=True
            )
            carry_here = jnp.sum(jnp.where(mine, carried, 0.0), axis=1, keepdims=True)
            here = lane == h
            size_grad = jnp.where(here, size_here, size_grad)
            carry_grad = jnp.where(here, carry_here, carry_grad)
            total_here = jnp.sum(jnp.where(mine[0:1, :], kept, 0.0), axis=1, keepdims=True)
            total_grad = jnp.where(lane_row == h, total_here, total_grad)
        grad_skip_ref[0:1, lanes] += jnp.sum(grad * x_pair, axis=0, keepdims=True)
        grad_act[:, lanes] = grad_x
    grad_gram_low = grad_gram.astype(BF16)
    grad_act[:, inner : inner + STATE] = grad_b + dot(grad_gram_low, c_output)
    grad_act[:, inner + STATE :] = grad_c + dot(grad_gram_low, b_input, ((0,), (0,)))
    row_t = row_sums[...].T
    grad_run = row_t + carry_grad - size * size_grad
    upper = (across >= down).astype(F32)
    grad_decay = dot(upper, grad_run, precision=HIGHEST) + total_grad
    grad_size = grad_decay * head_ref[1:2, :] + size_grad
    grad_raw = jnp.where(lane < inner // HEADDIM, grad_size * jax.nn.sigmoid(raw), 0.0)
    grad_dt_ref[...] = grad_raw.astype(BF16)
    grad_head_ref[0:1, :] += jnp.sum(grad_raw, axis=0, keepdims=True)
    grad_head_ref[1:2, :] += jnp.sum(grad_decay * log_decay, axis=0, keepdims=True)

    for at in range(0, channels, LANES):
        lanes = slice(at, at + LANES)
        grad_sum = grad_act[:, lanes] * slope_ref[:, lanes].astype(F32)
        window[0:chunk, lanes] = grad_sum
        pre = pre_ref[:, lanes].astype(F32)
        grad_pre = taps_ref[3:4, lanes] * grad_sum
        grad_taps_ref[3:4, lanes] += jnp.sum(pre * grad_sum, axis=0, keepdims=True)
        grad_taps_ref[4:5, lanes] += jnp.sum(grad_sum, axis=0, keepdims=True)
        for ahead in range(1, CONV):
            later = window[ahead : ahead + chunk, lanes] * col_ref[:, 3 + ahead : 4 + ahead]
            grad_pre += taps_ref[3 - ahead : 4 - ahead, lanes] * later
            grad_taps_ref[3 - ahead : 4 - ahead, lanes] += jnp.sum(
                pre * later, axis=0, keepdims=True
            )
        grad_pre_ref[:, lanes] = grad_pre.astype(BF16)
    window[chunk:, :] = window[0:8, :]


def scan_calls(micro, parts, tok_count, inner):
    chunk = min(LANES, tok_count)
    per_part = tok_count // chunk
    count = parts * per_part
    channels = inner + 2 * STATE
    tokens = micro * parts * tok_count

    def blocks(flip):
        def time(step):
            return count - 1 - step if flip else step

        def place(m, step, own):
            t = time(step)
            part = lax.bitwise_xor(t // per_part, own[0])
            return ((part * micro + m) * per_part + t % per_part, 0)

        def tok(width):
            return pl.BlockSpec((chunk, width), place)

        col = pl.BlockSpec((None, chunk, 8), lambda m, step, own: (m, time(step), 0))
        row = pl.BlockSpec((None, None, 1, chunk), lambda m, step, own: (m, time(step), 0, 0))
        stat = pl.BlockSpec((None, None, 8, chunk), lambda m, step, own: (m, time(step), 0, 0))
        states = pl.BlockSpec((None, None, STATE, inner), lambda m, step, own: (m, time(step), 0, 0))

        def const(rows, width):
            return pl.BlockSpec((rows, width), lambda m, step, own: (0, 0))

        return tok, col, row, stat, states, const

    def call(kernel, flip, ins, outs, shapes, scratch, flops, moved):
        return pl.pallas_call(
            partial(kernel, chunk),
            grid_spec=pltpu.PrefetchScalarGridSpec(
                num_scalar_prefetch=1,
                grid=(micro, count),
                in_specs=ins,
                out_specs=outs,
                scratch_shapes=scratch,
            ),
            out_shape=shapes,
            compiler_params=pltpu.CompilerParams(
                dimension_semantics=("arbitrary", "arbitrary"), vmem_limit_bytes=VMEM
            ),
            cost_estimate=pl.CostEstimate(flops=flops, bytes_accessed=moved, transcendentals=0),
        )

    struct = jax.ShapeDtypeStruct
    tok, col, row, stat, states, const = blocks(False)
    forward = call(
        forward_kernel,
        False,
        [tok(channels), tok(inner), tok(LANES), tok(inner), col, row]
        + [const(8, channels), const(8, LANES), const(1, inner), const(1, inner)],
        [tok(channels), tok(channels), tok(inner), tok(inner), states, stat],
        [
            struct((tokens, channels), BF16),
            struct((tokens, channels), BF16),
            struct((tokens, inner), F32),
            struct((tokens, inner), BF16),
            struct((micro, count, STATE, inner), BF16),
            struct((micro, count, 8, chunk), F32),
        ],
        [pltpu.VMEM((STATE, inner), F32), pltpu.VMEM((chunk + 8, channels), F32)],
        tokens * inner * 8 * chunk,
        tokens * inner * 60,
    )
    gating = call(
        gate_kernel,
        False,
        [tok(inner), tok(inner), tok(inner), stat, const(1, inner)],
        [tok(inner), tok(inner), tok(inner), const(8, inner)],
        [struct((tokens, inner), BF16)] * 3 + [struct((8, inner), F32)],
        [],
        tokens * inner * 30,
        tokens * inner * 16,
    )
    tok, col, row, stat, states, const = blocks(True)
    backward = call(
        backward_kernel,
        True,
        [tok(channels), tok(channels), tok(channels), tok(LANES), tok(inner), states, col, row]
        + [const(8, channels), const(8, LANES), const(1, inner)],
        [tok(channels), tok(LANES), const(8, channels), const(8, inner), const(8, LANES)],
        [
            struct((tokens, channels), BF16),
            struct((tokens, LANES), BF16),
            struct((8, channels), F32),
            struct((8, inner), F32),
            struct((8, LANES), F32),
        ],
        [
            pltpu.VMEM((STATE, inner), F32),
            pltpu.VMEM((chunk + 8, channels), F32),
            pltpu.VMEM((chunk, channels), F32),
            pltpu.VMEM((LANES, chunk), F32),
        ],
        tokens * inner * 20 * chunk,
        tokens * inner * 100,
    )
    return forward, gating, backward


def padded(row, width):
    return jnp.pad(row, ((0, 0), (0, width - row.shape[1])))


def on_device(
    tokens,
    segment_ids,
    cotangent,
    norm_gain,
    in_weight,
    conv_weight,
    conv_bias,
    dt_bias,
    a_log,
    skip_d,
    inner_gain,
    out_weight,
):
    micro, _, tok_count, width = tokens.shape
    parts = lax.axis_size("fsdp")
    groups = lax.axis_size("group")
    own = lax.axis_index("fsdp")
    inner = INNER // parts
    heads = HEADS // parts
    channels = inner + 2 * STATE
    rows = width // parts
    seq = tok_count * parts
    tok_all = micro * seq

    taps_here = jnp.concatenate([conv_weight, conv_bias[None]], axis=0).astype(F32)
    packed = jnp.concatenate(
        [
            norm_gain.astype(F32),
            taps_here.reshape(-1),
            segment_ids.astype(F32).reshape(-1),
        ]
    )
    packed = lax.all_gather(packed, "fsdp", axis=0, tiled=False)
    cut = norm_gain.shape[0]
    gain_norm = packed[:, :cut].reshape(-1)
    taps_size = taps_here.size
    taps = packed[:, cut : cut + taps_size].reshape(parts, CONV + 1, -1)
    taps = taps.transpose(1, 0, 2).reshape(CONV + 1, XBC)
    seg = packed[:, cut + taps_size :].reshape(parts, micro, tok_count)
    seg = seg.transpose(1, 0, 2).reshape(micro, seq)
    taps = jnp.concatenate(
        [lax.dynamic_slice_in_dim(taps, own * inner, inner, 1), taps[:, INNER:]], axis=1
    )
    taps = jnp.pad(taps, ((0, 8 - CONV - 1), (0, 0)))
    times = jnp.arange(seq, dtype=F32)[None]
    cols = [seg]
    for back in range(1, CONV):
        cols.append((seg <= times - back).astype(F32))
    for ahead in range(1, CONV):
        later = jnp.pad(seg[:, ahead:], ((0, 0), (0, ahead)), constant_values=-1.0)
        cols.append((later == seg).astype(F32))
    cols.append(jnp.zeros_like(seg))
    cols = jnp.stack(cols, axis=-1)
    chunk = min(LANES, tok_count)
    seg_row = seg.reshape(micro, -1, 1, chunk)
    head_row = jnp.concatenate(
        [dt_bias.astype(F32)[None], -jnp.exp(a_log.astype(F32))[None]], axis=0
    )
    head_row = jnp.pad(head_row, ((0, 6), (0, LANES - heads)))
    skip_row = jnp.repeat(skip_d.astype(F32), HEADDIM)[None]
    gain_row = inner_gain.astype(F32)[None]

    blocks = []
    for r in range(parts):
        at = (own ^ r) * inner
        blocks.append(
            jnp.concatenate(
                [
                    lax.dynamic_slice_in_dim(in_weight, at, inner, 1),
                    lax.dynamic_slice_in_dim(in_weight, INNER + at, inner, 1),
                ],
                axis=1,
            )
        )
    tail = lax.all_gather(in_weight[:, 2 * INNER :], "fsdp", axis=0, tiled=True)
    mine = jnp.concatenate(absolute(traded_shared(blocks)), axis=0)
    weight_gate = mine[:, :inner]
    weight_xbc = jnp.concatenate([mine[:, inner:], tail[:, : 2 * STATE]], axis=1)
    weight_dt = padded(lax.dynamic_slice_in_dim(tail, 2 * STATE + own * heads, heads, 1), LANES)

    tok_rows = tokens[:, 0].astype(F32)
    inverse = lax.rsqrt(jnp.mean(tok_rows * tok_rows, axis=-1, keepdims=True) + EPSILON)
    normed = (tok_rows * inverse * gain_norm).astype(BF16)
    cot_here = cotangent[:, 0]
    normed_all = jnp.stack(gathered(normed)).reshape(tok_all, width)
    cot_all = jnp.stack(gathered(cot_here)).reshape(tok_all, width)

    gate = jnp.dot(normed_all, weight_gate, preferred_element_type=F32)
    pre = jnp.dot(normed_all, weight_xbc, preferred_element_type=F32).astype(BF16)
    dt_raw = jnp.dot(normed_all, weight_dt, preferred_element_type=F32)
    back = dot(cot_all, out_weight, ((1,), (1,))).astype(BF16)

    forward, gating, backward = scan_calls(micro, parts, tok_count, inner)
    own_arg = own.astype(jnp.int32)[None]
    act, slope, ssm, gained, entering, stat = forward(
        own_arg, pre, gate, dt_raw, back, cols, seg_row, taps, head_row, skip_row, gain_row
    )
    stat = jnp.pad(lax.psum(stat[:, :, :2], "fsdp"), ((0, 0), (0, 0), (0, 6), (0, 0)))
    grad_ssm, grad_gate, gated, grad_inner = gating(own_arg, ssm, gate, back, stat, gain_row)

    mixed = jnp.dot(gained, out_weight, preferred_element_type=F32).astype(BF16)
    mixed = scattered(mixed.reshape(parts, micro, tok_count, width))
    own_stat = lax.dynamic_slice_in_dim(
        stat[:, :, 0].reshape(micro, seq), own * tok_count, tok_count, 1
    )
    own_scale = lax.rsqrt(own_stat * (1.0 / INNER) + EPSILON)[:, :, None]
    mixed = (tok_rows + mixed * own_scale).astype(BF16)

    grad_out = dot(gated, cot_all, ((0,), (0,))).astype(BF16)
    sides = (2, groups // 2)
    grad_out = group_gather(group_scatter(grad_out.reshape(sides + (inner // groups, width))))
    grad_out = grad_out.reshape(inner, width).astype(F32)

    def in_piece(value):
        wide = value.shape[1]
        value = value.reshape((parts,) + sides + (rows // groups, wide))
        return group_scatter(value.transpose(1, 2, 0, 3, 4))

    piece_gate = in_piece(dot(normed_all, grad_gate, ((0,), (0,))).astype(BF16))
    grad_pre, grad_dt, grad_taps, grad_skip, grad_head = backward(
        own_arg,
        act,
        slope,
        pre,
        dt_raw,
        grad_ssm,
        entering,
        cols,
        seg_row,
        taps,
        head_row,
        skip_row,
    )
    grad_rest = jnp.concatenate([grad_pre, grad_dt], axis=1)
    piece_rest = in_piece(dot(normed_all, grad_rest, ((0,), (0,))).astype(BF16))

    def finish(piece):
        part = piece.shape[1]
        here = [lax.dynamic_index_in_dim(piece, own ^ r, 0, keepdims=False) for r in range(parts)]
        return jnp.stack(absolute(traded(here)), axis=1)

    gate_cols = group_gather(finish(piece_gate)).reshape(rows, INNER)
    rest = finish(piece_rest)
    shared = jnp.sum(rest[:, :, inner:channels].astype(F32), axis=1).astype(BF16)
    step_cols = rest[:, :, channels : channels + heads].reshape(-1, HEADS)
    rest = jnp.concatenate([rest[:, :, :inner].reshape(-1, INNER), shared, step_cols], axis=1)
    rest_cols = group_gather(rest).reshape(rows, -1)
    grad_in = jnp.concatenate([gate_cols, rest_cols], axis=1).astype(F32)

    weight_rest = jnp.concatenate([weight_xbc, weight_dt], axis=1)
    grad_normed = dot(grad_gate, weight_gate, ((1,), (1,))) + dot(
        grad_rest, weight_rest, ((1,), (1,))
    )
    grad_normed = scattered(grad_normed.reshape(parts, micro, tok_count, width))
    hat = tok_rows * inverse
    through = grad_normed * gain_norm
    grad_tok = inverse * (through - hat * jnp.mean(hat * through, axis=-1, keepdims=True))
    grad_tok = (cot_here.astype(F32) + grad_tok).astype(BF16)
    grad_norm = jnp.sum(grad_normed * hat, axis=(0, 1))

    taps_all = jnp.zeros((CONV + 1, XBC), F32)
    taps_all = lax.dynamic_update_slice_in_dim(
        taps_all, grad_taps[: CONV + 1, :inner], own * inner, 1
    )
    taps_all = taps_all.at[:, INNER:].set(grad_taps[: CONV + 1, inner:])
    joint = summed(jnp.concatenate([taps_all.reshape(-1), grad_norm]), "fsdp")
    skip_sum = jnp.sum(grad_skip[0].reshape(heads, HEADDIM), axis=1)
    joint = summed(
        jnp.concatenate(
            [joint, grad_inner[0], grad_head[0, :heads], grad_head[1, :heads], skip_sum]
        ),
        "group",
    )
    at = (CONV + 1) * XBC
    share = XBC // parts
    taps_all = lax.dynamic_slice_in_dim(
        joint[:at].reshape(CONV + 1, XBC), own * share, share, 1
    )
    grad_norm = lax.dynamic_slice_in_dim(joint, at + own * rows, rows, 0)
    at += width
    grad_inner = joint[at : at + inner]
    at += inner
    grad_bias, grad_rate, grad_skip = (
        joint[at + k * heads : at + (k + 1) * heads] for k in range(3)
    )
    return (
        mixed[:, None],
        grad_tok[:, None],
        grad_norm,
        grad_in,
        taps_all[:CONV],
        taps_all[CONV],
        grad_bias,
        grad_rate,
        grad_skip,
        grad_inner,
        grad_out,
    )


def solution(mesh):
    rows = P(None, "group", "fsdp", None)
    shard = P("fsdp")
    in_specs = (rows, P(None, "group", "fsdp"), rows, shard, P("fsdp", None), P(None, "fsdp"))
    in_specs += (shard,) * 5 + (P("fsdp", None),)
    out_specs = (rows, rows, shard, P("fsdp", None), P(None, "fsdp")) + (shard,) * 5
    out_specs += (P("fsdp", None),)
    return jax.shard_map(
        on_device, mesh=mesh, in_specs=in_specs, out_specs=out_specs, check_vma=False
    )
```

```python
from functools import partial

import jax
import jax.numpy as jnp
from jax import lax
from jax.experimental import pallas as pl
from jax.experimental.pallas import tpu as pltpu
from jax.sharding import PartitionSpec as P

INNER = 4096
HEADS = 64
HEADDIM = 64
STATE = 128
CONV = 4
XBC = 4352
LANES = 128
EPSILON = 1e-05
FAR = -1e30
HIGHEST = lax.Precision.HIGHEST
VMEM = 48 * 1024 * 1024
F32 = jnp.float32
BF16 = jnp.bfloat16


def swap(value, axis, bit):
    count = lax.axis_size(axis)
    return lax.ppermute(value, axis, [(i, i ^ bit) for i in range(count)])


def after(value, *earlier):
    return lax.optimization_barrier((value,) + earlier)[0] if earlier else value


def bits_of(count):
    return [1 << k for k in reversed(range(count.bit_length() - 1))]


def gather_far(piece):
    held = {0: piece}
    for bit in bits_of(lax.axis_size("fsdp"))[:-1]:
        for r, part in list(held.items()):
            held[r ^ bit] = swap(part, "fsdp", bit)
    return held


def gather_near(held, *later):
    for r, part in list(held.items()):
        held[r ^ 1] = swap(after(part, *later), "fsdp", 1)
    return [held[r] for r in range(len(held))]


def gathered(piece):
    return gather_near(gather_far(piece))


def permuted(parts, own):
    stacked = jnp.stack(parts)
    return [
        lax.dynamic_index_in_dim(stacked, own ^ i, 0, keepdims=False) for i in range(len(parts))
    ]


def absolute(parts):
    return permuted(parts, lax.axis_index("fsdp"))


def traded(blocks, send, arrived):
    held = {r: {0: block} for r, block in enumerate(blocks)}
    for bit in bits_of(len(blocks)):
        going = [r for r in sorted(held) if r & bit]
        sources = sorted(held[going[0]])
        got = send(jnp.stack([held[r][s] for r in going for s in sources]), bit)
        arrived.append(got)
        place = 0
        for r in going:
            for s in sources:
                held[r ^ bit][s ^ bit] = got[place]
                place += 1
            del held[r]
    return [held[0][s] for s in sorted(held[0])]


def traded_weights(in_rows, inner, between):
    own = lax.axis_index("fsdp")
    side = lax.axis_index("group") & 3
    rows = in_rows.shape[1]
    half = inner // 2
    parts = lax.axis_size("fsdp")

    def block(r, kind, first, size):
        at = kind * INNER + (own ^ r) * inner + first
        return lax.dynamic_slice(in_rows, (at, jnp.zeros_like(at)), (size, rows))

    def piece(r, s):
        if s in held[r]:
            return held[r][s]
        return jnp.stack([block(r, kind, 0, inner) for kind in (0, 1)]).reshape(4, half, rows)

    def quarter(r, s):
        if s in held[r]:
            return held[r][s][0]
        return block(r, side // 2, (side & 1) * half, half)

    held = {r: {} for r in range(parts)}
    sources = [0]
    pins = None
    for bit in bits_of(parts):
        going = [r for r in sorted(held) if r & bit]
        order = [(r, s) for r in going for s in sources]
        if bit > 1:
            sent = jnp.stack([quarter(r, s) for r, s in order])
            mine = swap(sent, "fsdp", bit)
            if pins is None:
                pins = between(sent, mine)
            by_x = swap(mine, "group", 1)
            by_z = swap(mine, "group", 2)
            cut = half // 2
            rest = [
                swap(after(by_z[:, :cut], *pins[0]), "group", 1),
                swap(after(by_x[:, cut:], *pins[0]), "group", 2),
            ]
            got = jnp.stack([mine, by_x, by_z, jnp.concatenate(rest, axis=1)], axis=1)
        else:
            got = [swap(after(piece(r, s), *pins[1]), "fsdp", bit) for r, s in order]
        for (r, s), part in zip(order, got):
            held[r ^ bit][s ^ bit] = part
        for r in going:
            del held[r]
        sources += [s ^ bit for s in sources]
    return [piece(0, s) for s in range(parts)]


def scattered(value, pins):
    bit = 1
    while value.shape[0] > 1:
        pairs = value.reshape((value.shape[0] // 2, 2) + value.shape[1:])
        got = swap(pairs[:, 1].astype(BF16), "fsdp", bit)
        got = after(got, *(pins[0] if pins else ()))
        pins = pins[1:]
        value = pairs[:, 0].astype(F32) + got.astype(F32)
        bit *= 2
    return value[0]


def summed(value, axis, kind=F32, pin=()):
    bits = bits_of(lax.axis_size(axis))[::-1]
    for bit in bits:
        got = swap(value.astype(kind), axis, bit)
        value = value + after(got, *(pin if bit == bits[0] else ())).astype(F32)
    return value


def lines():
    count = lax.axis_size("group")
    return [list(range(side, count, 2)) for side in (0, 1)]


class Lines:
    def __init__(self):
        self.last = None

    def order(self, value):
        return value if self.last is None else after(value, self.last)

    def scatter(self, value):
        self.last = lax.psum_scatter(
            self.order(value), "group", scatter_dimension=0, axis_index_groups=lines()
        )
        return self.last

    def gather(self, value):
        self.last = lax.all_gather(
            self.order(value), "group", axis=0, axis_index_groups=lines()
        )
        return self.last


class Chain:
    def __init__(self, part):
        self.count = lax.axis_size("group") // 2
        self.own = part
        self.up = []
        self.down = []

    def shifted(self, value, by):
        pairs = [(i, i + 2 * by) for i in range(2 * self.count) if 0 <= i + 2 * by < 2 * self.count]
        return lax.ppermute(value, "group", pairs)

    def step(self, *earlier):
        up, down = (self.up[-1], self.down[-1]) if self.up else (self.own, self.own)
        self.up.append(self.shifted(after(up, *earlier), 1))
        self.down.append(self.shifted(after(down, *earlier), -1))
        return self.up[-1], self.down[-1]

    def result(self):
        while len(self.up) < self.count - 1:
            self.step()
        place = lax.axis_index("group") // 2
        every = jnp.stack(self.down[::-1] + [self.own] + self.up)
        middle = self.count - 1
        return jnp.stack(
            [
                lax.dynamic_index_in_dim(every, middle + place - i, 0, keepdims=False)
                for i in range(self.count)
            ]
        )


def dot(a, b, contract=((1,), (0,)), precision=None):
    return lax.dot_general(a, b, (contract, ((), ())), precision=precision, preferred_element_type=F32)


def steps(dt_ref, head_ref, tri):
    raw = dt_ref[...] + head_ref[0:1, :]
    size = jnp.maximum(raw, 0.0) + jnp.log1p(jnp.exp(-jnp.abs(raw)))
    log_decay = size * head_ref[1:2, :]
    running = dot(tri, log_decay, precision=HIGHEST)
    return raw, size, log_decay, running


def columns(row, chunk):
    return jnp.broadcast_to(row, (LANES, chunk)).T


def squared(array, chunk):
    return array if chunk == LANES else array[:, :chunk]


def forward_kernel(
    chunk,
    own_ref,
    pre_ref,
    tail_ref,
    gate_ref,
    dt_ref,
    back_ref,
    row_ref,
    taps_ref,
    head_ref,
    skip_ref,
    gain_ref,
    act_ref,
    slope_ref,
    out_ref,
    gained_ref,
    enter_ref,
    stat_ref,
    state,
    window,
    carried,
    flown,
):
    where = pl.program_id(0)
    inner = gate_ref.shape[1]
    channels = act_ref.shape[1]

    @pl.when(where == 0)
    def _():
        state[...] = jnp.zeros_like(state)
        window[0:8, :] = jnp.zeros((8, channels), F32)

    start = (where * chunk).astype(F32)
    seg_row = row_ref[0:1, :]
    seg_col = columns(seg_row, chunk)
    time = lax.broadcasted_iota(jnp.int32, (chunk, LANES), 0).astype(F32) + start
    seen = [(seg_col <= time - back).astype(F32) for back in range(1, CONV)]
    window[8:, :inner] = pre_ref[...].astype(F32)
    window[8:, inner:] = tail_ref[...].astype(F32)
    for at in range(0, channels, LANES):
        lanes = slice(at, at + LANES)
        total = taps_ref[4:5, lanes] + taps_ref[3:4, lanes] * window[8 : 8 + chunk, lanes]
        for back in range(1, CONV):
            total += taps_ref[3 - back : 4 - back, lanes] * (
                window[8 - back : 8 - back + chunk, lanes] * seen[back - 1]
            )
        sig = jax.nn.sigmoid(total)
        act_ref[:, lanes] = (total * sig).astype(BF16)
        slope_ref[:, lanes] = (sig * (1.0 + total * (1.0 - sig))).astype(BF16)
    window[0:8, :] = window[chunk : chunk + 8, :]

    seg_last = seg_row[:, chunk - 1 : chunk]
    down = lax.broadcasted_iota(jnp.int32, (chunk, chunk), 0)
    across = lax.broadcasted_iota(jnp.int32, (chunk, chunk), 1)
    tri = (across <= down).astype(F32)
    _, size, _, running = steps(dt_ref, head_ref, tri)
    running_t = running.T
    size_t = size.T
    b_input = act_ref[:, inner : inner + STATE]
    c_output = act_ref[:, inner + STATE :]
    gram = dot(c_output, b_input, ((1,), (1,)))
    veil = jnp.where((squared(seg_col, chunk) == seg_row) & (across <= down), 0.0, FAR)
    crossing = (seg_col < start).astype(F32)
    ending = (seg_col == seg_last).astype(F32)
    passing = (seg_last < start).astype(F32)
    last = running[chunk - 1 : chunk, :]
    low = lax.broadcasted_iota(jnp.int32, (chunk, LANES), 1) < HEADDIM
    low_row = low[0:1, :]
    entering = state[...].astype(BF16)
    enter_ref[...] = entering
    carried[...] = dot(c_output, entering)
    squares = jnp.zeros((chunk, LANES), F32)
    products = jnp.zeros((chunk, LANES), F32)
    for pair in range(inner // LANES):
        lanes = slice(pair * LANES, (pair + 1) * LANES)
        heads = (2 * pair, 2 * pair + 1)
        x_pair = act_ref[:, lanes].astype(F32)
        run = [running[:, h : h + 1] for h in heads]
        mixing = [
            (jnp.exp(run[k] - running_t[h : h + 1, :] + veil) * gram * size_t[h : h + 1, :]).astype(
                BF16
            )
            for k, h in enumerate(heads)
        ]
        halves = [jnp.where(low, x_pair, 0.0).astype(BF16), jnp.where(low, 0.0, x_pair).astype(BF16)]
        inside = dot(jnp.concatenate(mixing, axis=1), jnp.concatenate(halves, axis=0))
        run_pair = jnp.where(low, run[0], run[1])
        size_pair = jnp.where(low, size[:, heads[0] : heads[0] + 1], size[:, heads[1] : heads[1] + 1])
        last_pair = jnp.where(
            low_row, last[:, heads[0] : heads[0] + 1], last[:, heads[1] : heads[1] + 1]
        )
        ssm = (
            inside
            + carried[:, lanes] * (jnp.exp(run_pair) * crossing)
            + skip_ref[:, lanes] * x_pair
        )
        outflow = jnp.exp(last_pair - run_pair) * ending * size_pair
        flown[:, lanes] = (x_pair * outflow).astype(BF16)
        state[:, lanes] = (jnp.exp(last_pair) * passing) * state[:, lanes]
        gate = gate_ref[:, lanes]
        gated = ssm * (gate * jax.nn.sigmoid(gate))
        out_ref[:, lanes] = ssm
        gained = gated * gain_ref[:, lanes]
        gained_ref[:, lanes] = gained.astype(BF16)
        squares += gated * gated
        products += gained * back_ref[:, lanes].astype(F32)
    state[...] += dot(b_input, flown[...], ((0,), (0,)))
    stat_ref[0:1, :] = jnp.sum(squares.T, axis=0, keepdims=True)
    stat_ref[1:2, :] = jnp.sum(products.T, axis=0, keepdims=True)
    stat_ref[2:8, :] = jnp.zeros((6, chunk), F32)


def gate_kernel(
    chunk,
    own_ref,
    out_ref,
    gate_ref,
    back_ref,
    stat_ref,
    gain_ref,
    grad_ssm_ref,
    grad_gate_ref,
    gated_ref,
    grad_gain_ref,
):
    inner = gate_ref.shape[1]

    @pl.when(pl.program_id(0) == 0)
    def _():
        grad_gain_ref[...] = jnp.zeros_like(grad_gain_ref)

    scale = lax.rsqrt(stat_ref[0:1, :] * (1.0 / INNER) + EPSILON)
    shift = scale * scale * scale * stat_ref[1:2, :] * (1.0 / INNER)
    scale = columns(scale, chunk)
    shift = columns(shift, chunk)
    for at in range(0, inner, LANES):
        lanes = slice(at, at + LANES)
        ssm = out_ref[:, lanes]
        gate = gate_ref[:, lanes]
        back = back_ref[:, lanes].astype(F32)
        sig = jax.nn.sigmoid(gate)
        silu = gate * sig
        gated = ssm * silu
        scaled = gated * scale
        gain = gain_ref[:, lanes]
        grad_gated = scale * (gain * back) - gated * shift
        grad_ssm_ref[:, lanes] = (grad_gated * silu).astype(BF16)
        grad_gate_ref[:, lanes] = (
            grad_gated * ssm * (sig * (1.0 + gate * (1.0 - sig)))
        ).astype(BF16)
        gated_ref[:, lanes] = (scaled * gain).astype(BF16)
        grad_gain_ref[0:1, lanes] += jnp.sum(scaled * back, axis=0, keepdims=True)


def backward_kernel(
    chunk,
    own_ref,
    act_ref,
    slope_ref,
    pre_ref,
    tail_ref,
    dt_ref,
    grad_ref,
    enter_ref,
    row_ref,
    taps_ref,
    head_ref,
    skip_ref,
    grad_pre_ref,
    grad_dt_ref,
    grad_taps_ref,
    grad_skip_ref,
    grad_head_ref,
    leaving,
    window,
    grad_act,
    row_sums,
    carried,
    fresh,
    into,
    flown,
):
    count = pl.num_programs(0)
    where = count - 1 - pl.program_id(0)
    inner = grad_ref.shape[1]
    channels = act_ref.shape[1]

    @pl.when(pl.program_id(0) == 0)
    def _():
        leaving[...] = jnp.zeros_like(leaving)
        window[chunk:, :] = jnp.zeros((8, channels), F32)
        grad_taps_ref[...] = jnp.zeros_like(grad_taps_ref)
        grad_skip_ref[...] = jnp.zeros_like(grad_skip_ref)
        grad_head_ref[...] = jnp.zeros_like(grad_head_ref)
        row_sums[...] = jnp.zeros_like(row_sums)

    start = (where * chunk).astype(F32)
    seg_row = row_ref[0:1, :]
    seg_col = columns(seg_row, chunk)
    seg_last = seg_row[:, chunk - 1 : chunk]
    down = lax.broadcasted_iota(jnp.int32, (chunk, chunk), 0)
    across = lax.broadcasted_iota(jnp.int32, (chunk, chunk), 1)
    tri = (across <= down).astype(F32)
    raw, size, log_decay, running = steps(dt_ref, head_ref, tri)
    running_t = running.T
    b_input = act_ref[:, inner : inner + STATE]
    c_output = act_ref[:, inner + STATE :]
    gram = dot(b_input, c_output, ((1,), (1,)))
    veil = jnp.where((squared(seg_col, chunk) == seg_row) & (down <= across), 0.0, FAR)
    crossing = (seg_col < start).astype(F32)
    ending = (seg_col == seg_last).astype(F32)
    passing = (seg_last < start).astype(F32)
    last = running[chunk - 1 : chunk, :]
    lane = lax.broadcasted_iota(jnp.int32, (chunk, LANES), 1)
    low = lane < HEADDIM
    low_row = low[0:1, :]
    lane_row = lane[0:1, :]
    left_low = leaving[...].astype(BF16)
    entering = enter_ref[...]
    carried[...] = dot(c_output, entering)
    fresh[...] = dot(b_input, left_low)
    grad_gram = jnp.zeros((chunk, chunk), F32)
    size_grad = jnp.zeros((chunk, LANES), F32)
    carry_grad = jnp.zeros((chunk, LANES), F32)
    total_grad = jnp.zeros((1, LANES), F32)
    for pair in range(inner // LANES):
        lanes = slice(pair * LANES, (pair + 1) * LANES)
        heads = (2 * pair, 2 * pair + 1)
        x_low = act_ref[:, lanes]
        x_pair = x_low.astype(F32)
        grad = grad_ref[:, lanes].astype(F32)
        halves = (low, jnp.logical_not(low))
        run = [running[:, h : h + 1] for h in heads]
        sizes = [size[:, h : h + 1] for h in heads]
        run_pair = jnp.where(low, run[0], run[1])
        size_pair = jnp.where(low, sizes[0], sizes[1])
        last_pair = jnp.where(
            low_row, last[:, heads[0] : heads[0] + 1], last[:, heads[1] : heads[1] + 1]
        )
        left = leaving[:, lanes]
        inflow = jnp.exp(run_pair) * crossing
        outflow = jnp.exp(last_pair - run_pair) * ending
        into_here = grad * inflow
        into[:, lanes] = into_here.astype(BF16)
        carry_here = into_here * carried[:, lanes]
        fresh_back = fresh[:, lanes] * outflow
        flown_here = x_pair * fresh_back
        flown[:, lanes] = (x_pair * outflow * size_pair).astype(BF16)
        whole = jnp.exp(last_pair) * passing
        kept = whole * jnp.sum(left * enter_ref[:, lanes].astype(F32), axis=0, keepdims=True)
        kept += jnp.sum(flown_here * size_pair, axis=0, keepdims=True)
        leaving[:, lanes] = whole * left
        both = jnp.concatenate(
            [jnp.where(low, grad, 0.0).astype(BF16), jnp.where(low, 0.0, grad).astype(BF16)], axis=0
        )
        back_both = dot(x_low, both, ((1,), (1,)))
        weights = []
        for k, h in enumerate(heads):
            mine = halves[k]
            decay = jnp.exp(running_t[h : h + 1, :] - run[k] + veil)
            weight = decay * gram
            weights.append((weight * sizes[k]).astype(BF16))
            back = back_both[:, k * chunk : (k + 1) * chunk]
            grad_gram += back * decay * sizes[k]
            straight = back * weight
            row_sums[h : h + 1, :] = jnp.sum(straight * sizes[k], axis=0, keepdims=True)
            flown_mine = jnp.where(mine, flown_here, 0.0)
            if chunk == LANES:
                size_here = jnp.sum(straight + flown_mine, axis=1, keepdims=True)
            else:
                size_here = jnp.sum(straight, axis=1, keepdims=True) + jnp.sum(
                    flown_mine, axis=1, keepdims=True
                )
            carry_mine = jnp.sum(jnp.where(mine, carry_here, 0.0), axis=1, keepdims=True)
            here = lane == h
            size_grad = jnp.where(here, size_here, size_grad)
            carry_grad = jnp.where(here, carry_mine, carry_grad)
            total_here = jnp.sum(jnp.where(mine[0:1, :], kept, 0.0), axis=1, keepdims=True)
            total_grad = jnp.where(lane_row == h, total_here, total_grad)
        grad_act[:, lanes] = (
            dot(jnp.concatenate(weights, axis=1), both)
            + fresh_back * size_pair
            + skip_ref[:, lanes] * grad
        )
        grad_skip_ref[0:1, lanes] += jnp.sum(grad * x_pair, axis=0, keepdims=True)
    grad_gram_low = grad_gram.astype(BF16)
    grad_act[:, inner : inner + STATE] = dot(grad_gram_low, c_output) + dot(
        flown[...], left_low, ((1,), (1,))
    )
    grad_act[:, inner + STATE :] = dot(grad_gram_low, b_input, ((0,), (0,))) + dot(
        into[...], entering, ((1,), (1,))
    )
    leaving[...] += dot(c_output, into[...], ((0,), (0,)))
    row_t = row_sums[...].T
    grad_run = row_t + carry_grad - size * size_grad
    upper = (across >= down).astype(F32)
    grad_decay = dot(upper, grad_run, precision=HIGHEST) + total_grad
    grad_size = grad_decay * head_ref[1:2, :] + size_grad
    grad_raw = jnp.where(lane < inner // HEADDIM, grad_size * jax.nn.sigmoid(raw), 0.0)
    grad_dt_ref[...] = grad_raw.astype(BF16)
    grad_head_ref[0:1, :] += jnp.sum(grad_raw, axis=0, keepdims=True)
    grad_head_ref[1:2, :] += jnp.sum(grad_decay * log_decay, axis=0, keepdims=True)

    same = [
        (columns(row_ref[ahead : ahead + 1, :], chunk) == seg_col).astype(F32)
        for ahead in range(1, CONV)
    ]
    for at in range(0, channels, LANES):
        lanes = slice(at, at + LANES)
        grad_sum = grad_act[:, lanes] * slope_ref[:, lanes].astype(F32)
        window[0:chunk, lanes] = grad_sum
        if at < inner:
            pre = pre_ref[:, lanes].astype(F32)
        else:
            pre = tail_ref[:, at - inner : at - inner + LANES].astype(F32)
        grad_pre = taps_ref[3:4, lanes] * grad_sum
        grad_taps_ref[3:4, lanes] += jnp.sum(pre * grad_sum, axis=0, keepdims=True)
        grad_taps_ref[4:5, lanes] += jnp.sum(grad_sum, axis=0, keepdims=True)
        for ahead in range(1, CONV):
            later = window[ahead : ahead + chunk, lanes] * same[ahead - 1]
            grad_pre += taps_ref[3 - ahead : 4 - ahead, lanes] * later
            grad_taps_ref[3 - ahead : 4 - ahead, lanes] += jnp.sum(
                pre * later, axis=0, keepdims=True
            )
        grad_pre_ref[:, lanes] = grad_pre.astype(BF16)
    window[chunk:, :] = window[0:8, :]


def scan_calls(parts, tok_count, inner):
    chunk = min(LANES, tok_count)
    per_part = tok_count // chunk
    count = parts * per_part
    channels = inner + 2 * STATE
    tokens = parts * tok_count

    def blocks(flip):
        def time(step):
            return count - 1 - step if flip else step

        def place(step, own):
            t = time(step)
            return lax.bitwise_xor(t // per_part, own[0]) * per_part + t % per_part

        def tok(width):
            return pl.BlockSpec((chunk, width), lambda step, own: (place(step, own), 0))

        row = pl.BlockSpec((None, 8, chunk), lambda step, own: (time(step), 0, 0))
        states = pl.BlockSpec((None, STATE, inner), lambda step, own: (time(step), 0, 0))

        def const(rows, width):
            return pl.BlockSpec((rows, width), lambda step, own: (0, 0))

        return tok, row, states, const

    def scan(kernel, ins, outs, shapes, scratch):
        return pl.pallas_call(
            partial(kernel, chunk),
            grid_spec=pltpu.PrefetchScalarGridSpec(
                num_scalar_prefetch=1,
                grid=(count,),
                in_specs=ins,
                out_specs=outs,
                scratch_shapes=scratch,
            ),
            out_shape=shapes,
            compiler_params=pltpu.CompilerParams(
                dimension_semantics=("arbitrary",), vmem_limit_bytes=VMEM
            ),
            cost_estimate=COST,
        )

    struct = jax.ShapeDtypeStruct
    tok, row, states, const = blocks(False)
    forward = scan(
        forward_kernel,
        [tok(inner), tok(2 * STATE), tok(inner), tok(LANES), tok(inner), row]
        + [const(8, channels), const(8, LANES), const(1, inner), const(1, inner)],
        [tok(channels), tok(channels), tok(inner), tok(inner), states, row],
        [
            struct((tokens, channels), BF16),
            struct((tokens, channels), BF16),
            struct((tokens, inner), F32),
            struct((tokens, inner), BF16),
            struct((count, STATE, inner), BF16),
            struct((count, 8, chunk), F32),
        ],
        [
            pltpu.VMEM((STATE, inner), F32),
            pltpu.VMEM((chunk + 8, channels), F32),
            pltpu.VMEM((chunk, inner), F32),
            pltpu.VMEM((chunk, inner), BF16),
        ],
    )
    gating = scan(
        gate_kernel,
        [tok(inner), tok(inner), tok(inner), row, const(1, inner)],
        [tok(inner), tok(inner), tok(inner), const(8, inner)],
        [struct((tokens, inner), BF16)] * 3 + [struct((8, inner), F32)],
        [],
    )
    tok, row, states, const = blocks(True)
    backward = scan(
        backward_kernel,
        [tok(channels), tok(channels), tok(inner), tok(2 * STATE), tok(LANES)]
        + [tok(inner), states, row]
        + [const(8, channels), const(8, LANES), const(1, inner)],
        [tok(channels), tok(LANES), const(8, channels), const(8, inner), const(8, LANES)],
        [
            struct((tokens, channels), BF16),
            struct((tokens, LANES), BF16),
            struct((8, channels), F32),
            struct((8, inner), F32),
            struct((8, LANES), F32),
        ],
        [
            pltpu.VMEM((STATE, inner), F32),
            pltpu.VMEM((chunk + 8, channels), F32),
            pltpu.VMEM((chunk, channels), F32),
            pltpu.VMEM((LANES, chunk), F32),
            pltpu.VMEM((chunk, inner), F32),
            pltpu.VMEM((chunk, inner), F32),
            pltpu.VMEM((chunk, inner), BF16),
            pltpu.VMEM((chunk, inner), BF16),
        ],
    )
    return forward, gating, backward


NN = ((1,), (0,))
NT = ((1,), (1,))
TN = ((0,), (0,))
COST = pl.CostEstimate(flops=1, bytes_accessed=1, transcendentals=0)


def call(kernel, grid, ins, outs, shapes, args, scratch=()):
    return pl.pallas_call(
        kernel,
        grid_spec=pltpu.PrefetchScalarGridSpec(
            num_scalar_prefetch=1,
            grid=grid,
            in_specs=ins,
            out_specs=outs,
            scratch_shapes=scratch,
        ),
        out_shape=shapes,
        compiler_params=pltpu.CompilerParams(
            dimension_semantics=("arbitrary",) * len(grid), vmem_limit_bytes=VMEM
        ),
        cost_estimate=COST,
    )(*args)


def fixed(shape):
    return pl.BlockSpec(shape, lambda i, own: (0,) * len(shape))


def own_heads(own, heads):
    head = lax.broadcasted_iota(jnp.int32, (HEADS, LANES), 0)
    lane = lax.broadcasted_iota(jnp.int32, (HEADS, LANES), 1)
    return ((head == own * heads + lane) & (lane < heads)).astype(F32)


def project_kernel(parts, own_ref, *refs):
    tok_refs, weights, tails = refs[:parts], refs[parts : 2 * parts], refs[2 * parts : 3 * parts]
    gain_ref, normed_ref, gate_ref, pre_ref, tail_ref, dt_ref, ordered = refs[3 * parts :]
    at = pl.program_id(0)
    rows = tails[0].shape[1]
    tok_count = tok_refs[0].shape[0]

    @pl.when(at == 0)
    def _():
        for r in range(parts):
            values = tok_refs[r][...].astype(F32)
            mean = jnp.mean(values * values, axis=-1, keepdims=True)
            normed_ref[r * tok_count : (r + 1) * tok_count, :] = (
                values * lax.rsqrt(mean + EPSILON) * gain_ref[...]
            ).astype(BF16)
        for s in range(parts):
            lanes = pl.ds(pl.multiple_of(lax.bitwise_xor(own_ref[0], s) * rows, LANES), rows)
            ordered[:, s * rows : (s + 1) * rows] = normed_ref[:, lanes]

    def total(refs):
        return dot(ordered[...], jnp.concatenate([ref[...] for ref in refs], axis=1), NT)

    @pl.when(at < 2)
    def _():
        gate_ref[...] = total(weights)

    @pl.when((at >= 2) & (at < 4))
    def _():
        pre_ref[...] = total(weights).astype(BF16)

    @pl.when(at == 4)
    def _():
        rest = total(tails)
        tail_ref[...] = rest[:, : 2 * STATE].astype(BF16)
        pick = own_heads(own_ref[0], HEADS // parts)
        dt_ref[...] = dot(rest[:, 2 * STATE :], pick, precision=HIGHEST)


def project(own_arg, tok_parts, weights, tails, gain):
    parts, (tok_count, width) = len(tok_parts), tok_parts[0].shape
    half, rows = weights[0].shape[1:]
    tokens = parts * tok_count

    def near(i, own):
        return (jnp.minimum(i, 3), 0, 0)

    def far(i, own):
        return (lax.bitwise_xor(jnp.minimum(i, 3), own[1]), 0, 0)

    struct = jax.ShapeDtypeStruct
    return call(
        partial(project_kernel, parts),
        (5,),
        [fixed((tok_count, width))] * parts
        + [pl.BlockSpec((None, half, rows), far if s > 1 else near) for s in range(parts)]
        + [fixed(tails[0].shape)] * parts
        + [fixed((1, width))],
        [
            fixed((tokens, width)),
            pl.BlockSpec((tokens, half), lambda i, own: (0, jnp.minimum(i, 1))),
            pl.BlockSpec((tokens, half), lambda i, own: (0, jnp.clip(i - 2, 0, 1))),
            fixed((tokens, 2 * STATE)),
            fixed((tokens, LANES)),
        ],
        [
            struct((tokens, width), BF16),
            struct((tokens, 2 * half), F32),
            struct((tokens, 2 * half), BF16),
            struct((tokens, 2 * STATE), BF16),
            struct((tokens, LANES), F32),
        ],
        (own_arg, *tok_parts, *weights, *tails, gain[None]),
        [pltpu.VMEM((tokens, width), BF16)],
    )


def back_kernel(parts, own_ref, *refs):
    weight_ref, all_ref, back_ref = refs[parts:]
    tok_count = refs[0].shape[0]

    @pl.when(pl.program_id(0) == 0)
    def _():
        for r in range(parts):
            all_ref[r * tok_count : (r + 1) * tok_count, :] = refs[r][...]

    back_ref[...] = dot(all_ref[...], weight_ref[...], NT).astype(BF16)


def project_back(own_arg, cot_parts, weight):
    parts, (tok_count, width) = len(cot_parts), cot_parts[0].shape
    inner = weight.shape[0]
    block = min(256, inner)
    tokens = parts * tok_count
    struct = jax.ShapeDtypeStruct
    return call(
        partial(back_kernel, parts),
        (inner // block,),
        [fixed((tok_count, width))] * parts
        + [pl.BlockSpec((block, width), lambda i, own: (i, 0))],
        [fixed((tokens, width)), pl.BlockSpec((tokens, block), lambda i, own: (0, i))],
        [struct((tokens, width), BF16), struct((tokens, inner), BF16)],
        (own_arg, *cot_parts, weight),
    )


def out_kernel(own_ref, a_ref, b_ref, out_ref):
    out_ref[...] = dot(a_ref[...], b_ref[...]).astype(BF16)


def project_out(own_arg, gained, weight):
    (tokens, inner), width = gained.shape, weight.shape[1]
    block = min(512, tokens)
    return call(
        out_kernel,
        (tokens // block,),
        [pl.BlockSpec((block, inner), lambda i, own: (i, 0)), fixed((inner, width))],
        [pl.BlockSpec((block, width), lambda i, own: (i, 0))],
        [jax.ShapeDtypeStruct((tokens, width), BF16)],
        (own_arg, gained, weight),
    )[0]


def into_kernel(parts, own_ref, gate_ref, pre_ref, dt_ref, *refs):
    weights, tails, out_ref = refs[:parts], refs[parts : 2 * parts], refs[-1]
    half, rows = weights[0].shape[1:]
    inner = 2 * half
    pick = own_heads(own_ref[0], HEADS // parts).astype(BF16)
    grad_dt = dot(dt_ref[...], pick, NT).astype(BF16)
    left = jnp.concatenate([gate_ref[...], pre_ref[...], grad_dt], axis=1)
    for s in range(parts):
        order = [lax.bitwise_xor(q, own_ref[1]) if s > 1 else q for q in range(4)]
        right = jnp.concatenate([weights[s][q] for q in order] + [tails[s][...]], axis=0)
        lanes = pl.ds(pl.multiple_of(lax.bitwise_xor(own_ref[0], s) * rows, LANES), rows)
        out_ref[:, lanes] = dot(left, right).astype(BF16)


def project_into(own_arg, grad_gate, grad_pre, grad_dt, weights, tails):
    parts = len(weights)
    (tokens, inner), channels = grad_gate.shape, grad_pre.shape[1]
    width = parts * weights[0].shape[2]
    block = min(512, tokens)

    def tok(size):
        return pl.BlockSpec((block, size), lambda i, own: (i, 0))

    return call(
        partial(into_kernel, parts),
        (tokens // block,),
        [tok(inner), tok(channels), tok(LANES)]
        + [fixed(w.shape) for w in weights]
        + [fixed(r.shape) for r in tails],
        [tok(width)],
        [jax.ShapeDtypeStruct((tokens, width), BF16)],
        (own_arg, grad_gate, grad_pre, grad_dt, *weights, *tails),
    )[0]


def weight_kernel(count, halves, own_ref, *refs):
    outs = refs[2 * count :]
    total = dot(refs[0][...], refs[count][...], TN)
    for m in range(1, count):
        total += dot(refs[m][...], refs[count + m][...], TN)
    if halves == 1:
        outs[0][...] = total
    else:
        first = pl.program_id(0) < pl.num_programs(0) // 2

        @pl.when(first)
        def _():
            outs[0][...] = total.astype(BF16)

        @pl.when(jnp.logical_not(first))
        def _():
            outs[1][...] = total.astype(BF16)


def weight_grad(own_arg, lefts, rights, inner):
    tokens, width = rights[0].shape
    block = min(256, inner // 2)
    per = inner // 2 // block

    def left(i, own):
        return (0, lax.bitwise_xor(i // per, 1 - (own[1] & 1)) * per + i % per)

    out = jax.ShapeDtypeStruct((inner // 2, width), BF16)
    return call(
        partial(weight_kernel, len(lefts), 2),
        (2 * per,),
        [pl.BlockSpec((tokens, block), left)] * len(lefts)
        + [fixed((tokens, width))] * len(rights),
        [
            pl.BlockSpec((block, width), lambda i, own: (jnp.minimum(i, per - 1), 0)),
            pl.BlockSpec((block, width), lambda i, own: (jnp.maximum(i - per, 0), 0)),
        ],
        [out, out],
        (own_arg, *lefts, *rights),
    )


def tail_grad(own_arg, lefts, first, rights):
    (tokens, width), columns = rights[0].shape, lefts[0].shape[1] - first
    block = LANES
    return call(
        partial(weight_kernel, len(lefts), 1),
        (columns // block,),
        [pl.BlockSpec((tokens, block), lambda i, own: (0, first // block + i))] * len(lefts)
        + [fixed((tokens, width))] * len(rights),
        [pl.BlockSpec((block, width), lambda i, own: (i, 0))],
        [jax.ShapeDtypeStruct((columns, width), F32)],
        (own_arg, *lefts, *rights),
    )[0]


def on_device(
    tokens,
    segment_ids,
    cotangent,
    norm_gain,
    in_weight,
    conv_weight,
    conv_bias,
    dt_bias,
    a_log,
    skip_d,
    inner_gain,
    out_weight,
):
    micro, _, tok_count, width = tokens.shape
    parts = lax.axis_size("fsdp")
    groups = lax.axis_size("group")
    own = lax.axis_index("fsdp")
    inner = INNER // parts
    heads = HEADS // parts
    channels = inner + 2 * STATE
    rows = width // parts
    seq = tok_count * parts
    chunk = min(LANES, tok_count)
    forward, gating, backward = scan_calls(parts, tok_count, inner)
    side = lax.axis_index("group") & 3
    own_arg = jnp.stack([own, side]).astype(jnp.int32)
    along = Lines()

    def small(sent):
        taps_here = jnp.concatenate([conv_weight, conv_bias[None]], axis=0).astype(F32)
        packed = jnp.concatenate(
            [
                norm_gain.astype(F32),
                taps_here.reshape(-1),
                segment_ids.astype(F32).reshape(-1),
            ]
        )
        held = gather_far(after(packed, sent))
        packed = jnp.stack(absolute(gather_near(held)))
        cut = norm_gain.shape[0]
        gain_norm = packed[:, :cut].reshape(-1)
        taps_size = taps_here.size
        taps = packed[:, cut : cut + taps_size].reshape(parts, CONV + 1, -1)
        taps = taps.transpose(1, 0, 2).reshape(CONV + 1, XBC)
        seg = packed[:, cut + taps_size :].reshape(parts, micro, tok_count)
        seg = seg.transpose(1, 0, 2).reshape(micro, seq)
        taps = jnp.concatenate(
            [lax.dynamic_slice_in_dim(taps, own * inner, inner, 1), taps[:, INNER:]], axis=1
        )
        taps = jnp.pad(taps, ((0, 8 - CONV - 1), (0, 0)))
        seg_rows = [seg] + [
            jnp.pad(seg[:, ahead:], ((0, 0), (0, ahead)), constant_values=-1.0)
            for ahead in range(1, CONV)
        ]
        seg_rows = jnp.stack([part.reshape(micro, -1, chunk) for part in seg_rows], axis=2)
        seg_rows = jnp.pad(seg_rows, ((0, 0), (0, 0), (0, 8 - CONV), (0, 0)))
        head_row = jnp.concatenate(
            [dt_bias.astype(F32)[None], -jnp.exp(a_log.astype(F32))[None]], axis=0
        )
        head_row = jnp.pad(head_row, ((0, 6), (0, LANES - heads)))
        skip_row = jnp.repeat(skip_d.astype(F32), HEADDIM)[None]
        gain_row = inner_gain.astype(F32)[None]
        return held[parts // 2], (gain_norm, taps, seg_rows, head_row, skip_row, gain_row)

    in_rows = in_weight.T
    started = {}

    def between(sent, got):
        packed, started["small"] = small(sent)
        started["tok"] = [gather_far(after(tokens[m, 0], got)) for m in range(micro)]
        first = started["tok"][0][parts // 2]
        last = started["tok"][-1][parts // 2]
        started["tail"] = gather_far(after(in_rows[2 * INNER :], first))
        started["cot"] = [gather_far(after(cotangent[0, 0], last))]
        return [first, packed], list(started["small"])

    weights = traded_weights(in_rows, inner, between)
    gain_norm, taps, seg_rows, head_row, skip_row, gain_row = started["small"]
    tails = gather_near(started["tail"], weights[1])
    tok_parts = [gather_near(held, weights[1]) for held in started["tok"]]

    tok_rows = tokens[:, 0].astype(F32)
    inverse = lax.rsqrt(jnp.mean(tok_rows * tok_rows, axis=-1, keepdims=True) + EPSILON)
    cot_here = cotangent[:, 0]

    projected = []
    last = started["tok"][-1][parts // 2]
    for m in range(micro):
        tok_here = [after(part, last, *[p[0] for p in projected[-1:]]) for part in tok_parts[m]]
        projected.append(project(own_arg, tok_here, weights, tails, gain_norm))
    normed_all = [p[0] for p in projected]
    for m in range(1, micro):
        started["cot"].append(
            gather_far(after(cotangent[m, 0], started["cot"][m - 1][parts // 2], normed_all[0]))
        )
    scans = []
    cot_all = []
    for m in range(micro):
        parts_here = gather_near(started["cot"][m], *(scans[m - 1][-1:] if m else normed_all[-1:]))
        cot, back = project_back(own_arg, parts_here, out_weight)
        _, gate, pre, tail, dt_raw = projected[m]
        outs = forward(
            own_arg, pre, tail, gate, dt_raw, back, seg_rows[m], taps, head_row, skip_row, gain_row
        )
        cot_all.append(cot)
        scans.append((gate, pre, tail, dt_raw, back) + tuple(outs))
    out_grads = []
    for m in range(micro):
        gate, _, _, _, back, _, _, ssm, gained, entering, stat = scans[m]
        stat = jnp.pad(summed(stat[:, :2], "fsdp"), ((0, 0), (0, 6), (0, 0)))
        out_grads.append((stat,) + tuple(gating(own_arg, ssm, gate, back, stat, gain_row)))

    def scan_back(m, *earlier):
        _, pre, tail, dt_raw, _, act, slope, _, _, entering, _ = scans[m]
        return backward(
            own_arg,
            act,
            slope,
            pre,
            tail,
            dt_raw,
            after(out_grads[m][1], *earlier),
            entering,
            seg_rows[m],
            taps,
            head_row,
            skip_row,
        )

    def across(away):
        return swap(away, "group", 1)

    def joined(keep, got):
        total = (keep.astype(F32) + got.astype(F32)).astype(BF16)
        return total.reshape(groups // 2, -1, width)

    def finish(half):
        arrived = []
        here = [lax.dynamic_slice_in_dim(half, (own ^ r) * rows, rows, 1) for r in range(parts)]
        here = traded(here, lambda value, bit: swap(value, "fsdp", bit), arrived)
        return jnp.stack(absolute(here)), arrived

    def by_part(value):
        return value.reshape(parts, tok_count, width)

    away_gate, keep_gate = weight_grad(own_arg, [g[2] for g in out_grads], normed_all, inner)
    got_gate = across(away_gate)
    gated = [after(g[3], keep_gate) for g in out_grads]
    away_out, keep_out = weight_grad(own_arg, gated, cot_all, inner)
    got_out = across(away_out)
    backs = [scan_back(0, keep_out)]
    mixed = [project_out(own_arg, after(scans[0][8], backs[0][0]), out_weight)]
    half_gate = joined(keep_gate, after(got_gate, mixed[0]))
    for m in range(1, micro):
        backs.append(scan_back(m, half_gate, *mixed[-1:]))
        mixed.append(project_out(own_arg, after(scans[m][8], backs[m][0]), out_weight))
    half_gate = along.scatter(half_gate)
    half_out = joined(keep_out, after(got_out, mixed[-1], half_gate))
    left = [after(b[0], half_out) for b in backs]
    away_x, keep_x = weight_grad(own_arg, left, normed_all, inner)
    got_x = across(away_x)
    half_out = along.scatter(half_out)
    gate_cols, arrived = finish(half_gate)

    def project_in(m, *earlier):
        grad_gate = after(out_grads[m][2], *earlier)
        return project_into(own_arg, grad_gate, *backs[m][:2], weights, tails)

    into = [project_in(0, keep_x, arrived[0])]
    chains = [Chain(gate_cols), Chain(half_out)]
    rights = [after(n, into[0], gate_cols, half_out) for n in normed_all]
    grad_tail = jnp.concatenate(
        [
            tail_grad(own_arg, [b[0] for b in backs], inner, rights),
            tail_grad(own_arg, [b[1] for b in backs], 0, rights),
        ],
        axis=0,
    )
    sent = [chains[0].step(keep_x)]
    into += [project_in(m, grad_tail, *sent[0], *into[-1:]) for m in range(1, micro)]
    chains[0].step(into[-1])
    chains[1].step(grad_tail)
    half_x = joined(keep_x, after(got_x, grad_tail, *into))
    for chain in (chains[0], chains[1], chains[1]):
        chain.step(half_x)
    mixed[0] = scattered(by_part(mixed[0]), [[backs[-1][0]], [keep_x]])
    mixed[1:] = [scattered(by_part(v), [[keep_x], [grad_tail]]) for v in mixed[1:]]
    into_sums = [
        scattered(by_part(v), [[grad_tail if m == 0 else half_x], [half_x]])
        for m, v in enumerate(into)
    ]
    step_part = lax.dynamic_update_slice_in_dim(
        jnp.zeros((HEADS, width), F32), grad_tail[2 * STATE : 2 * STATE + heads], own * heads, 0
    )
    grad_tail = jnp.concatenate([grad_tail[: 2 * STATE], step_part], axis=0)
    grad_tail = jnp.stack(
        [lax.dynamic_slice_in_dim(grad_tail, (own ^ r) * rows, rows, 1) for r in range(parts)]
    )
    grad_tail = scattered(grad_tail, [[into[-1]], [half_x]])
    scattered_x = along.scatter(half_x)
    half_x = scattered_x
    gate_lines = chains[0].result()
    out_lines = chains[1].result()
    x_lines = along.gather(finish(half_x)[0])
    grad_tail = summed(grad_tail, "group", BF16, [x_lines])

    def placed(whole, lines, kind, side):
        lines = lines.transpose(1, 0, 2, 3).reshape(parts, inner // 2, rows).astype(F32)
        for f in range(parts):
            at = kind * INNER + f * inner + side * (inner // 2)
            whole = lax.dynamic_update_slice(whole, lines[f], (at, jnp.zeros_like(at)))
        return whole

    lane = lax.axis_index("group") & 1
    got_lines = across(gate_lines)
    got_out = across(out_lines)
    got_x = across(x_lines)
    whole = jnp.zeros((2 * INNER + 2 * STATE + HEADS, rows), F32)
    whole = placed(whole, gate_lines, 0, lane)
    whole = placed(whole, after(got_lines, x_lines), 0, 1 - lane)
    whole = placed(whole, x_lines, 1, lane)
    whole = lax.dynamic_update_slice_in_dim(whole, grad_tail, 2 * INNER, 0)
    grad_in = placed(whole, got_x, 1, 1 - lane).T
    grad_out = jnp.stack(
        [
            jnp.where(lane == 0, out_lines, got_out),
            jnp.where(lane == 0, got_out, out_lines),
        ]
    )
    grad_out = grad_out.reshape(inner, width).astype(F32)

    for m in range(micro):
        stat = lax.dynamic_slice_in_dim(
            out_grads[m][0][:, 0].reshape(seq), own * tok_count, tok_count, 0
        )
        scale = lax.rsqrt(stat * (1.0 / INNER) + EPSILON)[:, None]
        mixed[m] = (tok_rows[m] + mixed[m] * scale).astype(BF16)

    grad_tok = []
    grad_norm = jnp.zeros((width,), F32)
    for m in range(micro):
        part = into_sums[m]
        hat = tok_rows[m] * inverse[m]
        through = part * gain_norm
        here = inverse[m] * (through - hat * jnp.mean(hat * through, axis=-1, keepdims=True))
        grad_tok.append((cot_here[m].astype(F32) + here).astype(BF16))
        grad_norm += jnp.sum(part * hat, axis=0)

    grad_taps = sum(b[2] for b in backs)[: CONV + 1]
    grad_skip = sum(b[3] for b in backs)[0]
    grad_head = sum(b[4] for b in backs)
    grad_inner = sum(g[4] for g in out_grads)[0]
    taps_all = lax.dynamic_update_slice_in_dim(
        jnp.zeros((CONV + 1, XBC), F32), grad_taps[:, :inner], own * inner, 1
    )
    taps_all = taps_all.at[:, INNER:].set(grad_taps[:, inner:])
    joint = summed(jnp.concatenate([taps_all.reshape(-1), grad_norm]), "fsdp")
    skip_sum = jnp.sum(grad_skip.reshape(heads, HEADDIM), axis=1)
    joint = summed(
        jnp.concatenate([joint, grad_inner, grad_head[0, :heads], grad_head[1, :heads], skip_sum]),
        "group",
        pin=[x_lines],
    )
    at = (CONV + 1) * XBC
    share = XBC // parts
    taps_all = lax.dynamic_slice_in_dim(joint[:at].reshape(CONV + 1, XBC), own * share, share, 1)
    grad_norm = lax.dynamic_slice_in_dim(joint, at + own * rows, rows, 0)
    at += width
    grad_inner = joint[at : at + inner]
    at += inner
    grad_bias, grad_rate, grad_skip = (
        joint[at + k * heads : at + (k + 1) * heads] for k in range(3)
    )
    return (
        jnp.stack(mixed)[:, None],
        jnp.stack(grad_tok)[:, None],
        grad_norm,
        grad_in,
        taps_all[:CONV],
        taps_all[CONV],
        grad_bias,
        grad_rate,
        grad_skip,
        grad_inner,
        grad_out,
    )


def solution(mesh):
    rows = P(None, "group", "fsdp", None)
    shard = P("fsdp")
    in_specs = (rows, P(None, "group", "fsdp"), rows, shard, P("fsdp", None), P(None, "fsdp"))
    in_specs += (shard,) * 5 + (P("fsdp", None),)
    out_specs = (rows, rows, shard, P("fsdp", None), P(None, "fsdp")) + (shard,) * 5
    out_specs += (P("fsdp", None),)
    return jax.shard_map(
        on_device, mesh=mesh, in_specs=in_specs, out_specs=out_specs, check_vma=False
    )
```

```python
from functools import partial

import jax
import jax.numpy as jnp
from jax import lax
from jax.experimental import pallas as pl
from jax.experimental.pallas import tpu as pltpu
from jax.sharding import PartitionSpec as P

INNER = 4096
HEADS = 64
HEADDIM = 64
STATE = 128
CONV = 4
XBC = 4352
LANES = 128
EPSILON = 1e-05
FAR = -1e30
HIGHEST = lax.Precision.HIGHEST
VMEM = 48 * 1024 * 1024
F32 = jnp.float32
BF16 = jnp.bfloat16


def swap(value, axis, bit):
    count = lax.axis_size(axis)
    with jax.named_scope(f"{axis}_{bit}"):
        return lax.ppermute(value, axis, [(i, i ^ bit) for i in range(count)])


def after(value, *earlier):
    return lax.optimization_barrier((value,) + earlier)[0] if earlier else value


def bits_of(count):
    return [1 << k for k in reversed(range(count.bit_length() - 1))]


def gather_far(piece):
    held = {0: piece}
    for bit in bits_of(lax.axis_size("fsdp"))[:-1]:
        for r, part in list(held.items()):
            held[r ^ bit] = swap(part, "fsdp", bit)
    return held


def gather_near(held, *later):
    for r, part in list(held.items()):
        held[r ^ 1] = swap(after(part, *later), "fsdp", 1)
    return [held[r] for r in range(len(held))]


def gathered(piece):
    return gather_near(gather_far(piece))


def permuted(parts, own):
    stacked = jnp.stack(parts)
    return [
        lax.dynamic_index_in_dim(stacked, own ^ i, 0, keepdims=False) for i in range(len(parts))
    ]


def absolute(parts):
    return permuted(parts, lax.axis_index("fsdp"))


def traded(blocks, send):
    held = {r: {0: block} for r, block in enumerate(blocks)}
    for bit in bits_of(len(blocks)):
        going = [r for r in sorted(held) if r & bit]
        sources = sorted(held[going[0]])
        got = send(jnp.stack([held[r][s] for r in going for s in sources]), bit)
        place = 0
        for r in going:
            for s in sources:
                held[r ^ bit][s ^ bit] = got[place]
                place += 1
            del held[r]
    return [held[0][s] for s in sorted(held[0])]


def traded_weights(in_rows, inner, between):
    own = lax.axis_index("fsdp")
    side = lax.axis_index("group") & 3
    rows = in_rows.shape[1]
    half = inner // 2
    parts = lax.axis_size("fsdp")

    def block(r, kind, first, size):
        at = kind * INNER + (own ^ r) * inner + first
        return lax.dynamic_slice(in_rows, (at, jnp.zeros_like(at)), (size, rows))

    def piece(r, s):
        if s in held[r]:
            return held[r][s]
        return jnp.stack([block(r, kind, 0, inner) for kind in (0, 1)]).reshape(4, half, rows)

    def quarter(r, s):
        if s in held[r]:
            return held[r][s][0]
        return block(r, side // 2, (side & 1) * half, half)

    held = {r: {} for r in range(parts)}
    sources = [0]
    pins = None
    for bit in bits_of(parts):
        going = [r for r in sorted(held) if r & bit]
        order = [(r, s) for r in going for s in sources]
        if bit > 1:
            sent = jnp.stack([quarter(r, s) for r, s in order])
            mine = swap(sent, "fsdp", bit)
            if pins is None:
                pins = between(sent, mine)
            by_x = swap(mine, "group", 1)
            by_z = swap(mine, "group", 2)
            cut = half // 2
            rest = [
                swap(after(by_z[:, :cut], *pins[0]), "group", 1),
                swap(after(by_x[:, cut:], *pins[0]), "group", 2),
            ]
            got = jnp.stack([mine, by_x, by_z, jnp.concatenate(rest, axis=1)], axis=1)
        else:
            got = [swap(after(piece(r, s), *pins[1]), "fsdp", bit) for r, s in order]
        for (r, s), part in zip(order, got):
            held[r ^ bit][s ^ bit] = part
        for r in going:
            del held[r]
        sources += [s ^ bit for s in sources]
    return [piece(0, s) for s in range(parts)]


def scattered(value):
    bit = 1
    while value.shape[0] > 1:
        pairs = value.reshape((value.shape[0] // 2, 2) + value.shape[1:])
        got = swap(pairs[:, 1].astype(BF16), "fsdp", bit)
        value = pairs[:, 0].astype(F32) + got.astype(F32)
        bit *= 2
    return value[0]


def summed(value, axis, kind=F32):
    for bit in bits_of(lax.axis_size(axis))[::-1]:
        value = value + swap(value.astype(kind), axis, bit).astype(F32)
    return value


def lines():
    count = lax.axis_size("group")
    return [list(range(side, count, 2)) for side in (0, 1)]


class Lines:
    def __init__(self):
        self.last = None

    def order(self, value):
        return value if self.last is None else after(value, self.last)

    def scatter(self, value, among=None):
        self.last = lax.psum_scatter(
            self.order(value), "group", scatter_dimension=0, axis_index_groups=among
        )
        return self.last

    def gather(self, value, among=None):
        self.last = lax.all_gather(
            self.order(value), "group", axis=0, axis_index_groups=among
        )
        return self.last


def dot(a, b, contract=((1,), (0,)), precision=None):
    return lax.dot_general(a, b, (contract, ((), ())), precision=precision, preferred_element_type=F32)


def steps(dt_ref, head_ref, tri):
    raw = dt_ref[...] + head_ref[0:1, :]
    size = jnp.maximum(raw, 0.0) + jnp.log1p(jnp.exp(-jnp.abs(raw)))
    log_decay = size * head_ref[1:2, :]
    running = dot(tri, log_decay, precision=HIGHEST)
    return raw, size, log_decay, running


def columns(row, chunk):
    return jnp.broadcast_to(row, (LANES, chunk)).T


def squared(array, chunk):
    return array if chunk == LANES else array[:, :chunk]


def forward_kernel(
    chunk,
    own_ref,
    pre_ref,
    tail_ref,
    gate_ref,
    dt_ref,
    back_ref,
    row_ref,
    taps_ref,
    head_ref,
    skip_ref,
    gain_ref,
    act_ref,
    slope_ref,
    out_ref,
    gained_ref,
    enter_ref,
    stat_ref,
    state,
    window,
    carried,
    flown,
):
    where = pl.program_id(0)
    inner = gate_ref.shape[1]
    channels = act_ref.shape[1]

    @pl.when(where == 0)
    def _():
        state[...] = jnp.zeros_like(state)
        window[0:8, :] = jnp.zeros((8, channels), F32)

    start = (where * chunk).astype(F32)
    seg_row = row_ref[0:1, :]
    seg_col = columns(seg_row, chunk)
    time = lax.broadcasted_iota(jnp.int32, (chunk, LANES), 0).astype(F32) + start
    seen = [(seg_col <= time - back).astype(F32) for back in range(1, CONV)]
    window[8:, :inner] = pre_ref[...].astype(F32)
    window[8:, inner:] = tail_ref[...].astype(F32)
    for at in range(0, channels, LANES):
        lanes = slice(at, at + LANES)
        total = taps_ref[4:5, lanes] + taps_ref[3:4, lanes] * window[8 : 8 + chunk, lanes]
        for back in range(1, CONV):
            total += taps_ref[3 - back : 4 - back, lanes] * (
                window[8 - back : 8 - back + chunk, lanes] * seen[back - 1]
            )
        sig = jax.nn.sigmoid(total)
        act_ref[:, lanes] = (total * sig).astype(BF16)
        slope_ref[:, lanes] = (sig * (1.0 + total * (1.0 - sig))).astype(BF16)
    window[0:8, :] = window[chunk : chunk + 8, :]

    seg_last = seg_row[:, chunk - 1 : chunk]
    down = lax.broadcasted_iota(jnp.int32, (chunk, chunk), 0)
    across = lax.broadcasted_iota(jnp.int32, (chunk, chunk), 1)
    tri = (across <= down).astype(F32)
    _, size, _, running = steps(dt_ref, head_ref, tri)
    running_t = running.T
    size_t = size.T
    b_input = act_ref[:, inner : inner + STATE]
    c_output = act_ref[:, inner + STATE :]
    gram = dot(c_output, b_input, ((1,), (1,)))
    veil = jnp.where((squared(seg_col, chunk) == seg_row) & (across <= down), 0.0, FAR)
    crossing = (seg_col < start).astype(F32)
    ending = (seg_col == seg_last).astype(F32)
    passing = (seg_last < start).astype(F32)
    last = running[chunk - 1 : chunk, :]
    low = lax.broadcasted_iota(jnp.int32, (chunk, LANES), 1) < HEADDIM
    low_row = low[0:1, :]
    entering = state[...].astype(BF16)
    enter_ref[...] = entering
    carried[...] = dot(c_output, entering)
    squares = jnp.zeros((chunk, LANES), F32)
    products = jnp.zeros((chunk, LANES), F32)
    for pair in range(inner // LANES):
        lanes = slice(pair * LANES, (pair + 1) * LANES)
        heads = (2 * pair, 2 * pair + 1)
        x_pair = act_ref[:, lanes].astype(F32)
        run = [running[:, h : h + 1] for h in heads]
        mixing = [
            (jnp.exp(run[k] - running_t[h : h + 1, :] + veil) * gram * size_t[h : h + 1, :]).astype(
                BF16
            )
            for k, h in enumerate(heads)
        ]
        halves = [jnp.where(low, x_pair, 0.0).astype(BF16), jnp.where(low, 0.0, x_pair).astype(BF16)]
        inside = dot(jnp.concatenate(mixing, axis=1), jnp.concatenate(halves, axis=0))
        run_pair = jnp.where(low, run[0], run[1])
        size_pair = jnp.where(low, size[:, heads[0] : heads[0] + 1], size[:, heads[1] : heads[1] + 1])
        last_pair = jnp.where(
            low_row, last[:, heads[0] : heads[0] + 1], last[:, heads[1] : heads[1] + 1]
        )
        ssm = (
            inside
            + carried[:, lanes] * (jnp.exp(run_pair) * crossing)
            + skip_ref[:, lanes] * x_pair
        )
        outflow = jnp.exp(last_pair - run_pair) * ending * size_pair
        flown[:, lanes] = (x_pair * outflow).astype(BF16)
        state[:, lanes] = (jnp.exp(last_pair) * passing) * state[:, lanes]
        gate = gate_ref[:, lanes]
        gated = ssm * (gate * jax.nn.sigmoid(gate))
        out_ref[:, lanes] = ssm
        gained = gated * gain_ref[:, lanes]
        gained_ref[:, lanes] = gained.astype(BF16)
        squares += gated * gated
        products += gained * back_ref[:, lanes].astype(F32)
    state[...] += dot(b_input, flown[...], ((0,), (0,)))
    stat_ref[0:1, :] = jnp.sum(squares.T, axis=0, keepdims=True)
    stat_ref[1:2, :] = jnp.sum(products.T, axis=0, keepdims=True)
    stat_ref[2:8, :] = jnp.zeros((6, chunk), F32)


def backward_kernel(
    chunk,
    own_ref,
    act_ref,
    slope_ref,
    pre_ref,
    tail_ref,
    dt_ref,
    grad_ref,
    enter_ref,
    row_ref,
    taps_ref,
    head_ref,
    skip_ref,
    grad_pre_ref,
    grad_dt_ref,
    grad_taps_ref,
    grad_skip_ref,
    grad_head_ref,
    leaving,
    window,
    grad_act,
    row_sums,
    carried,
    fresh,
    into,
    flown,
):
    count = pl.num_programs(0)
    where = count - 1 - pl.program_id(0)
    inner = grad_ref.shape[1]
    channels = act_ref.shape[1]

    @pl.when(pl.program_id(0) == 0)
    def _():
        leaving[...] = jnp.zeros_like(leaving)
        window[chunk:, :] = jnp.zeros((8, channels), F32)
        grad_taps_ref[...] = jnp.zeros_like(grad_taps_ref)
        grad_skip_ref[...] = jnp.zeros_like(grad_skip_ref)
        grad_head_ref[...] = jnp.zeros_like(grad_head_ref)
        row_sums[...] = jnp.zeros_like(row_sums)

    start = (where * chunk).astype(F32)
    seg_row = row_ref[0:1, :]
    seg_col = columns(seg_row, chunk)
    seg_last = seg_row[:, chunk - 1 : chunk]
    down = lax.broadcasted_iota(jnp.int32, (chunk, chunk), 0)
    across = lax.broadcasted_iota(jnp.int32, (chunk, chunk), 1)
    tri = (across <= down).astype(F32)
    raw, size, log_decay, running = steps(dt_ref, head_ref, tri)
    running_t = running.T
    b_input = act_ref[:, inner : inner + STATE]
    c_output = act_ref[:, inner + STATE :]
    gram = dot(b_input, c_output, ((1,), (1,)))
    veil = jnp.where((squared(seg_col, chunk) == seg_row) & (down <= across), 0.0, FAR)
    crossing = (seg_col < start).astype(F32)
    ending = (seg_col == seg_last).astype(F32)
    passing = (seg_last < start).astype(F32)
    last = running[chunk - 1 : chunk, :]
    lane = lax.broadcasted_iota(jnp.int32, (chunk, LANES), 1)
    low = lane < HEADDIM
    low_row = low[0:1, :]
    lane_row = lane[0:1, :]
    left_low = leaving[...].astype(BF16)
    entering = enter_ref[...]
    carried[...] = dot(c_output, entering)
    fresh[...] = dot(b_input, left_low)
    grad_gram = jnp.zeros((chunk, chunk), F32)
    size_grad = jnp.zeros((chunk, LANES), F32)
    carry_grad = jnp.zeros((chunk, LANES), F32)
    total_grad = jnp.zeros((1, LANES), F32)
    for pair in range(inner // LANES):
        lanes = slice(pair * LANES, (pair + 1) * LANES)
        heads = (2 * pair, 2 * pair + 1)
        x_low = act_ref[:, lanes]
        x_pair = x_low.astype(F32)
        grad = grad_ref[:, lanes].astype(F32)
        halves = (low, jnp.logical_not(low))
        run = [running[:, h : h + 1] for h in heads]
        sizes = [size[:, h : h + 1] for h in heads]
        run_pair = jnp.where(low, run[0], run[1])
        size_pair = jnp.where(low, sizes[0], sizes[1])
        last_pair = jnp.where(
            low_row, last[:, heads[0] : heads[0] + 1], last[:, heads[1] : heads[1] + 1]
        )
        left = leaving[:, lanes]
        inflow = jnp.exp(run_pair) * crossing
        outflow = jnp.exp(last_pair - run_pair) * ending
        into_here = grad * inflow
        into[:, lanes] = into_here.astype(BF16)
        carry_here = into_here * carried[:, lanes]
        fresh_back = fresh[:, lanes] * outflow
        flown_here = x_pair * fresh_back
        flown[:, lanes] = (x_pair * outflow * size_pair).astype(BF16)
        whole = jnp.exp(last_pair) * passing
        kept = whole * jnp.sum(left * enter_ref[:, lanes].astype(F32), axis=0, keepdims=True)
        kept += jnp.sum(flown_here * size_pair, axis=0, keepdims=True)
        leaving[:, lanes] = whole * left
        both = jnp.concatenate(
            [jnp.where(low, grad, 0.0).astype(BF16), jnp.where(low, 0.0, grad).astype(BF16)], axis=0
        )
        back_both = dot(x_low, both, ((1,), (1,)))
        weights = []
        for k, h in enumerate(heads):
            mine = halves[k]
            decay = jnp.exp(running_t[h : h + 1, :] - run[k] + veil)
            weight = decay * gram
            weights.append((weight * sizes[k]).astype(BF16))
            back = back_both[:, k * chunk : (k + 1) * chunk]
            grad_gram += back * decay * sizes[k]
            straight = back * weight
            row_sums[h : h + 1, :] = jnp.sum(straight * sizes[k], axis=0, keepdims=True)
            flown_mine = jnp.where(mine, flown_here, 0.0)
            if chunk == LANES:
                size_here = jnp.sum(straight + flown_mine, axis=1, keepdims=True)
            else:
                size_here = jnp.sum(straight, axis=1, keepdims=True) + jnp.sum(
                    flown_mine, axis=1, keepdims=True
                )
            carry_mine = jnp.sum(jnp.where(mine, carry_here, 0.0), axis=1, keepdims=True)
            here = lane == h
            size_grad = jnp.where(here, size_here, size_grad)
            carry_grad = jnp.where(here, carry_mine, carry_grad)
            total_here = jnp.sum(jnp.where(mine[0:1, :], kept, 0.0), axis=1, keepdims=True)
            total_grad = jnp.where(lane_row == h, total_here, total_grad)
        grad_act[:, lanes] = (
            dot(jnp.concatenate(weights, axis=1), both)
            + fresh_back * size_pair
            + skip_ref[:, lanes] * grad
        )
        grad_skip_ref[0:1, lanes] += jnp.sum(grad * x_pair, axis=0, keepdims=True)
    grad_gram_low = grad_gram.astype(BF16)
    grad_act[:, inner : inner + STATE] = dot(grad_gram_low, c_output) + dot(
        flown[...], left_low, ((1,), (1,))
    )
    grad_act[:, inner + STATE :] = dot(grad_gram_low, b_input, ((0,), (0,))) + dot(
        into[...], entering, ((1,), (1,))
    )
    leaving[...] += dot(c_output, into[...], ((0,), (0,)))
    row_t = row_sums[...].T
    grad_run = row_t + carry_grad - size * size_grad
    upper = (across >= down).astype(F32)
    grad_decay = dot(upper, grad_run, precision=HIGHEST) + total_grad
    grad_size = grad_decay * head_ref[1:2, :] + size_grad
    grad_raw = jnp.where(lane < inner // HEADDIM, grad_size * jax.nn.sigmoid(raw), 0.0)
    grad_dt_ref[...] = grad_raw.astype(BF16)
    grad_head_ref[0:1, :] += jnp.sum(grad_raw, axis=0, keepdims=True)
    grad_head_ref[1:2, :] += jnp.sum(grad_decay * log_decay, axis=0, keepdims=True)

    same = [
        (columns(row_ref[ahead : ahead + 1, :], chunk) == seg_col).astype(F32)
        for ahead in range(1, CONV)
    ]
    for at in range(0, channels, LANES):
        lanes = slice(at, at + LANES)
        grad_sum = grad_act[:, lanes] * slope_ref[:, lanes].astype(F32)
        window[0:chunk, lanes] = grad_sum
        if at < inner:
            pre = pre_ref[:, lanes].astype(F32)
        else:
            pre = tail_ref[:, at - inner : at - inner + LANES].astype(F32)
        grad_pre = taps_ref[3:4, lanes] * grad_sum
        grad_taps_ref[3:4, lanes] += jnp.sum(pre * grad_sum, axis=0, keepdims=True)
        grad_taps_ref[4:5, lanes] += jnp.sum(grad_sum, axis=0, keepdims=True)
        for ahead in range(1, CONV):
            later = window[ahead : ahead + chunk, lanes] * same[ahead - 1]
            grad_pre += taps_ref[3 - ahead : 4 - ahead, lanes] * later
            grad_taps_ref[3 - ahead : 4 - ahead, lanes] += jnp.sum(
                pre * later, axis=0, keepdims=True
            )
        grad_pre_ref[:, lanes] = grad_pre.astype(BF16)
    window[chunk:, :] = window[0:8, :]


def scan_calls(parts, tok_count, inner):
    chunk = min(LANES, tok_count)
    per_part = tok_count // chunk
    count = parts * per_part
    channels = inner + 2 * STATE
    tokens = parts * tok_count

    def blocks(flip):
        def time(step):
            return count - 1 - step if flip else step

        def place(step, own):
            t = time(step)
            return lax.bitwise_xor(t // per_part, own[0]) * per_part + t % per_part

        def tok(width):
            return pl.BlockSpec((chunk, width), lambda step, own: (place(step, own), 0))

        row = pl.BlockSpec((None, 8, chunk), lambda step, own: (time(step), 0, 0))
        states = pl.BlockSpec((None, STATE, inner), lambda step, own: (time(step), 0, 0))

        def const(rows, width):
            return pl.BlockSpec((rows, width), lambda step, own: (0, 0))

        return tok, row, states, const

    def scan(kernel, ins, outs, shapes, scratch):
        return pl.pallas_call(
            partial(kernel, chunk),
            grid_spec=pltpu.PrefetchScalarGridSpec(
                num_scalar_prefetch=1,
                grid=(count,),
                in_specs=ins,
                out_specs=outs,
                scratch_shapes=scratch,
            ),
            out_shape=shapes,
            compiler_params=pltpu.CompilerParams(
                dimension_semantics=("arbitrary",), vmem_limit_bytes=VMEM
            ),
            cost_estimate=COST,
        )

    struct = jax.ShapeDtypeStruct
    tok, row, states, const = blocks(False)
    forward = scan(
        forward_kernel,
        [tok(inner), tok(2 * STATE), tok(inner), tok(LANES), tok(inner), row]
        + [const(8, channels), const(8, LANES), const(1, inner), const(1, inner)],
        [tok(channels), tok(channels), tok(inner), tok(inner), states, row],
        [
            struct((tokens, channels), BF16),
            struct((tokens, channels), BF16),
            struct((tokens, inner), F32),
            struct((tokens, inner), BF16),
            struct((count, STATE, inner), BF16),
            struct((count, 8, chunk), F32),
        ],
        [
            pltpu.VMEM((STATE, inner), F32),
            pltpu.VMEM((chunk + 8, channels), F32),
            pltpu.VMEM((chunk, inner), F32),
            pltpu.VMEM((chunk, inner), BF16),
        ],
    )
    tok, row, states, const = blocks(True)
    backward = scan(
        backward_kernel,
        [tok(channels), tok(channels), tok(inner), tok(2 * STATE), tok(LANES)]
        + [tok(inner), states, row]
        + [const(8, channels), const(8, LANES), const(1, inner)],
        [tok(channels), tok(LANES), const(8, channels), const(8, inner), const(8, LANES)],
        [
            struct((tokens, channels), BF16),
            struct((tokens, LANES), BF16),
            struct((8, channels), F32),
            struct((8, inner), F32),
            struct((8, LANES), F32),
        ],
        [
            pltpu.VMEM((STATE, inner), F32),
            pltpu.VMEM((chunk + 8, channels), F32),
            pltpu.VMEM((chunk, channels), F32),
            pltpu.VMEM((LANES, chunk), F32),
            pltpu.VMEM((chunk, inner), F32),
            pltpu.VMEM((chunk, inner), F32),
            pltpu.VMEM((chunk, inner), BF16),
            pltpu.VMEM((chunk, inner), BF16),
        ],
    )
    return forward, backward


NN = ((1,), (0,))
NT = ((1,), (1,))
TN = ((0,), (0,))
COST = pl.CostEstimate(flops=1, bytes_accessed=1, transcendentals=0)


def call(kernel, grid, ins, outs, shapes, args, scratch=()):
    return pl.pallas_call(
        kernel,
        grid_spec=pltpu.PrefetchScalarGridSpec(
            num_scalar_prefetch=1,
            grid=grid,
            in_specs=ins,
            out_specs=outs,
            scratch_shapes=scratch,
        ),
        out_shape=shapes,
        compiler_params=pltpu.CompilerParams(
            dimension_semantics=("arbitrary",) * len(grid), vmem_limit_bytes=VMEM
        ),
        cost_estimate=COST,
    )(*args)


def fixed(shape):
    return pl.BlockSpec(shape, lambda i, own: (0,) * len(shape))


def own_heads(own, heads):
    head = lax.broadcasted_iota(jnp.int32, (HEADS, LANES), 0)
    lane = lax.broadcasted_iota(jnp.int32, (HEADS, LANES), 1)
    return ((head == own * heads + lane) & (lane < heads)).astype(F32)


def project_kernel(parts, own_ref, *refs):
    tok_refs, weights, tails = refs[:parts], refs[parts : 2 * parts], refs[2 * parts : 3 * parts]
    gain_ref, normed_ref, gate_ref, pre_ref, tail_ref, dt_ref, ordered = refs[3 * parts :]
    at = pl.program_id(0)
    rows = tails[0].shape[1]
    tok_count = tok_refs[0].shape[0]

    @pl.when(at == 0)
    def _():
        for r in range(parts):
            values = tok_refs[r][...].astype(F32)
            mean = jnp.mean(values * values, axis=-1, keepdims=True)
            normed_ref[r * tok_count : (r + 1) * tok_count, :] = (
                values * lax.rsqrt(mean + EPSILON) * gain_ref[...]
            ).astype(BF16)
        for s in range(parts):
            lanes = pl.ds(pl.multiple_of(lax.bitwise_xor(own_ref[0], s) * rows, LANES), rows)
            ordered[:, s * rows : (s + 1) * rows] = normed_ref[:, lanes]

    def total(refs):
        return dot(ordered[...], jnp.concatenate([ref[...] for ref in refs], axis=1), NT)

    @pl.when(at < 2)
    def _():
        gate_ref[...] = total(weights)

    @pl.when((at >= 2) & (at < 4))
    def _():
        pre_ref[...] = total(weights).astype(BF16)

    @pl.when(at == 4)
    def _():
        rest = total(tails)
        tail_ref[...] = rest[:, : 2 * STATE].astype(BF16)
        pick = own_heads(own_ref[0], HEADS // parts)
        dt_ref[...] = dot(rest[:, 2 * STATE :], pick, precision=HIGHEST)


def project(own_arg, tok_parts, weights, tails, gain):
    parts, (tok_count, width) = len(tok_parts), tok_parts[0].shape
    half, rows = weights[0].shape[1:]
    tokens = parts * tok_count

    def near(i, own):
        return (jnp.minimum(i, 3), 0, 0)

    def far(i, own):
        return (lax.bitwise_xor(jnp.minimum(i, 3), own[1]), 0, 0)

    struct = jax.ShapeDtypeStruct
    return call(
        partial(project_kernel, parts),
        (5,),
        [fixed((tok_count, width))] * parts
        + [pl.BlockSpec((None, half, rows), far if s > 1 else near) for s in range(parts)]
        + [fixed(tails[0].shape)] * parts
        + [fixed((1, width))],
        [
            fixed((tokens, width)),
            pl.BlockSpec((tokens, half), lambda i, own: (0, jnp.minimum(i, 1))),
            pl.BlockSpec((tokens, half), lambda i, own: (0, jnp.clip(i - 2, 0, 1))),
            fixed((tokens, 2 * STATE)),
            fixed((tokens, LANES)),
        ],
        [
            struct((tokens, width), BF16),
            struct((tokens, 2 * half), F32),
            struct((tokens, 2 * half), BF16),
            struct((tokens, 2 * STATE), BF16),
            struct((tokens, LANES), F32),
        ],
        (own_arg, *tok_parts, *weights, *tails, gain[None]),
        [pltpu.VMEM((tokens, width), BF16)],
    )


def back_kernel(parts, own_ref, *refs):
    weight_ref, all_ref, back_ref = refs[parts:]
    tok_count = refs[0].shape[0]

    @pl.when(pl.program_id(0) == 0)
    def _():
        for r in range(parts):
            all_ref[r * tok_count : (r + 1) * tok_count, :] = refs[r][...]

    back_ref[...] = dot(all_ref[...], weight_ref[...], NT).astype(BF16)


def project_back(own_arg, cot_parts, weight):
    parts, (tok_count, width) = len(cot_parts), cot_parts[0].shape
    inner = weight.shape[0]
    block = min(256, inner)
    tokens = parts * tok_count
    struct = jax.ShapeDtypeStruct
    return call(
        partial(back_kernel, parts),
        (inner // block,),
        [fixed((tok_count, width))] * parts
        + [pl.BlockSpec((block, width), lambda i, own: (i, 0))],
        [fixed((tokens, width)), pl.BlockSpec((tokens, block), lambda i, own: (0, i))],
        [struct((tokens, width), BF16), struct((tokens, inner), BF16)],
        (own_arg, *cot_parts, weight),
    )


def split_rows(value, even_ref, odd_ref):
    size = even_ref.shape[0]
    even_ref[...] = value[:size].astype(BF16)
    odd_ref[...] = value[size:].astype(BF16)


def split_outs(tok_count, parts, width):
    spec = pl.BlockSpec((None, tok_count, width), lambda i, own: (i, 0, 0))
    shape = jax.ShapeDtypeStruct((parts // 2, tok_count, width), BF16)
    return [spec, spec], [shape, shape]


def out_kernel(own_ref, a_ref, b_ref, even_ref, odd_ref):
    split_rows(dot(a_ref[...], b_ref[...]), even_ref, odd_ref)


def project_out(own_arg, gained, weight, parts):
    (tokens, inner), width = gained.shape, weight.shape[1]
    tok_count = tokens // parts
    specs, shapes = split_outs(tok_count, parts, width)
    return call(
        out_kernel,
        (parts // 2,),
        [pl.BlockSpec((2 * tok_count, inner), lambda i, own: (i, 0)), fixed((inner, width))],
        specs,
        shapes,
        (own_arg, gained, weight),
    )


def into_kernel(parts, own_ref, gate_ref, pre_ref, dt_ref, *refs):
    weights, tails = refs[:parts], refs[parts : 2 * parts]
    even_ref, odd_ref = refs[2 * parts :]
    half, rows = weights[0].shape[1:]
    pick = own_heads(own_ref[0], HEADS // parts).astype(BF16)
    grad_dt = dot(dt_ref[...], pick, NT).astype(BF16)
    left = jnp.concatenate([gate_ref[...], pre_ref[...], grad_dt], axis=1)
    for s in range(parts):
        order = [lax.bitwise_xor(q, own_ref[1]) if s > 1 else q for q in range(4)]
        right = jnp.concatenate([weights[s][q] for q in order] + [tails[s][...]], axis=0)
        lanes = pl.ds(pl.multiple_of(lax.bitwise_xor(own_ref[0], s) * rows, LANES), rows)
        split_rows(dot(left, right), even_ref.at[:, lanes], odd_ref.at[:, lanes])


def project_into(own_arg, grad_gate, grad_pre, grad_dt, weights, tails):
    parts = len(weights)
    (tokens, inner), channels = grad_gate.shape, grad_pre.shape[1]
    width = parts * weights[0].shape[2]
    tok_count = tokens // parts

    def tok(size):
        return pl.BlockSpec((2 * tok_count, size), lambda i, own: (i, 0))

    specs, shapes = split_outs(tok_count, parts, width)
    return call(
        partial(into_kernel, parts),
        (parts // 2,),
        [tok(inner), tok(channels), tok(LANES)]
        + [fixed(w.shape) for w in weights]
        + [fixed(r.shape) for r in tails],
        specs,
        shapes,
        (own_arg, grad_gate, grad_pre, grad_dt, *weights, *tails),
    )


def tail_kernel(count, parts, own_ref, *refs):
    pres, dts, normed = refs[:count], refs[count : 2 * count], refs[2 * count : 3 * count]
    even_ref, odd_ref = refs[3 * count :]
    pick = own_heads(own_ref[0], HEADS // parts)

    def total(lefts):
        terms = [dot(a[...], b[...], TN) for a, b in zip(lefts, normed)]
        return sum(terms[1:], terms[0])

    value = [total(pres), dot(pick.astype(BF16), total(dts).astype(BF16))]
    value = jnp.concatenate(value, axis=0).astype(BF16)

    @pl.when(pl.program_id(0) % 2 == 0)
    def _():
        even_ref[...] = value

    @pl.when(pl.program_id(0) % 2 == 1)
    def _():
        odd_ref[...] = value


def tail_grad(own_arg, grad_pres, grad_dts, normed, parts):
    (tokens, channels), width = grad_pres[0].shape, normed[0].shape[1]
    count, columns, rows = len(normed), 2 * STATE + HEADS, width // parts
    spec = pl.BlockSpec((None, columns, rows), lambda r, own: (r // 2, 0, 0))
    shape = jax.ShapeDtypeStruct((parts // 2, columns, rows), BF16)
    return call(
        partial(tail_kernel, count, parts),
        (parts,),
        [pl.BlockSpec((tokens, 2 * STATE), lambda r, own: (0, channels // (2 * STATE) - 1))] * count
        + [fixed((tokens, LANES))] * count
        + [pl.BlockSpec((tokens, rows), lambda r, own: (0, lax.bitwise_xor(own[0], r)))] * count,
        [spec, spec],
        [shape, shape],
        (own_arg, *grad_pres, *grad_dts, *normed),
    )


def add_kernel(own_ref, a_ref, b_ref, keep_ref, send_ref):
    keep_ref[...] = a_ref[0].astype(F32) + b_ref[0].astype(F32)
    send_ref[...] = (a_ref[1].astype(F32) + b_ref[1].astype(F32)).astype(BF16)


def add_parts(own_arg, even, got):
    _, size, width = even.shape
    block = size // 2
    both = pl.BlockSpec((2, block, width), lambda i, own: (0, i, 0))
    one = pl.BlockSpec((block, width), lambda i, own: (i, 0))
    struct = jax.ShapeDtypeStruct
    return call(
        add_kernel,
        (2,),
        [both, both],
        [one, one],
        [struct((size, width), F32), struct((size, width), BF16)],
        (own_arg, even, got),
    )


class Split:
    def __init__(self, own_arg, parts):
        self.own_arg = own_arg
        self.even, self.odd = parts
        self.plain = self.even.shape[0] != 2
        self.sent = self.even
        if not self.plain:
            self.got = swap(self.odd, "fsdp", 1)

    def middle(self, *earlier):
        if not self.plain:
            got = after(self.got, *earlier)
            self.keep, self.sent = add_parts(self.own_arg, self.even, got)
            self.got = swap(self.sent, "fsdp", 2)
        return self.sent

    def final(self, *earlier):
        if not self.plain:
            return self.keep, after(self.got, *earlier)
        every = jnp.stack([self.even, self.odd], axis=1)
        every = every.reshape((-1,) + self.even.shape[1:])
        total = scattered(after(every, *earlier))
        return total, jnp.zeros(total.shape, BF16)


def mixed_kernel(own_ref, tok_ref, scale_ref, keep_ref, got_ref, out_ref):
    total = keep_ref[...] + got_ref[...].astype(F32)
    out_ref[...] = (tok_ref[...].astype(F32) + total * scale_ref[...]).astype(BF16)


def mixed_rows(own_arg, tok, scale, terms):
    size, width = tok.shape
    block = min(128, size)
    one = pl.BlockSpec((block, width), lambda i, own: (i, 0))
    return call(
        mixed_kernel,
        (size // block,),
        [one, pl.BlockSpec((block, 1), lambda i, own: (i, 0)), one, one],
        [one],
        [jax.ShapeDtypeStruct((size, width), BF16)],
        (own_arg, tok, scale, *terms),
    )[0]


def norm_kernel(own_ref, tok_ref, cot_ref, gain_ref, keep_ref, got_ref, out_ref, sum_ref):
    @pl.when(pl.program_id(0) == 0)
    def _():
        sum_ref[...] = jnp.zeros_like(sum_ref)

    tok = tok_ref[...].astype(F32)
    inverse = lax.rsqrt(jnp.mean(tok * tok, axis=-1, keepdims=True) + EPSILON)
    hat = tok * inverse
    part = keep_ref[...] + got_ref[...].astype(F32)
    through = part * gain_ref[...]
    here = inverse * (through - hat * jnp.mean(hat * through, axis=-1, keepdims=True))
    out_ref[...] = (cot_ref[...].astype(F32) + here).astype(BF16)
    sum_ref[0:1, :] += jnp.sum(part * hat, axis=0, keepdims=True)


def norm_rows(own_arg, tok, cot, gain, terms):
    size, width = tok.shape
    block = min(128, size)
    one = pl.BlockSpec((block, width), lambda i, own: (i, 0))
    return call(
        norm_kernel,
        (size // block,),
        [one, one, fixed((1, width)), one, one],
        [one, fixed((8, width))],
        [jax.ShapeDtypeStruct((size, width), BF16), jax.ShapeDtypeStruct((8, width), F32)],
        (own_arg, tok, cot, gain[None], *terms),
    )


def join_kernel(own_ref, a_ref, b_ref, out_ref):
    out_ref[...] = (a_ref[...].astype(F32) + b_ref[...].astype(F32)).astype(BF16)


def join(own_arg, keep, got):
    size, width = keep.shape
    one = pl.BlockSpec((size // 4, width), lambda i, own: (i, 0))
    return call(
        join_kernel,
        (4,),
        [one, one],
        [one],
        [jax.ShapeDtypeStruct((size, width), BF16)],
        (own_arg, keep, got),
    )[0]


def pick_kernel(order, own_ref, *refs):
    out_ref = refs[-1]
    rows = out_ref.shape[-1]
    for i, (ref, block, lane) in enumerate(order):
        if lane:
            lanes = pl.ds(pl.multiple_of(lax.bitwise_xor(own_ref[0], block) * rows, LANES), rows)
            out_ref[i] = refs[ref][:, lanes]
        else:
            out_ref[i] = refs[ref][block]


def picked(own_arg, order, args, rows):
    shape = (len(order), args[0].shape[0], rows)
    return call(
        partial(pick_kernel, order),
        (1,),
        [fixed(arg.shape) for arg in args],
        [fixed(shape)],
        [jax.ShapeDtypeStruct(shape, BF16)],
        (own_arg, *args),
    )[0]


def place_kernel(own_ref, half_ref, far_ref, near_ref, out_ref):
    rows = out_ref.shape[-1]
    own = own_ref[0]
    lanes = pl.ds(pl.multiple_of(own * rows, LANES), rows)
    out_ref[own] = half_ref[:, lanes]
    out_ref[lax.bitwise_xor(own, 2)] = far_ref[0]
    out_ref[lax.bitwise_xor(own, 1)] = near_ref[0]
    out_ref[lax.bitwise_xor(own, 3)] = near_ref[1]


class Trade:
    def __init__(self, own_arg, half, parts):
        self.own_arg, self.half, self.parts = own_arg, half, parts
        self.rows = half.shape[1] // parts
        self.sent = half
        self.plain = parts != 4
        if not self.plain:
            self.sent = picked(own_arg, [(0, 2, True), (0, 3, True)], [half], self.rows)
            self.far = swap(self.sent, "fsdp", 2)

    def middle(self, *earlier):
        if not self.plain:
            self.far = after(self.far, *earlier)
            order = [(0, 1, True), (1, 1, False)]
            self.sent = picked(self.own_arg, order, [self.half, self.far], self.rows)
            self.near = swap(self.sent, "fsdp", 1)
        return self.sent

    def final(self, *earlier):
        if self.plain:
            own = lax.axis_index("fsdp")
            here = [
                lax.dynamic_slice_in_dim(self.half, (own ^ r) * self.rows, self.rows, 1)
                for r in range(self.parts)
            ]
            here = traded(here, lambda value, bit: swap(value, "fsdp", bit))
            return jnp.stack(absolute(here))
        near = after(self.near, *earlier)
        shape = (self.parts, self.half.shape[0], self.rows)
        return call(
            place_kernel,
            (1,),
            [fixed(self.half.shape), fixed(self.far.shape), fixed(near.shape)],
            [fixed(shape)],
            [jax.ShapeDtypeStruct(shape, BF16)],
            (self.own_arg, self.half, self.far, near),
        )[0]


def weight_kernel(count, own_ref, *refs):
    out_ref = refs[-1]
    total = dot(refs[0][...], refs[count][...], TN)
    for m in range(1, count):
        total += dot(refs[m][...], refs[count + m][...], TN)
    out_ref[...] = total.astype(out_ref.dtype)


def half_of(own, kept):
    return lax.bitwise_xor(own[1] & 1, 0 if kept else 1)


def weight_grad(own_arg, lefts, rights, inner, kept):
    tokens, width = rights[0].shape
    half, block = inner // 2, 512
    return call(
        partial(weight_kernel, len(lefts)),
        (width // block,),
        [pl.BlockSpec((tokens, half), lambda i, own: (0, half_of(own, kept)))] * len(lefts)
        + [pl.BlockSpec((tokens, block), lambda i, own: (0, i))] * len(rights),
        [pl.BlockSpec((half, block), lambda i, own: (0, i))],
        [jax.ShapeDtypeStruct((half, width), BF16)],
        (own_arg, *lefts, *rights),
    )[0]


def gate_kernel(micro, chunk, per_part, own_ref, *refs):
    gain_ref, refs = refs[0], refs[1:]
    ssm, gate, back, stat, normed = (refs[k * micro : (k + 1) * micro] for k in range(5))
    outs = refs[5 * micro :]
    grad_ssm, grad_gate, gated_all = (outs[k * micro : (k + 1) * micro] for k in range(3))
    grad_gain_ref, out_ref = outs[3 * micro :]
    count = stat[0].shape[0]
    half = gain_ref.shape[1]

    @pl.when(pl.program_id(1) == 0)
    def _():
        grad_gain_ref[...] = jnp.zeros_like(grad_gain_ref)

        def step(t, carry):
            place = lax.bitwise_xor(t // per_part, own_ref[0]) * per_part + t % per_part
            rows = pl.ds(pl.multiple_of(place * chunk, chunk), chunk)
            for m in range(micro):
                sums = stat[m][t]
                scale = lax.rsqrt(sums[0:1, :] * (1.0 / INNER) + EPSILON)
                shift = scale * scale * scale * sums[1:2, :] * (1.0 / INNER)
                scale = columns(scale, chunk)
                shift = columns(shift, chunk)
                for at in range(0, half, LANES):
                    lanes = slice(at, at + LANES)
                    out = ssm[m][rows, lanes]
                    branch = gate[m][rows, lanes]
                    grad = back[m][rows, lanes].astype(F32)
                    sig = jax.nn.sigmoid(branch)
                    silu = branch * sig
                    gated = out * silu
                    scaled = gated * scale
                    gain = gain_ref[:, lanes]
                    grad_gated = scale * (gain * grad) - gated * shift
                    grad_ssm[m][rows, lanes] = (grad_gated * silu).astype(BF16)
                    grad_gate[m][rows, lanes] = (
                        grad_gated * out * (sig * (1.0 + branch * (1.0 - sig)))
                    ).astype(BF16)
                    gated_all[m][rows, lanes] = (scaled * gain).astype(BF16)
                    grad_gain_ref[0:1, lanes] += jnp.sum(scaled * grad, axis=0, keepdims=True)
            return carry

        lax.fori_loop(0, count, step, 0)

    terms = [dot(a[...], b[...], TN) for a, b in zip(grad_gate, normed)]
    out_ref[...] = sum(terms[1:], terms[0]).astype(BF16).reshape(out_ref.shape)


def gate_grads(own_arg, scans, stats, normed, gain, per_part, lines):
    micro = len(scans)
    (tokens, inner), width = scans[0][0].shape, normed[0].shape[1]
    half, block = inner // 2, 512
    chunk = stats[0].shape[2]
    cols = pl.BlockSpec((tokens, half), lambda h, i, own: (0, h))
    row = pl.BlockSpec((1, half), lambda h, i, own: (0, h))
    sums = pl.BlockSpec((8, half), lambda h, i, own: (0, h))
    lanes = pl.BlockSpec((tokens, block), lambda h, i, own: (0, i))
    whole = pl.BlockSpec(stats[0].shape, lambda h, i, own: (0, 0, 0))
    struct = jax.ShapeDtypeStruct
    outs = call(
        partial(gate_kernel, micro, chunk, per_part),
        (2, width // block),
        [row] + [cols] * (3 * micro) + [whole] * micro + [lanes] * micro,
        [cols] * (3 * micro)
        + [sums]
        + [pl.BlockSpec((lines, None, half // lines, block), lambda h, i, own: (0, h, 0, i))],
        [struct((tokens, inner), BF16)] * (3 * micro)
        + [struct((8, inner), F32), struct((lines, 2, half // lines, width), BF16)],
        (own_arg, gain, *[scan[k] for k in range(3) for scan in scans], *stats, *normed),
    )
    split = [outs[k * micro : (k + 1) * micro] for k in range(3)]
    return split + list(outs[3 * micro :])


def fill_kernel(own_ref, part_ref, *refs):
    out_ref = refs[-1]
    out_ref[...] = part_ref[...].reshape(out_ref.shape).astype(F32)


def fill(own_arg, whole, rows, part, grid, part_spec, out_spec):
    width = part.shape[-1]
    return pl.pallas_call(
        fill_kernel,
        grid_spec=pltpu.PrefetchScalarGridSpec(
            num_scalar_prefetch=1,
            grid=grid,
            in_specs=[part_spec] + [pl.BlockSpec(memory_space=pl.ANY)] * (whole is not None),
            out_specs=out_spec,
        ),
        out_shape=jax.ShapeDtypeStruct((rows, width), F32),
        input_output_aliases={} if whole is None else {2: 0},
        compiler_params=pltpu.CompilerParams(
            dimension_semantics=("arbitrary",) * len(grid), vmem_limit_bytes=VMEM
        ),
        cost_estimate=COST,
    )(*([own_arg, part] + ([] if whole is None else [whole])))


IN_ROWS = 2 * INNER + 2 * STATE + HEADS


def fill_lines(own_arg, whole, part, kept):
    lines, parts, share, rows = part.shape
    return fill(
        own_arg,
        whole,
        IN_ROWS,
        part,
        (parts,),
        pl.BlockSpec((lines, None, share, rows), lambda f, own: (0, f, 0, 0)),
        pl.BlockSpec((lines * share, rows), lambda f, own: (2 * f + half_of(own, kept), 0)),
    )


def fill_tail(own_arg, whole, part):
    return fill(
        own_arg,
        whole,
        IN_ROWS,
        part,
        (part.shape[0] // HEADS,),
        pl.BlockSpec((HEADS, part.shape[1]), lambda i, own: (i, 0)),
        pl.BlockSpec((HEADS, part.shape[1]), lambda i, own: (2 * INNER // HEADS + i, 0)),
    )


def fill_heads(own_arg, whole, part, first):
    lines, _, parts, share, rows = part.shape
    size = lines * share
    return fill(
        own_arg,
        whole,
        IN_ROWS,
        part,
        (parts, 2),
        pl.BlockSpec((lines, None, None, share, rows), lambda f, k, own: (0, k, f, 0, 0)),
        pl.BlockSpec((size, rows), lambda f, k, own: (first // size + 2 * f + k, 0)),
    )


def on_device(
    tokens,
    segment_ids,
    cotangent,
    norm_gain,
    in_weight,
    conv_weight,
    conv_bias,
    dt_bias,
    a_log,
    skip_d,
    inner_gain,
    out_weight,
):
    micro, _, tok_count, width = tokens.shape
    parts = lax.axis_size("fsdp")
    groups = lax.axis_size("group")
    own = lax.axis_index("fsdp")
    inner = INNER // parts
    heads = HEADS // parts
    channels = inner + 2 * STATE
    rows = width // parts
    seq = tok_count * parts
    chunk = min(LANES, tok_count)
    forward, backward = scan_calls(parts, tok_count, inner)
    side = lax.axis_index("group") & 3
    own_arg = jnp.stack([own, side]).astype(jnp.int32)
    along = Lines()

    def small(sent):
        taps_here = jnp.concatenate([conv_weight, conv_bias[None]], axis=0).astype(F32)
        packed = jnp.concatenate(
            [
                norm_gain.astype(F32),
                taps_here.reshape(-1),
                segment_ids.astype(F32).reshape(-1),
            ]
        )
        held = gather_far(after(packed, sent))
        packed = jnp.stack(absolute(gather_near(held)))
        cut = norm_gain.shape[0]
        gain_norm = packed[:, :cut].reshape(-1)
        taps_size = taps_here.size
        taps = packed[:, cut : cut + taps_size].reshape(parts, CONV + 1, -1)
        taps = taps.transpose(1, 0, 2).reshape(CONV + 1, XBC)
        seg = packed[:, cut + taps_size :].reshape(parts, micro, tok_count)
        seg = seg.transpose(1, 0, 2).reshape(micro, seq)
        taps = jnp.concatenate(
            [lax.dynamic_slice_in_dim(taps, own * inner, inner, 1), taps[:, INNER:]], axis=1
        )
        taps = jnp.pad(taps, ((0, 8 - CONV - 1), (0, 0)))
        seg_rows = [seg] + [
            jnp.pad(seg[:, ahead:], ((0, 0), (0, ahead)), constant_values=-1.0)
            for ahead in range(1, CONV)
        ]
        seg_rows = jnp.stack([part.reshape(micro, -1, chunk) for part in seg_rows], axis=2)
        seg_rows = jnp.pad(seg_rows, ((0, 0), (0, 0), (0, 8 - CONV), (0, 0)))
        head_row = jnp.concatenate(
            [dt_bias.astype(F32)[None], -jnp.exp(a_log.astype(F32))[None]], axis=0
        )
        head_row = jnp.pad(head_row, ((0, 6), (0, LANES - heads)))
        skip_row = jnp.repeat(skip_d.astype(F32), HEADDIM)[None]
        gain_row = inner_gain.astype(F32)[None]
        return held[parts // 2], (gain_norm, taps, seg_rows, head_row, skip_row, gain_row)

    in_rows = in_weight.T
    started = {}

    def between(sent, got):
        packed, started["small"] = small(sent)
        started["tok"] = [gather_far(after(tokens[0, 0], got))]
        started["tail"] = gather_far(after(in_rows[2 * INNER :], got))
        first = started["tok"][0][parts // 2]
        started["tok"] += [gather_far(after(tokens[m, 0], first)) for m in range(1, micro)]
        started["cot"] = [gather_far(after(cotangent[0, 0], first))]
        return [first, packed], [started["tail"][parts // 2], *started["small"]]

    with jax.named_scope("weights"):
        weights = traded_weights(in_rows, inner, between)
    gain_norm, taps, seg_rows, head_row, skip_row, gain_row = started["small"]
    tails = gather_near(started["tail"], weights[1])

    projected = []
    for m in range(micro):
        tok_here = gather_near(started["tok"][m], weights[1], *[p[0] for p in projected[-1:]])
        projected.append(project(own_arg, tok_here, weights, tails, gain_norm))
    normed_all = [p[0] for p in projected]
    for m in range(1, micro):
        started["cot"].append(
            gather_far(after(cotangent[m, 0], started["tok"][m][parts // 2], normed_all[0]))
        )
    scans = []
    cot_all = []
    for m in range(micro):
        parts_here = gather_near(started["cot"][m], *(scans[m - 1][-1:] if m else normed_all[-1:]))
        cot, back = project_back(own_arg, parts_here, out_weight)
        _, gate, pre, tail, dt_raw = projected[m]
        outs = forward(
            own_arg, pre, tail, gate, dt_raw, back, seg_rows[m], taps, head_row, skip_row, gain_row
        )
        cot_all.append(cot)
        scans.append((gate, pre, tail, dt_raw, back) + tuple(outs))
    stats = [
        jnp.pad(summed(scan[-1][:, :2], "fsdp"), ((0, 0), (0, 6), (0, 0))) for scan in scans
    ]

    def scan_back(m, *earlier):
        _, pre, tail, dt_raw, _, act, slope, _, _, entering, _ = scans[m]
        return backward(
            own_arg,
            act,
            slope,
            pre,
            tail,
            dt_raw,
            after(grad_ssm[m], *earlier),
            entering,
            seg_rows[m],
            taps,
            head_row,
            skip_row,
        )

    def across(away):
        return swap(away, "group", 1)

    lines_count = groups // 2
    lane = lax.axis_index("group") & 1

    def joined(keep, got):
        return join(own_arg, keep, got).reshape(lines_count, -1, width)

    grad_ssm, grad_gates, gated, grad_inner, gate_out = gate_grads(
        own_arg,
        [(scan[7], scan[0], scan[4]) for scan in scans],
        stats,
        normed_all,
        gain_row,
        tok_count // chunk,
        lines_count,
    )
    half_gate = along.scatter(gate_out.reshape(groups, -1, width))
    gated = [after(g, gate_out) for g in gated]
    away_out = weight_grad(own_arg, gated, cot_all, inner, False)
    with jax.named_scope("away_out"):
        got_out = across(away_out)
    gated = [after(g, away_out) for g in gated]
    keep_out = weight_grad(own_arg, gated, cot_all, inner, True)
    backs = [scan_back(0, keep_out)]
    half_out = joined(keep_out, after(got_out, backs[0][0]))
    with jax.named_scope("trade_gate"):
        trade = Trade(own_arg, after(half_gate, half_out), parts)
    for m in range(1, micro):
        backs.append(scan_back(m, half_out, trade.sent))
    with jax.named_scope("trade_gate"):
        trade.middle(backs[-1][0])
        gate_cols = trade.final()
    left = [after(b[0], gate_cols) for b in backs]
    away_x = weight_grad(own_arg, left, normed_all, inner, False)
    with jax.named_scope("away_heads"):
        got_x = across(away_x)
    left = [after(b[0], away_x) for b in backs]
    keep_x = weight_grad(own_arg, left, normed_all, inner, True)
    half_out = along.scatter(half_out, lines())
    gate_lines = along.gather(after(gate_cols, away_x), lines())

    into = []
    for m in range(micro):
        grad_gate = after(grad_gates[m], keep_x, *(part[0] for part in into[-1:]))
        into.append(project_into(own_arg, grad_gate, *backs[m][:2], weights, tails))
    half_x = joined(keep_x, after(got_x, into[-1][0]))
    with jax.named_scope("gate_lines"):
        got_lines = across(after(gate_lines, half_x))
    rights = [after(n, half_x) for n in normed_all]
    tail_part = tail_grad(own_arg, [b[0] for b in backs], [b[1] for b in backs], rights, parts)

    def split(pair, name):
        with jax.named_scope(name):
            return Split(own_arg, [after(part, half_x) for part in pair])

    into = [split(pair, "into") for pair in into]
    tail_part = split(tail_part, "tail")
    with jax.named_scope("into"):
        for part in into:
            part.middle()
    with jax.named_scope("tail"):
        tail_part.middle()
    half_x = along.scatter(half_x, lines())
    with jax.named_scope("trade_heads"):
        trade = Trade(own_arg, half_x, parts)
    sent = trade.sent
    grad_tok = []
    grad_norm = jnp.zeros((width,), F32)
    for m in range(micro):
        terms = into[m].final(sent, got_lines)
        tok, gain = norm_rows(own_arg, tokens[m, 0], cotangent[m, 0], gain_norm, terms)
        grad_tok.append(tok)
        grad_norm += gain[0]
        if m == 0:
            with jax.named_scope("trade_heads"):
                sent = trade.middle(tok)
    with jax.named_scope("trade_heads"):
        x_cols = trade.final(tok)
    keep, got = tail_part.final()
    grad_tail = keep + got.astype(F32)

    grad_taps = sum(b[2] for b in backs)[: CONV + 1]
    grad_skip = sum(b[3] for b in backs)[0]
    grad_head = sum(b[4] for b in backs)
    taps_all = lax.dynamic_update_slice_in_dim(
        jnp.zeros((CONV + 1, XBC), F32), grad_taps[:, :inner], own * inner, 1
    )
    taps_all = taps_all.at[:, INNER:].set(grad_taps[:, inner:])
    with jax.named_scope("small"):
        joint = summed(jnp.concatenate([taps_all.reshape(-1), grad_norm]), "fsdp")
    skip_sum = jnp.sum(grad_skip.reshape(heads, HEADDIM), axis=1)
    joint = jnp.concatenate(
        [joint, grad_inner[0], grad_head[0, :heads], grad_head[1, :heads], skip_sum]
    )

    with jax.named_scope("small"):
        joint = summed(joint, "group")
    with jax.named_scope("tail"):
        grad_tail = summed(grad_tail, "group", BF16)
    mixed = []
    for m in range(micro):
        gained = after(scans[m][8], x_cols, *(part.even for part in mixed[-1:]))
        part = project_out(own_arg, gained, out_weight, parts)
        with jax.named_scope("mixed"):
            mixed.append(Split(own_arg, part))
    out_lines = along.gather(half_out, lines())
    with jax.named_scope("out_lines"):
        got_out = across(after(out_lines, joint, grad_tail))
    x_all = along.gather(after(x_cols, joint, grad_tail))
    with jax.named_scope("mixed"):
        for part in mixed:
            part.middle(mixed[-1].even)

    def all_lines(value):
        return value.reshape(lines_count, 2, parts, -1, rows)

    whole = fill_lines(own_arg, None, after(gate_lines, x_cols), True)
    whole = fill_lines(own_arg, whole, after(got_lines, x_cols), False)
    whole = fill_tail(own_arg, whole, grad_tail)
    grad_out = jnp.stack(
        [
            jnp.where(lane == 0, out_lines, got_out),
            jnp.where(lane == 0, got_out, out_lines),
        ]
    )
    grad_out = grad_out.reshape(inner, width).astype(F32)

    for m in range(micro):
        stat = lax.dynamic_slice_in_dim(
            stats[m][:, 0].reshape(seq), own * tok_count, tok_count, 0
        )
        scale = lax.rsqrt(stat * (1.0 / INNER) + EPSILON)[:, None]
        mixed[m] = mixed_rows(own_arg, tokens[m, 0], scale, mixed[m].final(whole))

    at = (CONV + 1) * XBC
    share = XBC // parts
    taps_all = lax.dynamic_slice_in_dim(joint[:at].reshape(CONV + 1, XBC), own * share, share, 1)
    grad_norm = lax.dynamic_slice_in_dim(joint, at + own * rows, rows, 0)
    at += width
    grad_inner = joint[at : at + inner]
    at += inner
    grad_bias, grad_rate, grad_skip = (
        joint[at + k * heads : at + (k + 1) * heads] for k in range(3)
    )
    mixed = jnp.stack(mixed)[:, None]
    grad_tok = jnp.stack(grad_tok)[:, None]
    x_all = after(x_all, whole, grad_out, grad_norm, mixed, grad_tok)
    grad_in = fill_heads(own_arg, whole, all_lines(x_all), INNER).T
    return (
        mixed,
        grad_tok,
        grad_norm,
        grad_in,
        taps_all[:CONV],
        taps_all[CONV],
        grad_bias,
        grad_rate,
        grad_skip,
        grad_inner,
        grad_out,
    )


def solution(mesh):
    rows = P(None, "group", "fsdp", None)
    shard = P("fsdp")
    in_specs = (rows, P(None, "group", "fsdp"), rows, shard, P("fsdp", None), P(None, "fsdp"))
    in_specs += (shard,) * 5 + (P("fsdp", None),)
    out_specs = (rows, rows, shard, P("fsdp", None), P(None, "fsdp")) + (shard,) * 5
    out_specs += (P("fsdp", None),)
    return jax.shard_map(
        on_device, mesh=mesh, in_specs=in_specs, out_specs=out_specs, check_vma=False
    )
```

```python
from functools import partial

import jax
import jax.numpy as jnp
from jax import lax
from jax.experimental import pallas as pl
from jax.experimental.pallas import tpu as pltpu
from jax.sharding import PartitionSpec as P

INNER = 4096
HEADS = 64
HEADDIM = 64
STATE = 128
CONV = 4
XBC = 4352
LANES = 128
EPSILON = 1e-05
FAR = -1e30
HIGHEST = lax.Precision.HIGHEST
VMEM = 48 * 1024 * 1024
F32 = jnp.float32
BF16 = jnp.bfloat16


def swap(value, axis, bit):
    count = lax.axis_size(axis)
    with jax.named_scope(f"{axis}_{bit}"):
        return lax.ppermute(value, axis, [(i, i ^ bit) for i in range(count)])


def after(value, *earlier):
    return lax.optimization_barrier((value,) + earlier)[0] if earlier else value


def bits_of(count):
    return [1 << k for k in reversed(range(count.bit_length() - 1))]


def gather_far(piece):
    held = {0: piece}
    for bit in bits_of(lax.axis_size("fsdp"))[:-1]:
        for r, part in list(held.items()):
            held[r ^ bit] = swap(part, "fsdp", bit)
    return held


def gather_near(held, *later):
    for r, part in list(held.items()):
        held[r ^ 1] = swap(after(part, *later), "fsdp", 1)
    return [held[r] for r in range(len(held))]


def gathered(piece):
    return gather_near(gather_far(piece))


def permuted(parts, own):
    stacked = jnp.stack(parts)
    return [
        lax.dynamic_index_in_dim(stacked, own ^ i, 0, keepdims=False) for i in range(len(parts))
    ]


def absolute(parts):
    return permuted(parts, lax.axis_index("fsdp"))


def traded(blocks, send):
    held = {r: {0: block} for r, block in enumerate(blocks)}
    for bit in bits_of(len(blocks)):
        going = [r for r in sorted(held) if r & bit]
        sources = sorted(held[going[0]])
        got = send(jnp.stack([held[r][s] for r in going for s in sources]), bit)
        place = 0
        for r in going:
            for s in sources:
                held[r ^ bit][s ^ bit] = got[place]
                place += 1
            del held[r]
    return [held[0][s] for s in sorted(held[0])]


def traded_weights(in_rows, inner, between):
    own = lax.axis_index("fsdp")
    side = lax.axis_index("group") & 3
    rows = in_rows.shape[1]
    half = inner // 2
    parts = lax.axis_size("fsdp")

    def block(r, kind, first, size):
        at = kind * INNER + (own ^ r) * inner + first
        return lax.dynamic_slice(in_rows, (at, jnp.zeros_like(at)), (size, rows))

    def piece(r, s):
        if s in held[r]:
            return held[r][s]
        return jnp.stack([block(r, kind, 0, inner) for kind in (0, 1)]).reshape(4, half, rows)

    def quarter(r, s):
        if s in held[r]:
            return held[r][s][0]
        return block(r, side // 2, (side & 1) * half, half)

    held = {r: {} for r in range(parts)}
    sources = [0]
    pins = None
    for bit in bits_of(parts):
        going = [r for r in sorted(held) if r & bit]
        order = [(r, s) for r in going for s in sources]
        if bit > 1:
            sent = jnp.stack([quarter(r, s) for r, s in order])
            mine = swap(sent, "fsdp", bit)
            if pins is None:
                pins = between(sent, mine)
            by_x = swap(mine, "group", 1)
            by_z = swap(mine, "group", 2)
            cut = half // 2
            rest = [
                swap(after(by_z[:, :cut], *pins[0]), "group", 1),
                swap(after(by_x[:, cut:], *pins[0]), "group", 2),
            ]
            got = jnp.stack([mine, by_x, by_z, jnp.concatenate(rest, axis=1)], axis=1)
        else:
            got = [swap(after(piece(r, s), *pins[1]), "fsdp", bit) for r, s in order]
        for (r, s), part in zip(order, got):
            held[r ^ bit][s ^ bit] = part
        for r in going:
            del held[r]
        sources += [s ^ bit for s in sources]
    return [piece(0, s) for s in range(parts)]


def scattered(value):
    bit = 1
    while value.shape[0] > 1:
        pairs = value.reshape((value.shape[0] // 2, 2) + value.shape[1:])
        got = swap(pairs[:, 1].astype(BF16), "fsdp", bit)
        value = pairs[:, 0].astype(F32) + got.astype(F32)
        bit *= 2
    return value[0]


def summed(value, axis, kind=F32):
    for bit in bits_of(lax.axis_size(axis))[::-1]:
        value = value + swap(value.astype(kind), axis, bit).astype(F32)
    return value


def lines():
    count = lax.axis_size("group")
    return [list(range(side, count, 2)) for side in (0, 1)]


class Lines:
    def __init__(self):
        self.last = None

    def order(self, value):
        return value if self.last is None else after(value, self.last)

    def scatter(self, value, among=None):
        self.last = lax.psum_scatter(
            self.order(value), "group", scatter_dimension=0, axis_index_groups=among
        )
        return self.last

    def gather(self, value, among=None):
        self.last = lax.all_gather(
            self.order(value), "group", axis=0, axis_index_groups=among
        )
        return self.last


def dot(a, b, contract=((1,), (0,)), precision=None):
    return lax.dot_general(a, b, (contract, ((), ())), precision=precision, preferred_element_type=F32)


def steps(dt_ref, head_ref, tri):
    raw = dt_ref[...] + head_ref[0:1, :]
    size = jnp.maximum(raw, 0.0) + jnp.log1p(jnp.exp(-jnp.abs(raw)))
    log_decay = size * head_ref[1:2, :]
    running = dot(tri, log_decay, precision=HIGHEST)
    return raw, size, log_decay, running


def columns(row, chunk):
    return jnp.broadcast_to(row, (LANES, chunk)).T


def squared(array, chunk):
    return array if chunk == LANES else array[:, :chunk]


def forward_kernel(
    chunk,
    own_ref,
    pre_ref,
    tail_ref,
    gate_ref,
    dt_ref,
    back_ref,
    row_ref,
    taps_ref,
    head_ref,
    skip_ref,
    gain_ref,
    act_ref,
    slope_ref,
    out_ref,
    gained_ref,
    enter_ref,
    stat_ref,
    state,
    window,
    carried,
    flown,
):
    where = pl.program_id(0)
    inner = gate_ref.shape[1]
    channels = act_ref.shape[1]

    @pl.when(where == 0)
    def _():
        state[...] = jnp.zeros_like(state)
        window[0:8, :] = jnp.zeros((8, channels), F32)

    start = (where * chunk).astype(F32)
    seg_row = row_ref[0:1, :]
    seg_col = columns(seg_row, chunk)
    time = lax.broadcasted_iota(jnp.int32, (chunk, LANES), 0).astype(F32) + start
    seen = [(seg_col <= time - back).astype(F32) for back in range(1, CONV)]
    window[8:, :inner] = pre_ref[...].astype(F32)
    window[8:, inner:] = tail_ref[...].astype(F32)
    for at in range(0, channels, LANES):
        lanes = slice(at, at + LANES)
        total = taps_ref[4:5, lanes] + taps_ref[3:4, lanes] * window[8 : 8 + chunk, lanes]
        for back in range(1, CONV):
            total += taps_ref[3 - back : 4 - back, lanes] * (
                window[8 - back : 8 - back + chunk, lanes] * seen[back - 1]
            )
        sig = jax.nn.sigmoid(total)
        act_ref[:, lanes] = (total * sig).astype(BF16)
        slope_ref[:, lanes] = (sig * (1.0 + total * (1.0 - sig))).astype(BF16)
    window[0:8, :] = window[chunk : chunk + 8, :]

    seg_last = seg_row[:, chunk - 1 : chunk]
    down = lax.broadcasted_iota(jnp.int32, (chunk, chunk), 0)
    across = lax.broadcasted_iota(jnp.int32, (chunk, chunk), 1)
    tri = (across <= down).astype(F32)
    _, size, _, running = steps(dt_ref, head_ref, tri)
    running_t = running.T
    size_t = size.T
    b_input = act_ref[:, inner : inner + STATE]
    c_output = act_ref[:, inner + STATE :]
    gram = dot(c_output, b_input, ((1,), (1,)))
    veil = jnp.where((squared(seg_col, chunk) == seg_row) & (across <= down), 0.0, FAR)
    crossing = (seg_col < start).astype(F32)
    ending = (seg_col == seg_last).astype(F32)
    passing = (seg_last < start).astype(F32)
    last = running[chunk - 1 : chunk, :]
    low = lax.broadcasted_iota(jnp.int32, (chunk, LANES), 1) < HEADDIM
    low_row = low[0:1, :]
    entering = state[...].astype(BF16)
    enter_ref[...] = entering
    carried[...] = dot(c_output, entering)
    squares = jnp.zeros((chunk, LANES), F32)
    products = jnp.zeros((chunk, LANES), F32)
    for pair in range(inner // LANES):
        lanes = slice(pair * LANES, (pair + 1) * LANES)
        heads = (2 * pair, 2 * pair + 1)
        x_pair = act_ref[:, lanes].astype(F32)
        run = [running[:, h : h + 1] for h in heads]
        mixing = [
            (jnp.exp(run[k] - running_t[h : h + 1, :] + veil) * gram * size_t[h : h + 1, :]).astype(
                BF16
            )
            for k, h in enumerate(heads)
        ]
        halves = [jnp.where(low, x_pair, 0.0).astype(BF16), jnp.where(low, 0.0, x_pair).astype(BF16)]
        inside = dot(jnp.concatenate(mixing, axis=1), jnp.concatenate(halves, axis=0))
        run_pair = jnp.where(low, run[0], run[1])
        size_pair = jnp.where(low, size[:, heads[0] : heads[0] + 1], size[:, heads[1] : heads[1] + 1])
        last_pair = jnp.where(
            low_row, last[:, heads[0] : heads[0] + 1], last[:, heads[1] : heads[1] + 1]
        )
        ssm = (
            inside
            + carried[:, lanes] * (jnp.exp(run_pair) * crossing)
            + skip_ref[:, lanes] * x_pair
        )
        outflow = jnp.exp(last_pair - run_pair) * ending * size_pair
        flown[:, lanes] = (x_pair * outflow).astype(BF16)
        state[:, lanes] = (jnp.exp(last_pair) * passing) * state[:, lanes]
        gate = gate_ref[:, lanes].astype(F32)
        gated = ssm * (gate * jax.nn.sigmoid(gate))
        out_ref[:, lanes] = ssm.astype(BF16)
        gained = gated * gain_ref[:, lanes]
        gained_ref[:, lanes] = gained.astype(BF16)
        squares += gated * gated
        products += gained * back_ref[:, lanes].astype(F32)
    state[...] += dot(b_input, flown[...], ((0,), (0,)))
    stat_ref[0:1, :] = jnp.sum(squares.T, axis=0, keepdims=True)
    stat_ref[1:2, :] = jnp.sum(products.T, axis=0, keepdims=True)
    stat_ref[2:8, :] = jnp.zeros((6, chunk), F32)


def backward_kernel(
    chunk,
    own_ref,
    act_ref,
    slope_ref,
    pre_ref,
    tail_ref,
    dt_ref,
    grad_ref,
    enter_ref,
    row_ref,
    taps_ref,
    head_ref,
    skip_ref,
    grad_pre_ref,
    grad_dt_ref,
    grad_taps_ref,
    grad_skip_ref,
    grad_head_ref,
    leaving,
    window,
    grad_act,
    row_sums,
    carried,
    fresh,
    into,
    flown,
):
    count = pl.num_programs(0)
    where = count - 1 - pl.program_id(0)
    inner = grad_ref.shape[1]
    channels = act_ref.shape[1]

    @pl.when(pl.program_id(0) == 0)
    def _():
        leaving[...] = jnp.zeros_like(leaving)
        window[chunk:, :] = jnp.zeros((8, channels), F32)
        grad_taps_ref[...] = jnp.zeros_like(grad_taps_ref)
        grad_skip_ref[...] = jnp.zeros_like(grad_skip_ref)
        grad_head_ref[...] = jnp.zeros_like(grad_head_ref)
        row_sums[...] = jnp.zeros_like(row_sums)

    start = (where * chunk).astype(F32)
    seg_row = row_ref[0:1, :]
    seg_col = columns(seg_row, chunk)
    seg_last = seg_row[:, chunk - 1 : chunk]
    down = lax.broadcasted_iota(jnp.int32, (chunk, chunk), 0)
    across = lax.broadcasted_iota(jnp.int32, (chunk, chunk), 1)
    tri = (across <= down).astype(F32)
    raw, size, log_decay, running = steps(dt_ref, head_ref, tri)
    running_t = running.T
    b_input = act_ref[:, inner : inner + STATE]
    c_output = act_ref[:, inner + STATE :]
    gram = dot(b_input, c_output, ((1,), (1,)))
    veil = jnp.where((squared(seg_col, chunk) == seg_row) & (down <= across), 0.0, FAR)
    crossing = (seg_col < start).astype(F32)
    ending = (seg_col == seg_last).astype(F32)
    passing = (seg_last < start).astype(F32)
    last = running[chunk - 1 : chunk, :]
    lane = lax.broadcasted_iota(jnp.int32, (chunk, LANES), 1)
    low = lane < HEADDIM
    low_row = low[0:1, :]
    lane_row = lane[0:1, :]
    left_low = leaving[...].astype(BF16)
    entering = enter_ref[...]
    carried[...] = dot(c_output, entering)
    fresh[...] = dot(b_input, left_low)
    grad_gram = jnp.zeros((chunk, chunk), F32)
    size_grad = jnp.zeros((chunk, LANES), F32)
    carry_grad = jnp.zeros((chunk, LANES), F32)
    total_grad = jnp.zeros((1, LANES), F32)
    for pair in range(inner // LANES):
        lanes = slice(pair * LANES, (pair + 1) * LANES)
        heads = (2 * pair, 2 * pair + 1)
        x_low = act_ref[:, lanes]
        x_pair = x_low.astype(F32)
        grad = grad_ref[:, lanes].astype(F32)
        halves = (low, jnp.logical_not(low))
        run = [running[:, h : h + 1] for h in heads]
        sizes = [size[:, h : h + 1] for h in heads]
        run_pair = jnp.where(low, run[0], run[1])
        size_pair = jnp.where(low, sizes[0], sizes[1])
        last_pair = jnp.where(
            low_row, last[:, heads[0] : heads[0] + 1], last[:, heads[1] : heads[1] + 1]
        )
        left = leaving[:, lanes]
        inflow = jnp.exp(run_pair) * crossing
        outflow = jnp.exp(last_pair - run_pair) * ending
        into_here = grad * inflow
        into[:, lanes] = into_here.astype(BF16)
        carry_here = into_here * carried[:, lanes]
        fresh_back = fresh[:, lanes] * outflow
        flown_here = x_pair * fresh_back
        flown[:, lanes] = (x_pair * outflow * size_pair).astype(BF16)
        whole = jnp.exp(last_pair) * passing
        kept = whole * jnp.sum(left * enter_ref[:, lanes].astype(F32), axis=0, keepdims=True)
        kept += jnp.sum(flown_here * size_pair, axis=0, keepdims=True)
        leaving[:, lanes] = whole * left
        both = jnp.concatenate(
            [jnp.where(low, grad, 0.0).astype(BF16), jnp.where(low, 0.0, grad).astype(BF16)], axis=0
        )
        back_both = dot(x_low, both, ((1,), (1,)))
        weights = []
        for k, h in enumerate(heads):
            mine = halves[k]
            decay = jnp.exp(running_t[h : h + 1, :] - run[k] + veil)
            weight = decay * gram
            weights.append((weight * sizes[k]).astype(BF16))
            back = back_both[:, k * chunk : (k + 1) * chunk]
            grad_gram += back * decay * sizes[k]
            straight = back * weight
            row_sums[h : h + 1, :] = jnp.sum(straight * sizes[k], axis=0, keepdims=True)
            flown_mine = jnp.where(mine, flown_here, 0.0)
            if chunk == LANES:
                size_here = jnp.sum(straight + flown_mine, axis=1, keepdims=True)
            else:
                size_here = jnp.sum(straight, axis=1, keepdims=True) + jnp.sum(
                    flown_mine, axis=1, keepdims=True
                )
            carry_mine = jnp.sum(jnp.where(mine, carry_here, 0.0), axis=1, keepdims=True)
            here = lane == h
            size_grad = jnp.where(here, size_here, size_grad)
            carry_grad = jnp.where(here, carry_mine, carry_grad)
            total_here = jnp.sum(jnp.where(mine[0:1, :], kept, 0.0), axis=1, keepdims=True)
            total_grad = jnp.where(lane_row == h, total_here, total_grad)
        grad_act[:, lanes] = (
            dot(jnp.concatenate(weights, axis=1), both)
            + fresh_back * size_pair
            + skip_ref[:, lanes] * grad
        )
        grad_skip_ref[0:1, lanes] += jnp.sum(grad * x_pair, axis=0, keepdims=True)
    grad_gram_low = grad_gram.astype(BF16)
    grad_act[:, inner : inner + STATE] = dot(grad_gram_low, c_output) + dot(
        flown[...], left_low, ((1,), (1,))
    )
    grad_act[:, inner + STATE :] = dot(grad_gram_low, b_input, ((0,), (0,))) + dot(
        into[...], entering, ((1,), (1,))
    )
    leaving[...] += dot(c_output, into[...], ((0,), (0,)))
    row_t = row_sums[...].T
    grad_run = row_t + carry_grad - size * size_grad
    upper = (across >= down).astype(F32)
    grad_decay = dot(upper, grad_run, precision=HIGHEST) + total_grad
    grad_size = grad_decay * head_ref[1:2, :] + size_grad
    grad_raw = jnp.where(lane < inner // HEADDIM, grad_size * jax.nn.sigmoid(raw), 0.0)
    grad_dt_ref[...] = grad_raw.astype(BF16)
    grad_head_ref[0:1, :] += jnp.sum(grad_raw, axis=0, keepdims=True)
    grad_head_ref[1:2, :] += jnp.sum(grad_decay * log_decay, axis=0, keepdims=True)

    same = [
        (columns(row_ref[ahead : ahead + 1, :], chunk) == seg_col).astype(F32)
        for ahead in range(1, CONV)
    ]
    for at in range(0, channels, LANES):
        lanes = slice(at, at + LANES)
        grad_sum = grad_act[:, lanes] * slope_ref[:, lanes].astype(F32)
        window[0:chunk, lanes] = grad_sum
        if at < inner:
            pre = pre_ref[:, lanes].astype(F32)
        else:
            pre = tail_ref[:, at - inner : at - inner + LANES].astype(F32)
        grad_pre = taps_ref[3:4, lanes] * grad_sum
        grad_taps_ref[3:4, lanes] += jnp.sum(pre * grad_sum, axis=0, keepdims=True)
        grad_taps_ref[4:5, lanes] += jnp.sum(grad_sum, axis=0, keepdims=True)
        for ahead in range(1, CONV):
            later = window[ahead : ahead + chunk, lanes] * same[ahead - 1]
            grad_pre += taps_ref[3 - ahead : 4 - ahead, lanes] * later
            grad_taps_ref[3 - ahead : 4 - ahead, lanes] += jnp.sum(
                pre * later, axis=0, keepdims=True
            )
        grad_pre_ref[:, lanes] = grad_pre.astype(BF16)
    window[chunk:, :] = window[0:8, :]


def scan_calls(parts, tok_count, inner):
    chunk = min(LANES, tok_count)
    per_part = tok_count // chunk
    count = parts * per_part
    channels = inner + 2 * STATE
    tokens = parts * tok_count

    def blocks(flip):
        def time(step):
            return count - 1 - step if flip else step

        def place(step, own):
            t = time(step)
            return lax.bitwise_xor(t // per_part, own[0]) * per_part + t % per_part

        def tok(width):
            return pl.BlockSpec((chunk, width), lambda step, own: (place(step, own), 0))

        row = pl.BlockSpec((None, 8, chunk), lambda step, own: (time(step), 0, 0))
        states = pl.BlockSpec((None, STATE, inner), lambda step, own: (time(step), 0, 0))

        def const(rows, width):
            return pl.BlockSpec((rows, width), lambda step, own: (0, 0))

        return tok, row, states, const

    def scan(kernel, ins, outs, shapes, scratch):
        return pl.pallas_call(
            partial(kernel, chunk),
            grid_spec=pltpu.PrefetchScalarGridSpec(
                num_scalar_prefetch=1,
                grid=(count,),
                in_specs=ins,
                out_specs=outs,
                scratch_shapes=scratch,
            ),
            out_shape=shapes,
            compiler_params=pltpu.CompilerParams(
                dimension_semantics=("arbitrary",), vmem_limit_bytes=VMEM
            ),
            cost_estimate=COST,
        )

    struct = jax.ShapeDtypeStruct
    tok, row, states, const = blocks(False)
    forward = scan(
        forward_kernel,
        [tok(inner), tok(2 * STATE), tok(inner), tok(LANES), tok(inner), row]
        + [const(8, channels), const(8, LANES), const(1, inner), const(1, inner)],
        [tok(channels), tok(channels), tok(inner), tok(inner), states, row],
        [
            struct((tokens, channels), BF16),
            struct((tokens, channels), BF16),
            struct((tokens, inner), BF16),
            struct((tokens, inner), BF16),
            struct((count, STATE, inner), BF16),
            struct((count, 8, chunk), F32),
        ],
        [
            pltpu.VMEM((STATE, inner), F32),
            pltpu.VMEM((chunk + 8, channels), F32),
            pltpu.VMEM((chunk, inner), F32),
            pltpu.VMEM((chunk, inner), BF16),
        ],
    )
    tok, row, states, const = blocks(True)
    backward = scan(
        backward_kernel,
        [tok(channels), tok(channels), tok(inner), tok(2 * STATE), tok(LANES)]
        + [tok(inner), states, row]
        + [const(8, channels), const(8, LANES), const(1, inner)],
        [tok(channels), tok(LANES), const(8, channels), const(8, inner), const(8, LANES)],
        [
            struct((tokens, channels), BF16),
            struct((tokens, LANES), BF16),
            struct((8, channels), F32),
            struct((8, inner), F32),
            struct((8, LANES), F32),
        ],
        [
            pltpu.VMEM((STATE, inner), F32),
            pltpu.VMEM((chunk + 8, channels), F32),
            pltpu.VMEM((chunk, channels), F32),
            pltpu.VMEM((LANES, chunk), F32),
            pltpu.VMEM((chunk, inner), F32),
            pltpu.VMEM((chunk, inner), F32),
            pltpu.VMEM((chunk, inner), BF16),
            pltpu.VMEM((chunk, inner), BF16),
        ],
    )
    return forward, backward


NN = ((1,), (0,))
NT = ((1,), (1,))
TN = ((0,), (0,))
COST = pl.CostEstimate(flops=1, bytes_accessed=1, transcendentals=0)


def call(kernel, grid, ins, outs, shapes, args, scratch=()):
    return pl.pallas_call(
        kernel,
        grid_spec=pltpu.PrefetchScalarGridSpec(
            num_scalar_prefetch=1,
            grid=grid,
            in_specs=ins,
            out_specs=outs,
            scratch_shapes=scratch,
        ),
        out_shape=shapes,
        compiler_params=pltpu.CompilerParams(
            dimension_semantics=("arbitrary",) * len(grid), vmem_limit_bytes=VMEM
        ),
        cost_estimate=COST,
    )(*args)


def fixed(shape):
    return pl.BlockSpec(shape, lambda i, own: (0,) * len(shape))


def own_heads(own, heads):
    head = lax.broadcasted_iota(jnp.int32, (HEADS, LANES), 0)
    lane = lax.broadcasted_iota(jnp.int32, (HEADS, LANES), 1)
    return ((head == own * heads + lane) & (lane < heads)).astype(F32)


def project_kernel(parts, own_ref, *refs):
    tok_refs, weights, tails = refs[:parts], refs[parts : 2 * parts], refs[2 * parts : 3 * parts]
    gain_ref, normed_ref, gate_ref, pre_ref, tail_ref, dt_ref, ordered = refs[3 * parts :]
    at = pl.program_id(0)
    rows = tails[0].shape[1]
    tok_count = tok_refs[0].shape[0]

    @pl.when(at == 0)
    def _():
        for r in range(parts):
            values = tok_refs[r][...].astype(F32)
            mean = jnp.mean(values * values, axis=-1, keepdims=True)
            normed_ref[r * tok_count : (r + 1) * tok_count, :] = (
                values * lax.rsqrt(mean + EPSILON) * gain_ref[...]
            ).astype(BF16)
        for s in range(parts):
            lanes = pl.ds(pl.multiple_of(lax.bitwise_xor(own_ref[0], s) * rows, LANES), rows)
            ordered[:, s * rows : (s + 1) * rows] = normed_ref[:, lanes]

    def total(refs):
        return dot(ordered[...], jnp.concatenate([ref[...] for ref in refs], axis=1), NT)

    @pl.when(at < 2)
    def _():
        gate_ref[...] = total(weights).astype(BF16)

    @pl.when((at >= 2) & (at < 4))
    def _():
        pre_ref[...] = total(weights).astype(BF16)

    @pl.when(at == 4)
    def _():
        rest = total(tails)
        tail_ref[...] = rest[:, : 2 * STATE].astype(BF16)
        pick = own_heads(own_ref[0], HEADS // parts)
        dt_ref[...] = dot(rest[:, 2 * STATE :], pick, precision=HIGHEST)


def project(own_arg, tok_parts, weights, tails, gain):
    parts, (tok_count, width) = len(tok_parts), tok_parts[0].shape
    half, rows = weights[0].shape[1:]
    tokens = parts * tok_count

    def near(i, own):
        return (jnp.minimum(i, 3), 0, 0)

    def far(i, own):
        return (lax.bitwise_xor(jnp.minimum(i, 3), own[1]), 0, 0)

    struct = jax.ShapeDtypeStruct
    return call(
        partial(project_kernel, parts),
        (5,),
        [fixed((tok_count, width))] * parts
        + [pl.BlockSpec((None, half, rows), far if s > 1 else near) for s in range(parts)]
        + [fixed(tails[0].shape)] * parts
        + [fixed((1, width))],
        [
            fixed((tokens, width)),
            pl.BlockSpec((tokens, half), lambda i, own: (0, jnp.minimum(i, 1))),
            pl.BlockSpec((tokens, half), lambda i, own: (0, jnp.clip(i - 2, 0, 1))),
            fixed((tokens, 2 * STATE)),
            fixed((tokens, LANES)),
        ],
        [
            struct((tokens, width), BF16),
            struct((tokens, 2 * half), BF16),
            struct((tokens, 2 * half), BF16),
            struct((tokens, 2 * STATE), BF16),
            struct((tokens, LANES), F32),
        ],
        (own_arg, *tok_parts, *weights, *tails, gain[None]),
        [pltpu.VMEM((tokens, width), BF16)],
    )


def back_kernel(parts, own_ref, *refs):
    weight_ref, all_ref, back_ref = refs[parts:]
    tok_count = refs[0].shape[0]

    @pl.when(pl.program_id(0) == 0)
    def _():
        for r in range(parts):
            all_ref[r * tok_count : (r + 1) * tok_count, :] = refs[r][...]

    back_ref[...] = dot(all_ref[...], weight_ref[...], NT).astype(BF16)


def project_back(own_arg, cot_parts, weight):
    parts, (tok_count, width) = len(cot_parts), cot_parts[0].shape
    inner = weight.shape[0]
    block = min(256, inner)
    tokens = parts * tok_count
    struct = jax.ShapeDtypeStruct
    return call(
        partial(back_kernel, parts),
        (inner // block,),
        [fixed((tok_count, width))] * parts
        + [pl.BlockSpec((block, width), lambda i, own: (i, 0))],
        [fixed((tokens, width)), pl.BlockSpec((tokens, block), lambda i, own: (0, i))],
        [struct((tokens, width), BF16), struct((tokens, inner), BF16)],
        (own_arg, *cot_parts, weight),
    )


def split_rows(value, even_ref, odd_ref):
    size = even_ref.shape[0]
    even_ref[...] = value[:size].astype(BF16)
    odd_ref[...] = value[size:].astype(BF16)


def split_outs(tok_count, parts, width):
    spec = pl.BlockSpec((None, tok_count, width), lambda i, own: (i, 0, 0))
    shape = jax.ShapeDtypeStruct((parts // 2, tok_count, width), BF16)
    return [spec, spec], [shape, shape]


def out_kernel(own_ref, a_ref, b_ref, even_ref, odd_ref):
    split_rows(dot(a_ref[...], b_ref[...]), even_ref, odd_ref)


def project_out(own_arg, gained, weight, parts):
    (tokens, inner), width = gained.shape, weight.shape[1]
    tok_count = tokens // parts
    specs, shapes = split_outs(tok_count, parts, width)
    return call(
        out_kernel,
        (parts // 2,),
        [pl.BlockSpec((2 * tok_count, inner), lambda i, own: (i, 0)), fixed((inner, width))],
        specs,
        shapes,
        (own_arg, gained, weight),
    )


def into_kernel(parts, own_ref, gate_ref, pre_ref, dt_ref, *refs):
    weights, tails = refs[:parts], refs[parts : 2 * parts]
    even_ref, odd_ref = refs[2 * parts :]
    half, rows = weights[0].shape[1:]
    pick = own_heads(own_ref[0], HEADS // parts).astype(BF16)
    grad_dt = dot(dt_ref[...], pick, NT).astype(BF16)
    left = jnp.concatenate([gate_ref[...], pre_ref[...], grad_dt], axis=1)
    for s in range(parts):
        order = [lax.bitwise_xor(q, own_ref[1]) if s > 1 else q for q in range(4)]
        right = jnp.concatenate([weights[s][q] for q in order] + [tails[s][...]], axis=0)
        lanes = pl.ds(pl.multiple_of(lax.bitwise_xor(own_ref[0], s) * rows, LANES), rows)
        split_rows(dot(left, right), even_ref.at[:, lanes], odd_ref.at[:, lanes])


def project_into(own_arg, grad_gate, grad_pre, grad_dt, weights, tails):
    parts = len(weights)
    (tokens, inner), channels = grad_gate.shape, grad_pre.shape[1]
    width = parts * weights[0].shape[2]
    tok_count = tokens // parts

    def tok(size):
        return pl.BlockSpec((2 * tok_count, size), lambda i, own: (i, 0))

    specs, shapes = split_outs(tok_count, parts, width)
    return call(
        partial(into_kernel, parts),
        (parts // 2,),
        [tok(inner), tok(channels), tok(LANES)]
        + [fixed(w.shape) for w in weights]
        + [fixed(r.shape) for r in tails],
        specs,
        shapes,
        (own_arg, grad_gate, grad_pre, grad_dt, *weights, *tails),
    )


def tail_kernel(count, parts, own_ref, *refs):
    pres, dts, normed = refs[:count], refs[count : 2 * count], refs[2 * count : 3 * count]
    even_ref, odd_ref = refs[3 * count :]
    pick = own_heads(own_ref[0], HEADS // parts)

    def total(lefts):
        terms = [dot(a[...], b[...], TN) for a, b in zip(lefts, normed)]
        return sum(terms[1:], terms[0])

    value = [total(pres), dot(pick.astype(BF16), total(dts).astype(BF16))]
    value = jnp.concatenate(value, axis=0).astype(BF16)

    @pl.when(pl.program_id(0) % 2 == 0)
    def _():
        even_ref[...] = value

    @pl.when(pl.program_id(0) % 2 == 1)
    def _():
        odd_ref[...] = value


def tail_grad(own_arg, grad_pres, grad_dts, normed, parts):
    (tokens, channels), width = grad_pres[0].shape, normed[0].shape[1]
    count, columns, rows = len(normed), 2 * STATE + HEADS, width // parts
    spec = pl.BlockSpec((None, columns, rows), lambda r, own: (r // 2, 0, 0))
    shape = jax.ShapeDtypeStruct((parts // 2, columns, rows), BF16)
    return call(
        partial(tail_kernel, count, parts),
        (parts,),
        [pl.BlockSpec((tokens, 2 * STATE), lambda r, own: (0, channels // (2 * STATE) - 1))] * count
        + [fixed((tokens, LANES))] * count
        + [pl.BlockSpec((tokens, rows), lambda r, own: (0, lax.bitwise_xor(own[0], r)))] * count,
        [spec, spec],
        [shape, shape],
        (own_arg, *grad_pres, *grad_dts, *normed),
    )


def add_kernel(own_ref, a_ref, b_ref, keep_ref, send_ref):
    keep_ref[...] = a_ref[0].astype(F32) + b_ref[0].astype(F32)
    send_ref[...] = (a_ref[1].astype(F32) + b_ref[1].astype(F32)).astype(BF16)


def add_parts(own_arg, even, got):
    _, size, width = even.shape
    block = size // 2
    both = pl.BlockSpec((2, block, width), lambda i, own: (0, i, 0))
    one = pl.BlockSpec((block, width), lambda i, own: (i, 0))
    struct = jax.ShapeDtypeStruct
    return call(
        add_kernel,
        (2,),
        [both, both],
        [one, one],
        [struct((size, width), F32), struct((size, width), BF16)],
        (own_arg, even, got),
    )


class Split:
    def __init__(self, own_arg, parts):
        self.own_arg = own_arg
        self.even, self.odd = parts
        self.plain = self.even.shape[0] != 2
        self.sent = self.even
        if not self.plain:
            self.got = swap(self.odd, "fsdp", 1)

    def middle(self, *earlier):
        if not self.plain:
            got = after(self.got, *earlier)
            self.keep, self.sent = add_parts(self.own_arg, self.even, got)
            self.got = swap(self.sent, "fsdp", 2)
        return self.sent

    def final(self, *earlier):
        if not self.plain:
            return self.keep, after(self.got, *earlier)
        every = jnp.stack([self.even, self.odd], axis=1)
        every = every.reshape((-1,) + self.even.shape[1:])
        total = scattered(after(every, *earlier))
        return total, jnp.zeros(total.shape, BF16)


def mixed_kernel(own_ref, tok_ref, scale_ref, keep_ref, got_ref, out_ref):
    total = keep_ref[...] + got_ref[...].astype(F32)
    out_ref[...] = (tok_ref[...].astype(F32) + total * scale_ref[...]).astype(BF16)


def mixed_rows(own_arg, tok, scale, terms):
    size, width = tok.shape
    block = min(128, size)
    one = pl.BlockSpec((block, width), lambda i, own: (i, 0))
    return call(
        mixed_kernel,
        (size // block,),
        [one, pl.BlockSpec((block, 1), lambda i, own: (i, 0)), one, one],
        [one],
        [jax.ShapeDtypeStruct((size, width), BF16)],
        (own_arg, tok, scale, *terms),
    )[0]


def norm_kernel(own_ref, tok_ref, cot_ref, gain_ref, keep_ref, got_ref, out_ref, sum_ref):
    @pl.when(pl.program_id(0) == 0)
    def _():
        sum_ref[...] = jnp.zeros_like(sum_ref)

    tok = tok_ref[...].astype(F32)
    inverse = lax.rsqrt(jnp.mean(tok * tok, axis=-1, keepdims=True) + EPSILON)
    hat = tok * inverse
    part = keep_ref[...] + got_ref[...].astype(F32)
    through = part * gain_ref[...]
    here = inverse * (through - hat * jnp.mean(hat * through, axis=-1, keepdims=True))
    out_ref[...] = (cot_ref[...].astype(F32) + here).astype(BF16)
    sum_ref[0:1, :] += jnp.sum(part * hat, axis=0, keepdims=True)


def norm_rows(own_arg, tok, cot, gain, terms):
    size, width = tok.shape
    block = min(128, size)
    one = pl.BlockSpec((block, width), lambda i, own: (i, 0))
    return call(
        norm_kernel,
        (size // block,),
        [one, one, fixed((1, width)), one, one],
        [one, fixed((8, width))],
        [jax.ShapeDtypeStruct((size, width), BF16), jax.ShapeDtypeStruct((8, width), F32)],
        (own_arg, tok, cot, gain[None], *terms),
    )


def join_kernel(own_ref, a_ref, b_ref, out_ref):
    out_ref[...] = (a_ref[...].astype(F32) + b_ref[...].astype(F32)).astype(BF16)


def join(own_arg, keep, got):
    size, width = keep.shape
    one = pl.BlockSpec((size // 4, width), lambda i, own: (i, 0))
    return call(
        join_kernel,
        (4,),
        [one, one],
        [one],
        [jax.ShapeDtypeStruct((size, width), BF16)],
        (own_arg, keep, got),
    )[0]


def pick_kernel(order, own_ref, *refs):
    out_ref = refs[-1]
    rows = out_ref.shape[-1]
    for i, (ref, block, lane) in enumerate(order):
        if lane:
            lanes = pl.ds(pl.multiple_of(lax.bitwise_xor(own_ref[0], block) * rows, LANES), rows)
            out_ref[i] = refs[ref][:, lanes]
        else:
            out_ref[i] = refs[ref][block]


def picked(own_arg, order, args, rows):
    shape = (len(order), args[0].shape[0], rows)
    return call(
        partial(pick_kernel, order),
        (1,),
        [fixed(arg.shape) for arg in args],
        [fixed(shape)],
        [jax.ShapeDtypeStruct(shape, BF16)],
        (own_arg, *args),
    )[0]


def place_kernel(own_ref, half_ref, far_ref, near_ref, out_ref):
    rows = out_ref.shape[-1]
    own = own_ref[0]
    lanes = pl.ds(pl.multiple_of(own * rows, LANES), rows)
    out_ref[own] = half_ref[:, lanes]
    out_ref[lax.bitwise_xor(own, 2)] = far_ref[0]
    out_ref[lax.bitwise_xor(own, 1)] = near_ref[0]
    out_ref[lax.bitwise_xor(own, 3)] = near_ref[1]


class Trade:
    def __init__(self, own_arg, half, parts):
        self.own_arg, self.half, self.parts = own_arg, half, parts
        self.rows = half.shape[1] // parts
        self.sent = half
        self.plain = parts != 4
        if not self.plain:
            self.sent = picked(own_arg, [(0, 2, True), (0, 3, True)], [half], self.rows)
            self.far = swap(self.sent, "fsdp", 2)

    def middle(self, *earlier):
        if not self.plain:
            self.far = after(self.far, *earlier)
            order = [(0, 1, True), (1, 1, False)]
            self.sent = picked(self.own_arg, order, [self.half, self.far], self.rows)
            self.near = swap(self.sent, "fsdp", 1)
        return self.sent

    def final(self, *earlier):
        if self.plain:
            own = lax.axis_index("fsdp")
            here = [
                lax.dynamic_slice_in_dim(self.half, (own ^ r) * self.rows, self.rows, 1)
                for r in range(self.parts)
            ]
            here = traded(here, lambda value, bit: swap(value, "fsdp", bit))
            return jnp.stack(absolute(here))
        near = after(self.near, *earlier)
        shape = (self.parts, self.half.shape[0], self.rows)
        return call(
            place_kernel,
            (1,),
            [fixed(self.half.shape), fixed(self.far.shape), fixed(near.shape)],
            [fixed(shape)],
            [jax.ShapeDtypeStruct(shape, BF16)],
            (self.own_arg, self.half, self.far, near),
        )[0]


def weight_kernel(count, own_ref, *refs):
    out_ref = refs[-1]
    total = dot(refs[0][...], refs[count][...], TN)
    for m in range(1, count):
        total += dot(refs[m][...], refs[count + m][...], TN)
    out_ref[...] = total.astype(out_ref.dtype)


def half_of(own, kept):
    return lax.bitwise_xor(own[1] & 1, 0 if kept else 1)


def weight_grad(own_arg, lefts, rights, inner, kept):
    tokens, width = rights[0].shape
    half, block = inner // 2, 512
    return call(
        partial(weight_kernel, len(lefts)),
        (width // block,),
        [pl.BlockSpec((tokens, half), lambda i, own: (0, half_of(own, kept)))] * len(lefts)
        + [pl.BlockSpec((tokens, block), lambda i, own: (0, i))] * len(rights),
        [pl.BlockSpec((half, block), lambda i, own: (0, i))],
        [jax.ShapeDtypeStruct((half, width), BF16)],
        (own_arg, *lefts, *rights),
    )[0]


def gate_kernel(micro, chunk, per_part, own_ref, *refs):
    gain_ref, refs = refs[0], refs[1:]
    ssm, gate, back, stat, normed = (refs[k * micro : (k + 1) * micro] for k in range(5))
    outs = refs[5 * micro :]
    grad_ssm, grad_gate, gated_all = (outs[k * micro : (k + 1) * micro] for k in range(3))
    grad_gain_ref, out_ref = outs[3 * micro :]
    count = stat[0].shape[0]
    half = gain_ref.shape[1]

    grad_gain_ref[...] = jnp.zeros_like(grad_gain_ref)

    def step(t, carry):
        place = lax.bitwise_xor(t // per_part, own_ref[0]) * per_part + t % per_part
        rows = pl.ds(pl.multiple_of(place * chunk, chunk), chunk)
        for m in range(micro):
            sums = stat[m][t]
            scale = lax.rsqrt(sums[0:1, :] * (1.0 / INNER) + EPSILON)
            shift = scale * scale * scale * sums[1:2, :] * (1.0 / INNER)
            scale = columns(scale, chunk)
            shift = columns(shift, chunk)
            for at in range(0, half, LANES):
                lanes = slice(at, at + LANES)
                out = ssm[m][rows, lanes].astype(F32)
                branch = gate[m][rows, lanes].astype(F32)
                grad = back[m][rows, lanes].astype(F32)
                sig = jax.nn.sigmoid(branch)
                silu = branch * sig
                gated = out * silu
                scaled = gated * scale
                gain = gain_ref[:, lanes]
                grad_gated = scale * (gain * grad) - gated * shift
                grad_ssm[m][rows, lanes] = (grad_gated * silu).astype(BF16)
                grad_gate[m][rows, lanes] = (
                    grad_gated * out * (sig * (1.0 + branch * (1.0 - sig)))
                ).astype(BF16)
                gated_all[m][rows, lanes] = (scaled * gain).astype(BF16)
                grad_gain_ref[0:1, lanes] += jnp.sum(scaled * grad, axis=0, keepdims=True)
        return carry

    lax.fori_loop(0, count, step, 0)

    terms = [dot(a[...], b[...], TN) for a, b in zip(grad_gate, normed)]
    out_ref[...] = sum(terms[1:], terms[0]).astype(BF16).reshape(out_ref.shape)


def gate_grads(own_arg, scans, stats, normed, gain, per_part, lines):
    micro = len(scans)
    (tokens, inner), width = scans[0][0].shape, normed[0].shape[1]
    share = inner // 2 // lines
    taken = max(1, min(lines, 256 // share))
    block = taken * share
    chunk = stats[0].shape[2]
    cols = pl.BlockSpec((tokens, block), lambda i, own: (0, i))
    row = pl.BlockSpec((1, block), lambda i, own: (0, i))
    sums = pl.BlockSpec((8, block), lambda i, own: (0, i))
    struct = jax.ShapeDtypeStruct
    outs = call(
        partial(gate_kernel, micro, chunk, per_part),
        (inner // block,),
        [row] + [cols] * (3 * micro) + [fixed(stats[0].shape)] * micro + [fixed((tokens, width))] * micro,
        [cols] * (3 * micro)
        + [sums]
        + [
            pl.BlockSpec(
                (taken, None, share, width),
                lambda i, own: (i % (lines // taken), i // (lines // taken), 0, 0),
            )
        ],
        [struct((tokens, inner), BF16)] * (3 * micro)
        + [struct((8, inner), F32), struct((lines, 2, share, width), BF16)],
        (own_arg, gain, *[scan[k] for k in range(3) for scan in scans], *stats, *normed),
    )
    split = [outs[k * micro : (k + 1) * micro] for k in range(3)]
    return split + list(outs[3 * micro :])


def fill_kernel(own_ref, part_ref, *refs):
    out_ref = refs[-1]
    out_ref[...] = part_ref[...].reshape(out_ref.shape).astype(F32)


def fill(own_arg, whole, rows, part, grid, part_spec, out_spec):
    width = part.shape[-1]
    return pl.pallas_call(
        fill_kernel,
        grid_spec=pltpu.PrefetchScalarGridSpec(
            num_scalar_prefetch=1,
            grid=grid,
            in_specs=[part_spec] + [pl.BlockSpec(memory_space=pl.ANY)] * (whole is not None),
            out_specs=out_spec,
        ),
        out_shape=jax.ShapeDtypeStruct((rows, width), F32),
        input_output_aliases={} if whole is None else {2: 0},
        compiler_params=pltpu.CompilerParams(
            dimension_semantics=("arbitrary",) * len(grid), vmem_limit_bytes=VMEM
        ),
        cost_estimate=COST,
    )(*([own_arg, part] + ([] if whole is None else [whole])))


IN_ROWS = 2 * INNER + 2 * STATE + HEADS


def fill_lines(own_arg, whole, part, kept):
    lines, parts, share, rows = part.shape
    return fill(
        own_arg,
        whole,
        IN_ROWS,
        part,
        (parts,),
        pl.BlockSpec((lines, None, share, rows), lambda f, own: (0, f, 0, 0)),
        pl.BlockSpec((lines * share, rows), lambda f, own: (2 * f + half_of(own, kept), 0)),
    )


def fill_tail(own_arg, whole, part):
    return fill(
        own_arg,
        whole,
        IN_ROWS,
        part,
        (part.shape[0] // HEADS,),
        pl.BlockSpec((HEADS, part.shape[1]), lambda i, own: (i, 0)),
        pl.BlockSpec((HEADS, part.shape[1]), lambda i, own: (2 * INNER // HEADS + i, 0)),
    )


def fill_heads(own_arg, whole, part, first):
    lines, _, parts, share, rows = part.shape
    size = lines * share
    return fill(
        own_arg,
        whole,
        IN_ROWS,
        part,
        (parts, 2),
        pl.BlockSpec((lines, None, None, share, rows), lambda f, k, own: (0, k, f, 0, 0)),
        pl.BlockSpec((size, rows), lambda f, k, own: (first // size + 2 * f + k, 0)),
    )


def on_device(
    tokens,
    segment_ids,
    cotangent,
    norm_gain,
    in_weight,
    conv_weight,
    conv_bias,
    dt_bias,
    a_log,
    skip_d,
    inner_gain,
    out_weight,
):
    micro, _, tok_count, width = tokens.shape
    parts = lax.axis_size("fsdp")
    groups = lax.axis_size("group")
    own = lax.axis_index("fsdp")
    inner = INNER // parts
    heads = HEADS // parts
    channels = inner + 2 * STATE
    rows = width // parts
    seq = tok_count * parts
    chunk = min(LANES, tok_count)
    forward, backward = scan_calls(parts, tok_count, inner)
    side = lax.axis_index("group") & 3
    own_arg = jnp.stack([own, side]).astype(jnp.int32)
    along = Lines()

    def small(sent):
        taps_here = jnp.concatenate([conv_weight, conv_bias[None]], axis=0).astype(F32)
        packed = jnp.concatenate(
            [
                norm_gain.astype(F32),
                taps_here.reshape(-1),
                segment_ids.astype(F32).reshape(-1),
            ]
        )
        held = gather_far(after(packed, sent))
        packed = jnp.stack(absolute(gather_near(held)))
        cut = norm_gain.shape[0]
        gain_norm = packed[:, :cut].reshape(-1)
        taps_size = taps_here.size
        taps = packed[:, cut : cut + taps_size].reshape(parts, CONV + 1, -1)
        taps = taps.transpose(1, 0, 2).reshape(CONV + 1, XBC)
        seg = packed[:, cut + taps_size :].reshape(parts, micro, tok_count)
        seg = seg.transpose(1, 0, 2).reshape(micro, seq)
        taps = jnp.concatenate(
            [lax.dynamic_slice_in_dim(taps, own * inner, inner, 1), taps[:, INNER:]], axis=1
        )
        taps = jnp.pad(taps, ((0, 8 - CONV - 1), (0, 0)))
        seg_rows = [seg] + [
            jnp.pad(seg[:, ahead:], ((0, 0), (0, ahead)), constant_values=-1.0)
            for ahead in range(1, CONV)
        ]
        seg_rows = jnp.stack([part.reshape(micro, -1, chunk) for part in seg_rows], axis=2)
        seg_rows = jnp.pad(seg_rows, ((0, 0), (0, 0), (0, 8 - CONV), (0, 0)))
        head_row = jnp.concatenate(
            [dt_bias.astype(F32)[None], -jnp.exp(a_log.astype(F32))[None]], axis=0
        )
        head_row = jnp.pad(head_row, ((0, 6), (0, LANES - heads)))
        skip_row = jnp.repeat(skip_d.astype(F32), HEADDIM)[None]
        gain_row = inner_gain.astype(F32)[None]
        return held[parts // 2], (gain_norm, taps, seg_rows, head_row, skip_row, gain_row)

    in_rows = in_weight.T
    started = {}

    def between(sent, got):
        packed, started["small"] = small(sent)
        started["tok"] = [gather_far(after(tokens[0, 0], got))]
        started["tail"] = gather_far(after(in_rows[2 * INNER :], got))
        first = started["tok"][0][parts // 2]
        started["tok"] += [gather_far(after(tokens[m, 0], first)) for m in range(1, micro)]
        started["cot"] = [gather_far(after(cotangent[0, 0], first))]
        return [first, packed], [started["tail"][parts // 2], *started["small"]]

    with jax.named_scope("weights"):
        weights = traded_weights(in_rows, inner, between)
    gain_norm, taps, seg_rows, head_row, skip_row, gain_row = started["small"]
    tails = gather_near(started["tail"], weights[1])

    projected = []
    for m in range(micro):
        tok_here = gather_near(started["tok"][m], weights[1], *[p[0] for p in projected[-1:]])
        projected.append(project(own_arg, tok_here, weights, tails, gain_norm))
    normed_all = [p[0] for p in projected]
    for m in range(1, micro):
        started["cot"].append(
            gather_far(after(cotangent[m, 0], started["tok"][m][parts // 2], normed_all[0]))
        )
    scans = []
    cot_all = []
    for m in range(micro):
        parts_here = gather_near(started["cot"][m], *(scans[m - 1][-1:] if m else normed_all[-1:]))
        cot, back = project_back(own_arg, parts_here, out_weight)
        _, gate, pre, tail, dt_raw = projected[m]
        outs = forward(
            own_arg, pre, tail, gate, dt_raw, back, seg_rows[m], taps, head_row, skip_row, gain_row
        )
        cot_all.append(cot)
        scans.append((gate, pre, tail, dt_raw, back) + tuple(outs))
    stats = [
        jnp.pad(summed(scan[-1][:, :2], "fsdp"), ((0, 0), (0, 6), (0, 0))) for scan in scans
    ]

    def scan_back(m, *earlier):
        _, pre, tail, dt_raw, _, act, slope, _, _, entering, _ = scans[m]
        return backward(
            own_arg,
            act,
            slope,
            pre,
            tail,
            dt_raw,
            after(grad_ssm[m], *earlier),
            entering,
            seg_rows[m],
            taps,
            head_row,
            skip_row,
        )

    def across(away):
        return swap(away, "group", 1)

    lines_count = groups // 2
    lane = lax.axis_index("group") & 1

    def joined(keep, got):
        return join(own_arg, keep, got).reshape(lines_count, -1, width)

    grad_ssm, grad_gates, gated, grad_inner, gate_out = gate_grads(
        own_arg,
        [(scan[7], scan[0], scan[4]) for scan in scans],
        stats,
        normed_all,
        gain_row,
        tok_count // chunk,
        lines_count,
    )
    half_gate = along.scatter(gate_out.reshape(groups, -1, width))
    gated = [after(g, gate_out) for g in gated]
    away_out = weight_grad(own_arg, gated, cot_all, inner, False)
    with jax.named_scope("away_out"):
        got_out = across(away_out)
    gated = [after(g, away_out) for g in gated]
    keep_out = weight_grad(own_arg, gated, cot_all, inner, True)
    backs = [scan_back(0, keep_out)]
    half_out = joined(keep_out, after(got_out, backs[0][0]))
    with jax.named_scope("trade_gate"):
        trade = Trade(own_arg, after(half_gate, half_out), parts)
    for m in range(1, micro):
        backs.append(scan_back(m, half_out, trade.sent))
    with jax.named_scope("trade_gate"):
        trade.middle(backs[-1][0])
        gate_cols = trade.final()
    left = [after(b[0], gate_cols) for b in backs]
    away_x = weight_grad(own_arg, left, normed_all, inner, False)
    with jax.named_scope("away_heads"):
        got_x = across(away_x)
    left = [after(b[0], away_x) for b in backs]
    keep_x = weight_grad(own_arg, left, normed_all, inner, True)
    half_out = along.scatter(half_out, lines())
    gate_lines = along.gather(after(gate_cols, away_x), lines())

    into = []
    for m in range(micro):
        grad_gate = after(grad_gates[m], keep_x, *(part[0] for part in into[-1:]))
        into.append(project_into(own_arg, grad_gate, *backs[m][:2], weights, tails))
    half_x = joined(keep_x, after(got_x, into[-1][0]))
    with jax.named_scope("gate_lines"):
        got_lines = across(after(gate_lines, half_x))
    rights = [after(n, half_x) for n in normed_all]
    tail_part = tail_grad(own_arg, [b[0] for b in backs], [b[1] for b in backs], rights, parts)

    def split(pair, name):
        with jax.named_scope(name):
            return Split(own_arg, [after(part, half_x) for part in pair])

    into = [split(pair, "into") for pair in into]
    tail_part = split(tail_part, "tail")
    with jax.named_scope("into"):
        for part in into:
            part.middle()
    with jax.named_scope("tail"):
        tail_part.middle()
    half_x = along.scatter(half_x, lines())
    with jax.named_scope("trade_heads"):
        trade = Trade(own_arg, half_x, parts)
    sent = trade.sent
    grad_tok = []
    grad_norm = jnp.zeros((width,), F32)
    for m in range(micro):
        terms = into[m].final(sent, got_lines)
        tok, gain = norm_rows(own_arg, tokens[m, 0], cotangent[m, 0], gain_norm, terms)
        grad_tok.append(tok)
        grad_norm += gain[0]
        if m == 0:
            with jax.named_scope("trade_heads"):
                sent = trade.middle(tok)
    with jax.named_scope("trade_heads"):
        x_cols = trade.final(tok)
    keep, got = tail_part.final()
    grad_tail = keep + got.astype(F32)

    grad_taps = sum(b[2] for b in backs)[: CONV + 1]
    grad_skip = sum(b[3] for b in backs)[0]
    grad_head = sum(b[4] for b in backs)
    taps_all = lax.dynamic_update_slice_in_dim(
        jnp.zeros((CONV + 1, XBC), F32), grad_taps[:, :inner], own * inner, 1
    )
    taps_all = taps_all.at[:, INNER:].set(grad_taps[:, inner:])
    with jax.named_scope("small"):
        joint = summed(jnp.concatenate([taps_all.reshape(-1), grad_norm]), "fsdp")
    skip_sum = jnp.sum(grad_skip.reshape(heads, HEADDIM), axis=1)
    joint = jnp.concatenate(
        [joint, grad_inner[0], grad_head[0, :heads], grad_head[1, :heads], skip_sum]
    )

    with jax.named_scope("small"):
        joint = summed(joint, "group")
    with jax.named_scope("tail"):
        grad_tail = summed(grad_tail, "group", BF16)
    mixed = []
    for m in range(micro):
        gained = after(scans[m][8], x_cols, *(part.even for part in mixed[-1:]))
        part = project_out(own_arg, gained, out_weight, parts)
        with jax.named_scope("mixed"):
            mixed.append(Split(own_arg, part))
    out_lines = along.gather(half_out, lines())
    with jax.named_scope("out_lines"):
        got_out = across(after(out_lines, joint, grad_tail))
    x_all = along.gather(after(x_cols, joint, grad_tail))
    with jax.named_scope("mixed"):
        for part in mixed:
            part.middle(mixed[-1].even)

    def all_lines(value):
        return value.reshape(lines_count, 2, parts, -1, rows)

    whole = fill_lines(own_arg, None, after(gate_lines, x_cols), True)
    whole = fill_lines(own_arg, whole, after(got_lines, x_cols), False)
    whole = fill_tail(own_arg, whole, grad_tail)
    grad_out = jnp.stack(
        [
            jnp.where(lane == 0, out_lines, got_out),
            jnp.where(lane == 0, got_out, out_lines),
        ]
    )
    grad_out = grad_out.reshape(inner, width).astype(F32)

    for m in range(micro):
        stat = lax.dynamic_slice_in_dim(
            stats[m][:, 0].reshape(seq), own * tok_count, tok_count, 0
        )
        scale = lax.rsqrt(stat * (1.0 / INNER) + EPSILON)[:, None]
        mixed[m] = mixed_rows(own_arg, tokens[m, 0], scale, mixed[m].final(whole))

    at = (CONV + 1) * XBC
    share = XBC // parts
    taps_all = lax.dynamic_slice_in_dim(joint[:at].reshape(CONV + 1, XBC), own * share, share, 1)
    grad_norm = lax.dynamic_slice_in_dim(joint, at + own * rows, rows, 0)
    at += width
    grad_inner = joint[at : at + inner]
    at += inner
    grad_bias, grad_rate, grad_skip = (
        joint[at + k * heads : at + (k + 1) * heads] for k in range(3)
    )
    mixed = jnp.stack(mixed)[:, None]
    grad_tok = jnp.stack(grad_tok)[:, None]
    x_all = after(x_all, whole, grad_out, grad_norm, mixed, grad_tok)
    grad_in = fill_heads(own_arg, whole, all_lines(x_all), INNER).T
    return (
        mixed,
        grad_tok,
        grad_norm,
        grad_in,
        taps_all[:CONV],
        taps_all[CONV],
        grad_bias,
        grad_rate,
        grad_skip,
        grad_inner,
        grad_out,
    )


def solution(mesh):
    rows = P(None, "group", "fsdp", None)
    shard = P("fsdp")
    in_specs = (rows, P(None, "group", "fsdp"), rows, shard, P("fsdp", None), P(None, "fsdp"))
    in_specs += (shard,) * 5 + (P("fsdp", None),)
    out_specs = (rows, rows, shard, P("fsdp", None), P(None, "fsdp")) + (shard,) * 5
    out_specs += (P("fsdp", None),)
    return jax.shard_map(
        on_device, mesh=mesh, in_specs=in_specs, out_specs=out_specs, check_vma=False
    )
```

```python
from functools import partial

import jax
import jax.numpy as jnp
from jax import lax
from jax.experimental import pallas as pl
from jax.experimental.pallas import tpu as pltpu
from jax.sharding import PartitionSpec as P

INNER = 4096
HEADS = 64
HEADDIM = 64
STATE = 128
CONV = 4
XBC = 4352
LANES = 128
EPSILON = 1e-05
FAR = -1e30
HIGHEST = lax.Precision.HIGHEST
VMEM = 48 * 1024 * 1024
F32 = jnp.float32
BF16 = jnp.bfloat16


def swap(value, axis, bit):
    count = lax.axis_size(axis)
    with jax.named_scope(f"{axis}_{bit}"):
        return lax.ppermute(value, axis, [(i, i ^ bit) for i in range(count)])


def after(value, *earlier):
    return lax.optimization_barrier((value,) + earlier)[0] if earlier else value


def bits_of(count):
    return [1 << k for k in reversed(range(count.bit_length() - 1))]


def gather_far(piece):
    held = {0: piece}
    for bit in bits_of(lax.axis_size("fsdp"))[:-1]:
        for r, part in list(held.items()):
            held[r ^ bit] = swap(part, "fsdp", bit)
    return held


def gather_near(held, *later):
    for r, part in list(held.items()):
        held[r ^ 1] = swap(after(part, *later), "fsdp", 1)
    return [held[r] for r in range(len(held))]


def gathered(piece):
    return gather_near(gather_far(piece))


def permuted(parts, own):
    stacked = jnp.stack(parts)
    return [
        lax.dynamic_index_in_dim(stacked, own ^ i, 0, keepdims=False) for i in range(len(parts))
    ]


def absolute(parts):
    return permuted(parts, lax.axis_index("fsdp"))


def traded(blocks, send):
    held = {r: {0: block} for r, block in enumerate(blocks)}
    for bit in bits_of(len(blocks)):
        going = [r for r in sorted(held) if r & bit]
        sources = sorted(held[going[0]])
        got = send(jnp.stack([held[r][s] for r in going for s in sources]), bit)
        place = 0
        for r in going:
            for s in sources:
                held[r ^ bit][s ^ bit] = got[place]
                place += 1
            del held[r]
    return [held[0][s] for s in sorted(held[0])]


def traded_weights(in_rows, inner, between):
    own = lax.axis_index("fsdp")
    side = lax.axis_index("group") & 3
    rows = in_rows.shape[1]
    half = inner // 2
    parts = lax.axis_size("fsdp")

    def block(r, kind, first, size):
        at = kind * INNER + (own ^ r) * inner + first
        return lax.dynamic_slice(in_rows, (at, jnp.zeros_like(at)), (size, rows))

    def piece(r, s):
        if s in held[r]:
            return held[r][s]
        return jnp.stack([block(r, kind, 0, inner) for kind in (0, 1)]).reshape(4, half, rows)

    def quarter(r, s):
        if s in held[r]:
            return held[r][s][0]
        return block(r, side // 2, (side & 1) * half, half)

    held = {r: {} for r in range(parts)}
    sources = [0]
    pins = None
    for bit in bits_of(parts):
        going = [r for r in sorted(held) if r & bit]
        order = [(r, s) for r in going for s in sources]
        if bit > 1:
            sent = jnp.stack([quarter(r, s) for r, s in order])
            mine = swap(sent, "fsdp", bit)
            if pins is None:
                pins = between(sent, mine)
            by_x = swap(mine, "group", 1)
            by_z = swap(mine, "group", 2)
            cut = half // 2
            rest = [
                swap(after(by_z[:, :cut], *pins[0]), "group", 1),
                swap(after(by_x[:, cut:], *pins[0]), "group", 2),
            ]
            got = jnp.stack([mine, by_x, by_z, jnp.concatenate(rest, axis=1)], axis=1)
        else:
            got = [swap(after(piece(r, s), *pins[1]), "fsdp", bit) for r, s in order]
        for (r, s), part in zip(order, got):
            held[r ^ bit][s ^ bit] = part
        for r in going:
            del held[r]
        sources += [s ^ bit for s in sources]
    return [piece(0, s) for s in range(parts)]


def scattered(value):
    bit = 1
    while value.shape[0] > 1:
        pairs = value.reshape((value.shape[0] // 2, 2) + value.shape[1:])
        got = swap(pairs[:, 1].astype(BF16), "fsdp", bit)
        value = pairs[:, 0].astype(F32) + got.astype(F32)
        bit *= 2
    return value[0]


def summed(value, axis, kind=F32, far_first=False, steps=None):
    bits = bits_of(lax.axis_size(axis))
    for bit in bits if far_first else bits[::-1]:
        value = value + swap(value.astype(kind), axis, bit).astype(F32)
        if steps is not None:
            steps.append(value)
    return value


def lines():
    count = lax.axis_size("group")
    return [list(range(side, count, 2)) for side in (0, 1)]


class Lines:
    def __init__(self):
        self.last = None

    def order(self, value):
        return value if self.last is None else after(value, self.last)

    def scatter(self, value, among=None):
        self.last = lax.psum_scatter(
            self.order(value), "group", scatter_dimension=0, axis_index_groups=among
        )
        return self.last

    def gather(self, value, among=None):
        self.last = lax.all_gather(
            self.order(value), "group", axis=0, axis_index_groups=among
        )
        return self.last


def dot(a, b, contract=((1,), (0,)), precision=None):
    return lax.dot_general(a, b, (contract, ((), ())), precision=precision, preferred_element_type=F32)


def steps(dt_ref, head_ref, tri):
    raw = dt_ref[...] + head_ref[0:1, :]
    size = jnp.maximum(raw, 0.0) + jnp.log1p(jnp.exp(-jnp.abs(raw)))
    log_decay = size * head_ref[1:2, :]
    running = dot(tri, log_decay, precision=HIGHEST)
    return raw, size, log_decay, running


def columns(row, chunk):
    return jnp.broadcast_to(row, (LANES, chunk)).T


def squared(array, chunk):
    return array if chunk == LANES else array[:, :chunk]


def forward_kernel(
    chunk,
    own_ref,
    pre_ref,
    tail_ref,
    gate_ref,
    dt_ref,
    back_ref,
    row_ref,
    taps_ref,
    head_ref,
    skip_ref,
    gain_ref,
    act_ref,
    slope_ref,
    out_ref,
    gained_ref,
    enter_ref,
    stat_ref,
    state,
    window,
    carried,
    flown,
):
    where = pl.program_id(0)
    inner = gate_ref.shape[1]
    channels = act_ref.shape[1]

    @pl.when(where == 0)
    def _():
        state[...] = jnp.zeros_like(state)
        window[0:8, :] = jnp.zeros((8, channels), F32)

    start = (where * chunk).astype(F32)
    seg_row = row_ref[0:1, :]
    seg_col = columns(seg_row, chunk)
    time = lax.broadcasted_iota(jnp.int32, (chunk, LANES), 0).astype(F32) + start
    seen = [(seg_col <= time - back).astype(F32) for back in range(1, CONV)]
    window[8:, :inner] = pre_ref[...].astype(F32)
    window[8:, inner:] = tail_ref[...].astype(F32)
    for at in range(0, channels, LANES):
        lanes = slice(at, at + LANES)
        total = taps_ref[4:5, lanes] + taps_ref[3:4, lanes] * window[8 : 8 + chunk, lanes]
        for back in range(1, CONV):
            total += taps_ref[3 - back : 4 - back, lanes] * (
                window[8 - back : 8 - back + chunk, lanes] * seen[back - 1]
            )
        sig = jax.nn.sigmoid(total)
        act_ref[:, lanes] = (total * sig).astype(BF16)
        slope_ref[:, lanes] = (sig * (1.0 + total * (1.0 - sig))).astype(BF16)
    window[0:8, :] = window[chunk : chunk + 8, :]

    seg_last = seg_row[:, chunk - 1 : chunk]
    down = lax.broadcasted_iota(jnp.int32, (chunk, chunk), 0)
    across = lax.broadcasted_iota(jnp.int32, (chunk, chunk), 1)
    tri = (across <= down).astype(F32)
    _, size, _, running = steps(dt_ref, head_ref, tri)
    running_t = running.T
    size_t = size.T
    b_input = act_ref[:, inner : inner + STATE]
    c_output = act_ref[:, inner + STATE :]
    gram = dot(c_output, b_input, ((1,), (1,)))
    veil = jnp.where((squared(seg_col, chunk) == seg_row) & (across <= down), 0.0, FAR)
    crossing = (seg_col < start).astype(F32)
    ending = (seg_col == seg_last).astype(F32)
    passing = (seg_last < start).astype(F32)
    last = running[chunk - 1 : chunk, :]
    low = lax.broadcasted_iota(jnp.int32, (chunk, LANES), 1) < HEADDIM
    low_row = low[0:1, :]
    entering = state[...].astype(BF16)
    enter_ref[...] = entering
    carried[...] = dot(c_output, entering)
    squares = jnp.zeros((chunk, LANES), F32)
    products = jnp.zeros((chunk, LANES), F32)
    for pair in range(inner // LANES):
        lanes = slice(pair * LANES, (pair + 1) * LANES)
        heads = (2 * pair, 2 * pair + 1)
        x_pair = act_ref[:, lanes].astype(F32)
        run = [running[:, h : h + 1] for h in heads]
        mixing = [
            (jnp.exp(run[k] - running_t[h : h + 1, :] + veil) * gram * size_t[h : h + 1, :]).astype(
                BF16
            )
            for k, h in enumerate(heads)
        ]
        halves = [jnp.where(low, x_pair, 0.0).astype(BF16), jnp.where(low, 0.0, x_pair).astype(BF16)]
        inside = dot(jnp.concatenate(mixing, axis=1), jnp.concatenate(halves, axis=0))
        run_pair = jnp.where(low, run[0], run[1])
        size_pair = jnp.where(low, size[:, heads[0] : heads[0] + 1], size[:, heads[1] : heads[1] + 1])
        last_pair = jnp.where(
            low_row, last[:, heads[0] : heads[0] + 1], last[:, heads[1] : heads[1] + 1]
        )
        ssm = (
            inside
            + carried[:, lanes] * (jnp.exp(run_pair) * crossing)
            + skip_ref[:, lanes] * x_pair
        )
        outflow = jnp.exp(last_pair - run_pair) * ending * size_pair
        flown[:, lanes] = (x_pair * outflow).astype(BF16)
        state[:, lanes] = (jnp.exp(last_pair) * passing) * state[:, lanes]
        gate = gate_ref[:, lanes].astype(F32)
        gated = ssm * (gate * jax.nn.sigmoid(gate))
        out_ref[:, lanes] = ssm.astype(BF16)
        gained = gated * gain_ref[:, lanes]
        gained_ref[:, lanes] = gained.astype(BF16)
        squares += gated * gated
        products += gained * back_ref[:, lanes].astype(F32)
    state[...] += dot(b_input, flown[...], ((0,), (0,)))
    stat_ref[0:1, :] = jnp.sum(squares.T, axis=0, keepdims=True)
    stat_ref[1:2, :] = jnp.sum(products.T, axis=0, keepdims=True)
    stat_ref[2:8, :] = jnp.zeros((6, chunk), F32)


def backward_kernel(
    chunk,
    own_ref,
    act_ref,
    slope_ref,
    pre_ref,
    tail_ref,
    dt_ref,
    grad_ref,
    enter_ref,
    row_ref,
    taps_ref,
    head_ref,
    skip_ref,
    grad_pre_ref,
    grad_dt_ref,
    grad_taps_ref,
    grad_skip_ref,
    grad_head_ref,
    leaving,
    window,
    grad_act,
    row_sums,
    carried,
    fresh,
    into,
    flown,
):
    count = pl.num_programs(0)
    where = count - 1 - pl.program_id(0)
    inner = grad_ref.shape[1]
    channels = act_ref.shape[1]

    @pl.when(pl.program_id(0) == 0)
    def _():
        leaving[...] = jnp.zeros_like(leaving)
        window[chunk:, :] = jnp.zeros((8, channels), F32)
        grad_taps_ref[...] = jnp.zeros_like(grad_taps_ref)
        grad_skip_ref[...] = jnp.zeros_like(grad_skip_ref)
        grad_head_ref[...] = jnp.zeros_like(grad_head_ref)
        row_sums[...] = jnp.zeros_like(row_sums)

    start = (where * chunk).astype(F32)
    seg_row = row_ref[0:1, :]
    seg_col = columns(seg_row, chunk)
    seg_last = seg_row[:, chunk - 1 : chunk]
    down = lax.broadcasted_iota(jnp.int32, (chunk, chunk), 0)
    across = lax.broadcasted_iota(jnp.int32, (chunk, chunk), 1)
    tri = (across <= down).astype(F32)
    raw, size, log_decay, running = steps(dt_ref, head_ref, tri)
    running_t = running.T
    b_input = act_ref[:, inner : inner + STATE]
    c_output = act_ref[:, inner + STATE :]
    gram = dot(b_input, c_output, ((1,), (1,)))
    veil = jnp.where((squared(seg_col, chunk) == seg_row) & (down <= across), 0.0, FAR)
    crossing = (seg_col < start).astype(F32)
    ending = (seg_col == seg_last).astype(F32)
    passing = (seg_last < start).astype(F32)
    last = running[chunk - 1 : chunk, :]
    lane = lax.broadcasted_iota(jnp.int32, (chunk, LANES), 1)
    low = lane < HEADDIM
    low_row = low[0:1, :]
    lane_row = lane[0:1, :]
    left_low = leaving[...].astype(BF16)
    entering = enter_ref[...]
    carried[...] = dot(c_output, entering)
    fresh[...] = dot(b_input, left_low)
    grad_gram = jnp.zeros((chunk, chunk), F32)
    size_grad = jnp.zeros((chunk, LANES), F32)
    carry_grad = jnp.zeros((chunk, LANES), F32)
    total_grad = jnp.zeros((1, LANES), F32)
    for pair in range(inner // LANES):
        lanes = slice(pair * LANES, (pair + 1) * LANES)
        heads = (2 * pair, 2 * pair + 1)
        x_low = act_ref[:, lanes]
        x_pair = x_low.astype(F32)
        grad = grad_ref[:, lanes].astype(F32)
        halves = (low, jnp.logical_not(low))
        run = [running[:, h : h + 1] for h in heads]
        sizes = [size[:, h : h + 1] for h in heads]
        run_pair = jnp.where(low, run[0], run[1])
        size_pair = jnp.where(low, sizes[0], sizes[1])
        last_pair = jnp.where(
            low_row, last[:, heads[0] : heads[0] + 1], last[:, heads[1] : heads[1] + 1]
        )
        left = leaving[:, lanes]
        inflow = jnp.exp(run_pair) * crossing
        outflow = jnp.exp(last_pair - run_pair) * ending
        into_here = grad * inflow
        into[:, lanes] = into_here.astype(BF16)
        carry_here = into_here * carried[:, lanes]
        fresh_back = fresh[:, lanes] * outflow
        flown_here = x_pair * fresh_back
        flown[:, lanes] = (x_pair * outflow * size_pair).astype(BF16)
        whole = jnp.exp(last_pair) * passing
        kept = whole * jnp.sum(left * enter_ref[:, lanes].astype(F32), axis=0, keepdims=True)
        kept += jnp.sum(flown_here * size_pair, axis=0, keepdims=True)
        leaving[:, lanes] = whole * left
        both = jnp.concatenate(
            [jnp.where(low, grad, 0.0).astype(BF16), jnp.where(low, 0.0, grad).astype(BF16)], axis=0
        )
        back_both = dot(x_low, both, ((1,), (1,)))
        weights = []
        for k, h in enumerate(heads):
            mine = halves[k]
            decay = jnp.exp(running_t[h : h + 1, :] - run[k] + veil)
            weight = decay * gram
            weights.append((weight * sizes[k]).astype(BF16))
            back = back_both[:, k * chunk : (k + 1) * chunk]
            grad_gram += back * decay * sizes[k]
            straight = back * weight
            row_sums[h : h + 1, :] = jnp.sum(straight * sizes[k], axis=0, keepdims=True)
            flown_mine = jnp.where(mine, flown_here, 0.0)
            if chunk == LANES:
                size_here = jnp.sum(straight + flown_mine, axis=1, keepdims=True)
            else:
                size_here = jnp.sum(straight, axis=1, keepdims=True) + jnp.sum(
                    flown_mine, axis=1, keepdims=True
                )
            carry_mine = jnp.sum(jnp.where(mine, carry_here, 0.0), axis=1, keepdims=True)
            here = lane == h
            size_grad = jnp.where(here, size_here, size_grad)
            carry_grad = jnp.where(here, carry_mine, carry_grad)
            total_here = jnp.sum(jnp.where(mine[0:1, :], kept, 0.0), axis=1, keepdims=True)
            total_grad = jnp.where(lane_row == h, total_here, total_grad)
        grad_act[:, lanes] = (
            dot(jnp.concatenate(weights, axis=1), both)
            + fresh_back * size_pair
            + skip_ref[:, lanes] * grad
        )
        grad_skip_ref[0:1, lanes] += jnp.sum(grad * x_pair, axis=0, keepdims=True)
    grad_gram_low = grad_gram.astype(BF16)
    grad_act[:, inner : inner + STATE] = dot(grad_gram_low, c_output) + dot(
        flown[...], left_low, ((1,), (1,))
    )
    grad_act[:, inner + STATE :] = dot(grad_gram_low, b_input, ((0,), (0,))) + dot(
        into[...], entering, ((1,), (1,))
    )
    leaving[...] += dot(c_output, into[...], ((0,), (0,)))
    row_t = row_sums[...].T
    grad_run = row_t + carry_grad - size * size_grad
    upper = (across >= down).astype(F32)
    grad_decay = dot(upper, grad_run, precision=HIGHEST) + total_grad
    grad_size = grad_decay * head_ref[1:2, :] + size_grad
    grad_raw = jnp.where(lane < inner // HEADDIM, grad_size * jax.nn.sigmoid(raw), 0.0)
    grad_dt_ref[...] = grad_raw.astype(BF16)
    grad_head_ref[0:1, :] += jnp.sum(grad_raw, axis=0, keepdims=True)
    grad_head_ref[1:2, :] += jnp.sum(grad_decay * log_decay, axis=0, keepdims=True)

    same = [
        (columns(row_ref[ahead : ahead + 1, :], chunk) == seg_col).astype(F32)
        for ahead in range(1, CONV)
    ]
    for at in range(0, channels, LANES):
        lanes = slice(at, at + LANES)
        grad_sum = grad_act[:, lanes] * slope_ref[:, lanes].astype(F32)
        window[0:chunk, lanes] = grad_sum
        if at < inner:
            pre = pre_ref[:, lanes].astype(F32)
        else:
            pre = tail_ref[:, at - inner : at - inner + LANES].astype(F32)
        grad_pre = taps_ref[3:4, lanes] * grad_sum
        grad_taps_ref[3:4, lanes] += jnp.sum(pre * grad_sum, axis=0, keepdims=True)
        grad_taps_ref[4:5, lanes] += jnp.sum(grad_sum, axis=0, keepdims=True)
        for ahead in range(1, CONV):
            later = window[ahead : ahead + chunk, lanes] * same[ahead - 1]
            grad_pre += taps_ref[3 - ahead : 4 - ahead, lanes] * later
            grad_taps_ref[3 - ahead : 4 - ahead, lanes] += jnp.sum(
                pre * later, axis=0, keepdims=True
            )
        grad_pre_ref[:, lanes] = grad_pre.astype(BF16)
    window[chunk:, :] = window[0:8, :]


def scan_calls(parts, tok_count, inner):
    chunk = min(LANES, tok_count)
    per_part = tok_count // chunk
    count = parts * per_part
    channels = inner + 2 * STATE
    tokens = parts * tok_count

    def blocks(flip):
        def time(step):
            return count - 1 - step if flip else step

        def place(step, own):
            t = time(step)
            return lax.bitwise_xor(t // per_part, own[0]) * per_part + t % per_part

        def tok(width):
            return pl.BlockSpec((chunk, width), lambda step, own: (place(step, own), 0))

        row = pl.BlockSpec((None, 8, chunk), lambda step, own: (time(step), 0, 0))
        states = pl.BlockSpec((None, STATE, inner), lambda step, own: (time(step), 0, 0))

        def const(rows, width):
            return pl.BlockSpec((rows, width), lambda step, own: (0, 0))

        return tok, row, states, const

    def scan(kernel, ins, outs, shapes, scratch):
        return pl.pallas_call(
            partial(kernel, chunk),
            grid_spec=pltpu.PrefetchScalarGridSpec(
                num_scalar_prefetch=1,
                grid=(count,),
                in_specs=ins,
                out_specs=outs,
                scratch_shapes=scratch,
            ),
            out_shape=shapes,
            compiler_params=pltpu.CompilerParams(
                dimension_semantics=("arbitrary",), vmem_limit_bytes=VMEM
            ),
            cost_estimate=COST,
        )

    struct = jax.ShapeDtypeStruct
    tok, row, states, const = blocks(False)
    forward = scan(
        forward_kernel,
        [tok(inner), tok(2 * STATE), tok(inner), tok(LANES), tok(inner), row]
        + [const(8, channels), const(8, LANES), const(1, inner), const(1, inner)],
        [tok(channels), tok(channels), tok(inner), tok(inner), states, row],
        [
            struct((tokens, channels), BF16),
            struct((tokens, channels), BF16),
            struct((tokens, inner), BF16),
            struct((tokens, inner), BF16),
            struct((count, STATE, inner), BF16),
            struct((count, 8, chunk), F32),
        ],
        [
            pltpu.VMEM((STATE, inner), F32),
            pltpu.VMEM((chunk + 8, channels), F32),
            pltpu.VMEM((chunk, inner), F32),
            pltpu.VMEM((chunk, inner), BF16),
        ],
    )
    tok, row, states, const = blocks(True)
    backward = scan(
        backward_kernel,
        [tok(channels), tok(channels), tok(inner), tok(2 * STATE), tok(LANES)]
        + [tok(inner), states, row]
        + [const(8, channels), const(8, LANES), const(1, inner)],
        [tok(channels), tok(LANES), const(8, channels), const(8, inner), const(8, LANES)],
        [
            struct((tokens, channels), BF16),
            struct((tokens, LANES), BF16),
            struct((8, channels), F32),
            struct((8, inner), F32),
            struct((8, LANES), F32),
        ],
        [
            pltpu.VMEM((STATE, inner), F32),
            pltpu.VMEM((chunk + 8, channels), F32),
            pltpu.VMEM((chunk, channels), F32),
            pltpu.VMEM((LANES, chunk), F32),
            pltpu.VMEM((chunk, inner), F32),
            pltpu.VMEM((chunk, inner), F32),
            pltpu.VMEM((chunk, inner), BF16),
            pltpu.VMEM((chunk, inner), BF16),
        ],
    )
    return forward, backward


NN = ((1,), (0,))
NT = ((1,), (1,))
TN = ((0,), (0,))
COST = pl.CostEstimate(flops=1, bytes_accessed=1, transcendentals=0)


def call(kernel, grid, ins, outs, shapes, args, scratch=()):
    return pl.pallas_call(
        kernel,
        grid_spec=pltpu.PrefetchScalarGridSpec(
            num_scalar_prefetch=1,
            grid=grid,
            in_specs=ins,
            out_specs=outs,
            scratch_shapes=scratch,
        ),
        out_shape=shapes,
        compiler_params=pltpu.CompilerParams(
            dimension_semantics=("arbitrary",) * len(grid), vmem_limit_bytes=VMEM
        ),
        cost_estimate=COST,
    )(*args)


def fixed(shape):
    return pl.BlockSpec(shape, lambda i, own: (0,) * len(shape))


def own_heads(own, heads):
    head = lax.broadcasted_iota(jnp.int32, (HEADS, LANES), 0)
    lane = lax.broadcasted_iota(jnp.int32, (HEADS, LANES), 1)
    return ((head == own * heads + lane) & (lane < heads)).astype(F32)


def project_kernel(parts, own_ref, *refs):
    tok_refs, weights, tails = refs[:parts], refs[parts : 2 * parts], refs[2 * parts : 3 * parts]
    gain_ref, normed_ref, gate_ref, pre_ref, tail_ref, dt_ref, ordered = refs[3 * parts :]
    at = pl.program_id(0)
    rows = tails[0].shape[1]
    tok_count = tok_refs[0].shape[0]

    @pl.when(at == 0)
    def _():
        for r in range(parts):
            values = tok_refs[r][...].astype(F32)
            mean = jnp.mean(values * values, axis=-1, keepdims=True)
            normed_ref[r * tok_count : (r + 1) * tok_count, :] = (
                values * lax.rsqrt(mean + EPSILON) * gain_ref[...]
            ).astype(BF16)
        for s in range(parts):
            lanes = pl.ds(pl.multiple_of(lax.bitwise_xor(own_ref[0], s) * rows, LANES), rows)
            ordered[:, s * rows : (s + 1) * rows] = normed_ref[:, lanes]

    def total(refs):
        return dot(ordered[...], jnp.concatenate([ref[...] for ref in refs], axis=1), NT)

    @pl.when(at < 2)
    def _():
        gate_ref[...] = total(weights).astype(BF16)

    @pl.when((at >= 2) & (at < 4))
    def _():
        pre_ref[...] = total(weights).astype(BF16)

    @pl.when(at == 4)
    def _():
        rest = total(tails)
        tail_ref[...] = rest[:, : 2 * STATE].astype(BF16)
        pick = own_heads(own_ref[0], HEADS // parts)
        dt_ref[...] = dot(rest[:, 2 * STATE :], pick, precision=HIGHEST)


def project(own_arg, tok_parts, weights, tails, gain):
    parts, (tok_count, width) = len(tok_parts), tok_parts[0].shape
    half, rows = weights[0].shape[1:]
    tokens = parts * tok_count

    def near(i, own):
        return (jnp.minimum(i, 3), 0, 0)

    def far(i, own):
        return (lax.bitwise_xor(jnp.minimum(i, 3), own[1]), 0, 0)

    struct = jax.ShapeDtypeStruct
    return call(
        partial(project_kernel, parts),
        (5,),
        [fixed((tok_count, width))] * parts
        + [pl.BlockSpec((None, half, rows), far if s > 1 else near) for s in range(parts)]
        + [fixed(tails[0].shape)] * parts
        + [fixed((1, width))],
        [
            fixed((tokens, width)),
            pl.BlockSpec((tokens, half), lambda i, own: (0, jnp.minimum(i, 1))),
            pl.BlockSpec((tokens, half), lambda i, own: (0, jnp.clip(i - 2, 0, 1))),
            fixed((tokens, 2 * STATE)),
            fixed((tokens, LANES)),
        ],
        [
            struct((tokens, width), BF16),
            struct((tokens, 2 * half), BF16),
            struct((tokens, 2 * half), BF16),
            struct((tokens, 2 * STATE), BF16),
            struct((tokens, LANES), F32),
        ],
        (own_arg, *tok_parts, *weights, *tails, gain[None]),
        [pltpu.VMEM((tokens, width), BF16)],
    )


def back_kernel(parts, own_ref, *refs):
    weight_ref, all_ref, back_ref = refs[parts:]
    tok_count = refs[0].shape[0]

    @pl.when(pl.program_id(0) == 0)
    def _():
        for r in range(parts):
            all_ref[r * tok_count : (r + 1) * tok_count, :] = refs[r][...]

    back_ref[...] = dot(all_ref[...], weight_ref[...], NT).astype(BF16)


def project_back(own_arg, cot_parts, weight):
    parts, (tok_count, width) = len(cot_parts), cot_parts[0].shape
    inner = weight.shape[0]
    block = min(256, inner)
    tokens = parts * tok_count
    struct = jax.ShapeDtypeStruct
    return call(
        partial(back_kernel, parts),
        (inner // block,),
        [fixed((tok_count, width))] * parts
        + [pl.BlockSpec((block, width), lambda i, own: (i, 0))],
        [fixed((tokens, width)), pl.BlockSpec((tokens, block), lambda i, own: (0, i))],
        [struct((tokens, width), BF16), struct((tokens, inner), BF16)],
        (own_arg, *cot_parts, weight),
    )


def split_rows(value, even_ref, odd_ref):
    size = even_ref.shape[0]
    even_ref[...] = value[:size].astype(BF16)
    odd_ref[...] = value[size:].astype(BF16)


def split_outs(tok_count, parts, width):
    spec = pl.BlockSpec((None, tok_count, width), lambda i, own: (i, 0, 0))
    shape = jax.ShapeDtypeStruct((parts // 2, tok_count, width), BF16)
    return [spec, spec], [shape, shape]


def out_kernel(own_ref, a_ref, b_ref, even_ref, odd_ref):
    split_rows(dot(a_ref[...], b_ref[...]), even_ref, odd_ref)


def project_out(own_arg, gained, weight, parts):
    (tokens, inner), width = gained.shape, weight.shape[1]
    tok_count = tokens // parts
    specs, shapes = split_outs(tok_count, parts, width)
    return call(
        out_kernel,
        (parts // 2,),
        [pl.BlockSpec((2 * tok_count, inner), lambda i, own: (i, 0)), fixed((inner, width))],
        specs,
        shapes,
        (own_arg, gained, weight),
    )


def into_kernel(parts, own_ref, gate_ref, pre_ref, dt_ref, *refs):
    weights, tails = refs[:parts], refs[parts : 2 * parts]
    even_ref, odd_ref = refs[2 * parts :]
    half, rows = weights[0].shape[1:]
    pick = own_heads(own_ref[0], HEADS // parts).astype(BF16)
    grad_dt = dot(dt_ref[...], pick, NT).astype(BF16)
    left = jnp.concatenate([gate_ref[...], pre_ref[...], grad_dt], axis=1)
    for s in range(parts):
        order = [lax.bitwise_xor(q, own_ref[1]) if s > 1 else q for q in range(4)]
        right = jnp.concatenate([weights[s][q] for q in order] + [tails[s][...]], axis=0)
        lanes = pl.ds(pl.multiple_of(lax.bitwise_xor(own_ref[0], s) * rows, LANES), rows)
        split_rows(dot(left, right), even_ref.at[:, lanes], odd_ref.at[:, lanes])


def project_into(own_arg, grad_gate, grad_pre, grad_dt, weights, tails):
    parts = len(weights)
    (tokens, inner), channels = grad_gate.shape, grad_pre.shape[1]
    width = parts * weights[0].shape[2]
    tok_count = tokens // parts

    def tok(size):
        return pl.BlockSpec((2 * tok_count, size), lambda i, own: (i, 0))

    specs, shapes = split_outs(tok_count, parts, width)
    return call(
        partial(into_kernel, parts),
        (parts // 2,),
        [tok(inner), tok(channels), tok(LANES)]
        + [fixed(w.shape) for w in weights]
        + [fixed(r.shape) for r in tails],
        specs,
        shapes,
        (own_arg, grad_gate, grad_pre, grad_dt, *weights, *tails),
    )


def tail_kernel(count, parts, own_ref, *refs):
    pres, dts, normed = refs[:count], refs[count : 2 * count], refs[2 * count : 3 * count]
    even_ref, odd_ref = refs[3 * count :]
    pick = own_heads(own_ref[0], HEADS // parts)

    def total(lefts):
        terms = [dot(a[...], b[...], TN) for a, b in zip(lefts, normed)]
        return sum(terms[1:], terms[0])

    value = [total(pres), dot(pick.astype(BF16), total(dts).astype(BF16))]
    value = jnp.concatenate(value, axis=0).astype(BF16)

    @pl.when(pl.program_id(0) % 2 == 0)
    def _():
        even_ref[...] = value

    @pl.when(pl.program_id(0) % 2 == 1)
    def _():
        odd_ref[...] = value


def tail_grad(own_arg, grad_pres, grad_dts, normed, parts):
    (tokens, channels), width = grad_pres[0].shape, normed[0].shape[1]
    count, columns, rows = len(normed), 2 * STATE + HEADS, width // parts
    spec = pl.BlockSpec((None, columns, rows), lambda r, own: (r // 2, 0, 0))
    shape = jax.ShapeDtypeStruct((parts // 2, columns, rows), BF16)
    return call(
        partial(tail_kernel, count, parts),
        (parts,),
        [pl.BlockSpec((tokens, 2 * STATE), lambda r, own: (0, channels // (2 * STATE) - 1))] * count
        + [fixed((tokens, LANES))] * count
        + [pl.BlockSpec((tokens, rows), lambda r, own: (0, lax.bitwise_xor(own[0], r)))] * count,
        [spec, spec],
        [shape, shape],
        (own_arg, *grad_pres, *grad_dts, *normed),
    )


def add_kernel(own_ref, a_ref, b_ref, keep_ref, send_ref):
    keep_ref[...] = a_ref[0].astype(F32) + b_ref[0].astype(F32)
    send_ref[...] = (a_ref[1].astype(F32) + b_ref[1].astype(F32)).astype(BF16)


def add_parts(own_arg, even, got):
    _, size, width = even.shape
    block = size // 2
    both = pl.BlockSpec((2, block, width), lambda i, own: (0, i, 0))
    one = pl.BlockSpec((block, width), lambda i, own: (i, 0))
    struct = jax.ShapeDtypeStruct
    return call(
        add_kernel,
        (2,),
        [both, both],
        [one, one],
        [struct((size, width), F32), struct((size, width), BF16)],
        (own_arg, even, got),
    )


class Split:
    def __init__(self, own_arg, parts):
        self.own_arg = own_arg
        self.even, self.odd = parts
        self.plain = self.even.shape[0] != 2
        self.sent = self.even
        if not self.plain:
            self.got = swap(self.odd, "fsdp", 1)

    def middle(self, *earlier):
        if not self.plain:
            got = after(self.got, *earlier)
            self.keep, self.sent = add_parts(self.own_arg, self.even, got)
            self.got = swap(self.sent, "fsdp", 2)
        return self.sent

    def final(self, *earlier):
        if not self.plain:
            return self.keep, after(self.got, *earlier)
        every = jnp.stack([self.even, self.odd], axis=1)
        every = every.reshape((-1,) + self.even.shape[1:])
        total = scattered(after(every, *earlier))
        return total, jnp.zeros(total.shape, BF16)


def mixed_kernel(own_ref, tok_ref, scale_ref, keep_ref, got_ref, out_ref):
    total = keep_ref[...] + got_ref[...].astype(F32)
    out_ref[...] = (tok_ref[...].astype(F32) + total * scale_ref[...]).astype(BF16)


def mixed_rows(own_arg, tok, scale, terms):
    size, width = tok.shape
    block = min(128, size)
    one = pl.BlockSpec((block, width), lambda i, own: (i, 0))
    return call(
        mixed_kernel,
        (size // block,),
        [one, pl.BlockSpec((block, 1), lambda i, own: (i, 0)), one, one],
        [one],
        [jax.ShapeDtypeStruct((size, width), BF16)],
        (own_arg, tok, scale, *terms),
    )[0]


def norm_kernel(own_ref, tok_ref, cot_ref, gain_ref, keep_ref, got_ref, out_ref, sum_ref):
    @pl.when(pl.program_id(0) == 0)
    def _():
        sum_ref[...] = jnp.zeros_like(sum_ref)

    tok = tok_ref[...].astype(F32)
    inverse = lax.rsqrt(jnp.mean(tok * tok, axis=-1, keepdims=True) + EPSILON)
    hat = tok * inverse
    part = keep_ref[...] + got_ref[...].astype(F32)
    through = part * gain_ref[...]
    here = inverse * (through - hat * jnp.mean(hat * through, axis=-1, keepdims=True))
    out_ref[...] = (cot_ref[...].astype(F32) + here).astype(BF16)
    sum_ref[0:1, :] += jnp.sum(part * hat, axis=0, keepdims=True)


def norm_rows(own_arg, tok, cot, gain, terms):
    size, width = tok.shape
    block = min(128, size)
    one = pl.BlockSpec((block, width), lambda i, own: (i, 0))
    return call(
        norm_kernel,
        (size // block,),
        [one, one, fixed((1, width)), one, one],
        [one, fixed((8, width))],
        [jax.ShapeDtypeStruct((size, width), BF16), jax.ShapeDtypeStruct((8, width), F32)],
        (own_arg, tok, cot, gain[None], *terms),
    )


def join_kernel(own_ref, a_ref, b_ref, out_ref):
    out_ref[...] = (a_ref[...].astype(F32) + b_ref[...].astype(F32)).astype(BF16)


def join(own_arg, keep, got):
    size, width = keep.shape
    one = pl.BlockSpec((size // 4, width), lambda i, own: (i, 0))
    return call(
        join_kernel,
        (4,),
        [one, one],
        [one],
        [jax.ShapeDtypeStruct((size, width), BF16)],
        (own_arg, keep, got),
    )[0]


def pick_kernel(order, own_ref, *refs):
    out_ref = refs[-1]
    rows = out_ref.shape[-1]
    for i, (ref, block, lane) in enumerate(order):
        if lane:
            lanes = pl.ds(pl.multiple_of(lax.bitwise_xor(own_ref[0], block) * rows, LANES), rows)
            out_ref[i] = refs[ref][:, lanes]
        else:
            out_ref[i] = refs[ref][block]


def picked(own_arg, order, args, rows):
    shape = (len(order), args[0].shape[0], rows)
    return call(
        partial(pick_kernel, order),
        (1,),
        [fixed(arg.shape) for arg in args],
        [fixed(shape)],
        [jax.ShapeDtypeStruct(shape, BF16)],
        (own_arg, *args),
    )[0]


def place_kernel(own_ref, half_ref, far_ref, near_ref, out_ref):
    rows = out_ref.shape[-1]
    own = own_ref[0]
    lanes = pl.ds(pl.multiple_of(own * rows, LANES), rows)
    out_ref[own] = half_ref[:, lanes]
    out_ref[lax.bitwise_xor(own, 2)] = far_ref[0]
    out_ref[lax.bitwise_xor(own, 1)] = near_ref[0]
    out_ref[lax.bitwise_xor(own, 3)] = near_ref[1]


class Trade:
    def __init__(self, own_arg, half, parts):
        self.own_arg, self.half, self.parts = own_arg, half, parts
        self.rows = half.shape[1] // parts
        self.sent = half
        self.plain = parts != 4
        if not self.plain:
            self.sent = picked(own_arg, [(0, 2, True), (0, 3, True)], [half], self.rows)
            self.far = swap(self.sent, "fsdp", 2)

    def middle(self, *earlier):
        if not self.plain:
            self.far = after(self.far, *earlier)
            order = [(0, 1, True), (1, 1, False)]
            self.sent = picked(self.own_arg, order, [self.half, self.far], self.rows)
            self.near = swap(self.sent, "fsdp", 1)
        return self.sent

    def final(self, *earlier):
        if self.plain:
            own = lax.axis_index("fsdp")
            here = [
                lax.dynamic_slice_in_dim(self.half, (own ^ r) * self.rows, self.rows, 1)
                for r in range(self.parts)
            ]
            here = traded(here, lambda value, bit: swap(value, "fsdp", bit))
            return jnp.stack(absolute(here))
        near = after(self.near, *earlier)
        shape = (self.parts, self.half.shape[0], self.rows)
        return call(
            place_kernel,
            (1,),
            [fixed(self.half.shape), fixed(self.far.shape), fixed(near.shape)],
            [fixed(shape)],
            [jax.ShapeDtypeStruct(shape, BF16)],
            (self.own_arg, self.half, self.far, near),
        )[0]


def weight_kernel(count, own_ref, *refs):
    out_ref = refs[-1]
    total = dot(refs[0][...], refs[count][...], TN)
    for m in range(1, count):
        total += dot(refs[m][...], refs[count + m][...], TN)
    out_ref[...] = total.astype(out_ref.dtype)


def half_of(own, kept):
    return lax.bitwise_xor(own[1] & 1, 0 if kept else 1)


def weight_grad(own_arg, lefts, rights, inner, kept):
    tokens, width = rights[0].shape
    half, block = inner // 2, 512
    return call(
        partial(weight_kernel, len(lefts)),
        (width // block,),
        [pl.BlockSpec((tokens, half), lambda i, own: (0, half_of(own, kept)))] * len(lefts)
        + [pl.BlockSpec((tokens, block), lambda i, own: (0, i))] * len(rights),
        [pl.BlockSpec((half, block), lambda i, own: (0, i))],
        [jax.ShapeDtypeStruct((half, width), BF16)],
        (own_arg, *lefts, *rights),
    )[0]


def gate_kernel(micro, chunk, per_part, own_ref, *refs):
    gain_ref, refs = refs[0], refs[1:]
    ssm, gate, back, stat, normed = (refs[k * micro : (k + 1) * micro] for k in range(5))
    outs = refs[5 * micro :]
    grad_ssm, grad_gate, gated_all = (outs[k * micro : (k + 1) * micro] for k in range(3))
    grad_gain_ref, out_ref = outs[3 * micro :]
    count = stat[0].shape[0]
    half = gain_ref.shape[1]

    grad_gain_ref[...] = jnp.zeros_like(grad_gain_ref)

    def step(t, carry):
        place = lax.bitwise_xor(t // per_part, own_ref[0]) * per_part + t % per_part
        rows = pl.ds(pl.multiple_of(place * chunk, chunk), chunk)
        for m in range(micro):
            sums = stat[m][t]
            scale = lax.rsqrt(sums[0:1, :] * (1.0 / INNER) + EPSILON)
            shift = scale * scale * scale * sums[1:2, :] * (1.0 / INNER)
            scale = columns(scale, chunk)
            shift = columns(shift, chunk)
            for at in range(0, half, LANES):
                lanes = slice(at, at + LANES)
                out = ssm[m][rows, lanes].astype(F32)
                branch = gate[m][rows, lanes].astype(F32)
                grad = back[m][rows, lanes].astype(F32)
                sig = jax.nn.sigmoid(branch)
                silu = branch * sig
                gated = out * silu
                scaled = gated * scale
                gain = gain_ref[:, lanes]
                grad_gated = scale * (gain * grad) - gated * shift
                grad_ssm[m][rows, lanes] = (grad_gated * silu).astype(BF16)
                grad_gate[m][rows, lanes] = (
                    grad_gated * out * (sig * (1.0 + branch * (1.0 - sig)))
                ).astype(BF16)
                gated_all[m][rows, lanes] = (scaled * gain).astype(BF16)
                grad_gain_ref[0:1, lanes] += jnp.sum(scaled * grad, axis=0, keepdims=True)
        return carry

    lax.fori_loop(0, count, step, 0)

    terms = [dot(a[...], b[...], TN) for a, b in zip(grad_gate, normed)]
    out_ref[...] = sum(terms[1:], terms[0]).astype(BF16).reshape(out_ref.shape)


def gate_grads(own_arg, scans, stats, normed, gain, per_part, lines):
    micro = len(scans)
    (tokens, inner), width = scans[0][0].shape, normed[0].shape[1]
    share = inner // 2 // lines
    taken = max(1, min(lines, 256 // share))
    block = taken * share
    chunk = stats[0].shape[2]
    cols = pl.BlockSpec((tokens, block), lambda i, own: (0, i))
    row = pl.BlockSpec((1, block), lambda i, own: (0, i))
    sums = pl.BlockSpec((8, block), lambda i, own: (0, i))
    struct = jax.ShapeDtypeStruct
    outs = call(
        partial(gate_kernel, micro, chunk, per_part),
        (inner // block,),
        [row] + [cols] * (3 * micro) + [fixed(stats[0].shape)] * micro + [fixed((tokens, width))] * micro,
        [cols] * (3 * micro)
        + [sums]
        + [
            pl.BlockSpec(
                (taken, None, share, width),
                lambda i, own: (i % (lines // taken), i // (lines // taken), 0, 0),
            )
        ],
        [struct((tokens, inner), BF16)] * (3 * micro)
        + [struct((8, inner), F32), struct((lines, 2, share, width), BF16)],
        (own_arg, gain, *[scan[k] for k in range(3) for scan in scans], *stats, *normed),
    )
    split = [outs[k * micro : (k + 1) * micro] for k in range(3)]
    return split + list(outs[3 * micro :])


def fill_kernel(own_ref, part_ref, *refs):
    out_ref = refs[-1]
    out_ref[...] = part_ref[...].reshape(out_ref.shape).astype(F32)


def fill(own_arg, whole, rows, part, grid, part_spec, out_spec):
    width = part.shape[-1]
    return pl.pallas_call(
        fill_kernel,
        grid_spec=pltpu.PrefetchScalarGridSpec(
            num_scalar_prefetch=1,
            grid=grid,
            in_specs=[part_spec] + [pl.BlockSpec(memory_space=pl.ANY)] * (whole is not None),
            out_specs=out_spec,
        ),
        out_shape=jax.ShapeDtypeStruct((rows, width), F32),
        input_output_aliases={} if whole is None else {2: 0},
        compiler_params=pltpu.CompilerParams(
            dimension_semantics=("arbitrary",) * len(grid), vmem_limit_bytes=VMEM
        ),
        cost_estimate=COST,
    )(*([own_arg, part] + ([] if whole is None else [whole])))


IN_ROWS = 2 * INNER + 2 * STATE + HEADS


def fill_lines(own_arg, whole, part, kept):
    lines, parts, share, rows = part.shape
    return fill(
        own_arg,
        whole,
        IN_ROWS,
        part,
        (parts,),
        pl.BlockSpec((lines, None, share, rows), lambda f, own: (0, f, 0, 0)),
        pl.BlockSpec((lines * share, rows), lambda f, own: (2 * f + half_of(own, kept), 0)),
    )


def fill_tail(own_arg, whole, part):
    return fill(
        own_arg,
        whole,
        IN_ROWS,
        part,
        (part.shape[0] // HEADS,),
        pl.BlockSpec((HEADS, part.shape[1]), lambda i, own: (i, 0)),
        pl.BlockSpec((HEADS, part.shape[1]), lambda i, own: (2 * INNER // HEADS + i, 0)),
    )


def fill_heads(own_arg, whole, part, first):
    lines, _, parts, share, rows = part.shape
    size = lines * share
    return fill(
        own_arg,
        whole,
        IN_ROWS,
        part,
        (parts, 2),
        pl.BlockSpec((lines, None, None, share, rows), lambda f, k, own: (0, k, f, 0, 0)),
        pl.BlockSpec((size, rows), lambda f, k, own: (first // size + 2 * f + k, 0)),
    )


def on_device(
    tokens,
    segment_ids,
    cotangent,
    norm_gain,
    in_weight,
    conv_weight,
    conv_bias,
    dt_bias,
    a_log,
    skip_d,
    inner_gain,
    out_weight,
):
    micro, _, tok_count, width = tokens.shape
    parts = lax.axis_size("fsdp")
    groups = lax.axis_size("group")
    own = lax.axis_index("fsdp")
    inner = INNER // parts
    heads = HEADS // parts
    channels = inner + 2 * STATE
    rows = width // parts
    seq = tok_count * parts
    chunk = min(LANES, tok_count)
    forward, backward = scan_calls(parts, tok_count, inner)
    side = lax.axis_index("group") & 3
    own_arg = jnp.stack([own, side]).astype(jnp.int32)
    along = Lines()

    def small(sent):
        taps_here = jnp.concatenate([conv_weight, conv_bias[None]], axis=0).astype(F32)
        packed = jnp.concatenate(
            [
                norm_gain.astype(F32),
                taps_here.reshape(-1),
                segment_ids.astype(F32).reshape(-1),
            ]
        )
        held = gather_far(after(packed, sent))
        packed = jnp.stack(absolute(gather_near(held)))
        cut = norm_gain.shape[0]
        gain_norm = packed[:, :cut].reshape(-1)
        taps_size = taps_here.size
        taps = packed[:, cut : cut + taps_size].reshape(parts, CONV + 1, -1)
        taps = taps.transpose(1, 0, 2).reshape(CONV + 1, XBC)
        seg = packed[:, cut + taps_size :].reshape(parts, micro, tok_count)
        seg = seg.transpose(1, 0, 2).reshape(micro, seq)
        taps = jnp.concatenate(
            [lax.dynamic_slice_in_dim(taps, own * inner, inner, 1), taps[:, INNER:]], axis=1
        )
        taps = jnp.pad(taps, ((0, 8 - CONV - 1), (0, 0)))
        seg_rows = [seg] + [
            jnp.pad(seg[:, ahead:], ((0, 0), (0, ahead)), constant_values=-1.0)
            for ahead in range(1, CONV)
        ]
        seg_rows = jnp.stack([part.reshape(micro, -1, chunk) for part in seg_rows], axis=2)
        seg_rows = jnp.pad(seg_rows, ((0, 0), (0, 0), (0, 8 - CONV), (0, 0)))
        head_row = jnp.concatenate(
            [dt_bias.astype(F32)[None], -jnp.exp(a_log.astype(F32))[None]], axis=0
        )
        head_row = jnp.pad(head_row, ((0, 6), (0, LANES - heads)))
        skip_row = jnp.repeat(skip_d.astype(F32), HEADDIM)[None]
        gain_row = inner_gain.astype(F32)[None]
        return held[parts // 2], (gain_norm, taps, seg_rows, head_row, skip_row, gain_row)

    in_rows = in_weight.T
    started = {}

    def between(sent, got):
        packed, started["small"] = small(sent)
        started["tok"] = [gather_far(after(tokens[0, 0], got))]
        started["tail"] = gather_far(after(in_rows[2 * INNER :], got))
        first = started["tok"][0][parts // 2]
        started["tok"] += [gather_far(after(tokens[m, 0], first)) for m in range(1, micro)]
        started["cot"] = [gather_far(after(cotangent[0, 0], first))]
        return [first, packed], [started["tail"][parts // 2], *started["small"]]

    with jax.named_scope("weights"):
        weights = traded_weights(in_rows, inner, between)
    gain_norm, taps, seg_rows, head_row, skip_row, gain_row = started["small"]
    tails = gather_near(started["tail"], weights[1])

    projected = []
    for m in range(micro):
        tok_here = gather_near(started["tok"][m], weights[1], *[p[0] for p in projected[-1:]])
        projected.append(project(own_arg, tok_here, weights, tails, gain_norm))
    normed_all = [p[0] for p in projected]
    for m in range(1, micro):
        started["cot"].append(
            gather_far(after(cotangent[m, 0], started["tok"][m][parts // 2], normed_all[0]))
        )
    scans = []
    cot_all = []
    for m in range(micro):
        parts_here = gather_near(started["cot"][m], *(scans[m - 1][-1:] if m else normed_all[-1:]))
        cot, back = project_back(own_arg, parts_here, out_weight)
        _, gate, pre, tail, dt_raw = projected[m]
        outs = forward(
            own_arg, pre, tail, gate, dt_raw, back, seg_rows[m], taps, head_row, skip_row, gain_row
        )
        cot_all.append(cot)
        scans.append((gate, pre, tail, dt_raw, back) + tuple(outs))
    stats = [
        jnp.pad(summed(scan[-1][:, :2], "fsdp"), ((0, 0), (0, 6), (0, 0))) for scan in scans
    ]

    def scan_back(m, *earlier):
        _, pre, tail, dt_raw, _, act, slope, _, _, entering, _ = scans[m]
        return backward(
            own_arg,
            act,
            slope,
            pre,
            tail,
            dt_raw,
            after(grad_ssm[m], *earlier),
            entering,
            seg_rows[m],
            taps,
            head_row,
            skip_row,
        )

    def across(away):
        return swap(away, "group", 1)

    lines_count = groups // 2
    lane = lax.axis_index("group") & 1

    def joined(keep, got):
        return join(own_arg, keep, got).reshape(lines_count, -1, width)

    grad_ssm, grad_gates, gated, grad_inner, gate_out = gate_grads(
        own_arg,
        [(scan[7], scan[0], scan[4]) for scan in scans],
        stats,
        normed_all,
        gain_row,
        tok_count // chunk,
        lines_count,
    )
    half_gate = along.scatter(gate_out.reshape(groups, -1, width))
    gated = [after(g, gate_out) for g in gated]
    away_out = weight_grad(own_arg, gated, cot_all, inner, False)
    with jax.named_scope("away_out"):
        got_out = across(away_out)
    gated = [after(g, away_out) for g in gated]
    keep_out = weight_grad(own_arg, gated, cot_all, inner, True)
    backs = [scan_back(0, keep_out)]
    half_out = joined(keep_out, after(got_out, backs[0][0]))
    with jax.named_scope("trade_gate"):
        trade = Trade(own_arg, after(half_gate, half_out), parts)
    for m in range(1, micro):
        backs.append(scan_back(m, half_out, trade.sent))
    with jax.named_scope("trade_gate"):
        trade.middle(backs[-1][0])
        gate_cols = trade.final()
    left = [after(b[0], gate_cols) for b in backs]
    away_x = weight_grad(own_arg, left, normed_all, inner, False)
    with jax.named_scope("away_heads"):
        got_x = across(away_x)
    left = [after(b[0], away_x) for b in backs]
    keep_x = weight_grad(own_arg, left, normed_all, inner, True)
    half_out = along.scatter(half_out, lines())
    gate_lines = along.gather(after(gate_cols, away_x), lines())

    into = []
    for m in range(micro):
        grad_gate = after(grad_gates[m], keep_x, *(part[0] for part in into[-1:]))
        into.append(project_into(own_arg, grad_gate, *backs[m][:2], weights, tails))
    half_x = joined(keep_x, after(got_x, into[-1][0]))
    with jax.named_scope("gate_lines"):
        got_lines = across(after(gate_lines, half_x))
    rights = [after(n, half_x) for n in normed_all]
    tail_part = tail_grad(own_arg, [b[0] for b in backs], [b[1] for b in backs], rights, parts)

    def split(pair, name):
        with jax.named_scope(name):
            return Split(own_arg, [after(part, half_x) for part in pair])

    into = [split(pair, "into") for pair in into]
    tail_part = split(tail_part, "tail")
    with jax.named_scope("into"):
        sent = [part.middle() for part in into]
    with jax.named_scope("tail"):
        sent.append(tail_part.middle())
    keep, got = tail_part.final(*sent)
    steps = [keep + got.astype(F32)]
    with jax.named_scope("tail"):
        grad_tail = summed(steps[0], "group", BF16, True, steps)
    mixed = []
    for m in range(micro):
        gained = after(scans[m][8], steps[0], *sent, *(pair[0] for pair in mixed[-1:]))
        mixed.append(project_out(own_arg, gained, out_weight, parts))
    half_x = along.scatter(half_x, lines())
    with jax.named_scope("trade_heads"):
        trade = Trade(own_arg, after(half_x, mixed[-1][0]), parts)
    out_pin = mixed[-1][0]
    sent = trade.sent
    grad_tok = []
    grad_norm = jnp.zeros((width,), F32)
    for m in range(micro):
        terms = into[m].final(sent, got_lines, steps[min(m + 1, len(steps) - 1)])
        tok, gain = norm_rows(own_arg, tokens[m, 0], cotangent[m, 0], gain_norm, terms)
        grad_tok.append(tok)
        grad_norm += gain[0]
        if m == 0:
            with jax.named_scope("trade_heads"):
                sent = trade.middle(tok)
    with jax.named_scope("trade_heads"):
        x_cols = trade.final(tok)
    grad_taps = sum(b[2] for b in backs)[: CONV + 1]
    grad_skip = sum(b[3] for b in backs)[0]
    grad_head = sum(b[4] for b in backs)
    taps_all = lax.dynamic_update_slice_in_dim(
        jnp.zeros((CONV + 1, XBC), F32), grad_taps[:, :inner], own * inner, 1
    )
    taps_all = taps_all.at[:, INNER:].set(grad_taps[:, inner:])
    with jax.named_scope("small"):
        joint = summed(jnp.concatenate([taps_all.reshape(-1), grad_norm]), "fsdp")
    skip_sum = jnp.sum(grad_skip.reshape(heads, HEADDIM), axis=1)
    joint = jnp.concatenate(
        [joint, grad_inner[0], grad_head[0, :heads], grad_head[1, :heads], skip_sum]
    )

    with jax.named_scope("small"):
        joint = summed(joint, "group")
    out_lines = along.gather(after(half_out, out_pin), lines())
    with jax.named_scope("out_lines"):
        got_out = across(after(out_lines, joint, grad_tail))
    x_all = along.gather(after(x_cols, joint, grad_tail))
    with jax.named_scope("mixed"):
        mixed = [Split(own_arg, [after(part, x_cols) for part in pair]) for pair in mixed]
        for part in mixed:
            part.middle()

    def all_lines(value):
        return value.reshape(lines_count, 2, parts, -1, rows)

    whole = fill_lines(own_arg, None, after(gate_lines, x_cols), True)
    whole = fill_lines(own_arg, whole, after(got_lines, x_cols), False)
    whole = fill_tail(own_arg, whole, grad_tail)
    grad_out = jnp.stack(
        [
            jnp.where(lane == 0, out_lines, got_out),
            jnp.where(lane == 0, got_out, out_lines),
        ]
    )
    grad_out = grad_out.reshape(inner, width).astype(F32)

    for m in range(micro):
        stat = lax.dynamic_slice_in_dim(
            stats[m][:, 0].reshape(seq), own * tok_count, tok_count, 0
        )
        scale = lax.rsqrt(stat * (1.0 / INNER) + EPSILON)[:, None]
        mixed[m] = mixed_rows(own_arg, tokens[m, 0], scale, mixed[m].final(whole))

    at = (CONV + 1) * XBC
    share = XBC // parts
    taps_all = lax.dynamic_slice_in_dim(joint[:at].reshape(CONV + 1, XBC), own * share, share, 1)
    grad_norm = lax.dynamic_slice_in_dim(joint, at + own * rows, rows, 0)
    at += width
    grad_inner = joint[at : at + inner]
    at += inner
    grad_bias, grad_rate, grad_skip = (
        joint[at + k * heads : at + (k + 1) * heads] for k in range(3)
    )
    mixed = jnp.stack(mixed)[:, None]
    grad_tok = jnp.stack(grad_tok)[:, None]
    x_all = after(x_all, whole, grad_out, grad_norm, mixed, grad_tok)
    grad_in = fill_heads(own_arg, whole, all_lines(x_all), INNER).T
    return (
        mixed,
        grad_tok,
        grad_norm,
        grad_in,
        taps_all[:CONV],
        taps_all[CONV],
        grad_bias,
        grad_rate,
        grad_skip,
        grad_inner,
        grad_out,
    )


def solution(mesh):
    rows = P(None, "group", "fsdp", None)
    shard = P("fsdp")
    in_specs = (rows, P(None, "group", "fsdp"), rows, shard, P("fsdp", None), P(None, "fsdp"))
    in_specs += (shard,) * 5 + (P("fsdp", None),)
    out_specs = (rows, rows, shard, P("fsdp", None), P(None, "fsdp")) + (shard,) * 5
    out_specs += (P("fsdp", None),)
    return jax.shard_map(
        on_device, mesh=mesh, in_specs=in_specs, out_specs=out_specs, check_vma=False
    )
```

```python
from functools import partial

import jax
import jax.numpy as jnp
from jax import lax
from jax.experimental import pallas as pl
from jax.experimental.pallas import tpu as pltpu
from jax.sharding import PartitionSpec as P

INNER = 4096
HEADS = 64
HEADDIM = 64
STATE = 128
CONV = 4
XBC = 4352
LANES = 128
EPSILON = 1e-05
FAR = -1e30
HIGHEST = lax.Precision.HIGHEST
VMEM = 48 * 1024 * 1024
F32 = jnp.float32
BF16 = jnp.bfloat16


def swap(value, axis, bit):
    count = lax.axis_size(axis)
    with jax.named_scope(f"{axis}_{bit}"):
        return lax.ppermute(value, axis, [(i, i ^ bit) for i in range(count)])


def after(value, *earlier):
    return lax.optimization_barrier((value,) + earlier)[0] if earlier else value


def bits_of(count):
    return [1 << k for k in reversed(range(count.bit_length() - 1))]


def gather_far(piece):
    held = {0: piece}
    for bit in bits_of(lax.axis_size("fsdp"))[:-1]:
        for r, part in list(held.items()):
            held[r ^ bit] = swap(part, "fsdp", bit)
    return held


def gather_near(held, *later):
    for r, part in list(held.items()):
        held[r ^ 1] = swap(after(part, *later) if r else part, "fsdp", 1)
    return [held[r] for r in range(len(held))]


def gathered(piece):
    return gather_near(gather_far(piece))


def permuted(parts, own):
    stacked = jnp.stack(parts)
    return [
        lax.dynamic_index_in_dim(stacked, own ^ i, 0, keepdims=False) for i in range(len(parts))
    ]


def absolute(parts):
    return permuted(parts, lax.axis_index("fsdp"))


def traded(blocks, send):
    held = {r: {0: block} for r, block in enumerate(blocks)}
    for bit in bits_of(len(blocks)):
        going = [r for r in sorted(held) if r & bit]
        sources = sorted(held[going[0]])
        got = send(jnp.stack([held[r][s] for r in going for s in sources]), bit)
        place = 0
        for r in going:
            for s in sources:
                held[r ^ bit][s ^ bit] = got[place]
                place += 1
            del held[r]
    return [held[0][s] for s in sorted(held[0])]


def traded_weights(in_rows, inner, between):
    own = lax.axis_index("fsdp")
    side = lax.axis_index("group") & 3
    rows = in_rows.shape[1]
    half = inner // 2
    parts = lax.axis_size("fsdp")

    def block(r, kind, first, size):
        at = kind * INNER + (own ^ r) * inner + first
        return lax.dynamic_slice(in_rows, (at, jnp.zeros_like(at)), (size, rows))

    def piece(r, s):
        if s in held[r]:
            return held[r][s]
        return jnp.stack([block(r, kind, 0, inner) for kind in (0, 1)]).reshape(4, half, rows)

    def quarter(r, s):
        if s in held[r]:
            return held[r][s][0]
        return block(r, side // 2, (side & 1) * half, half)

    held = {r: {} for r in range(parts)}
    sources = [0]
    pins = None
    for bit in bits_of(parts):
        going = [r for r in sorted(held) if r & bit]
        order = [(r, s) for r in going for s in sources]
        if bit > 1:
            sent = jnp.stack([quarter(r, s) for r, s in order])
            mine = swap(sent, "fsdp", bit)
            if pins is None:
                pins = between(sent, mine)
            by_x = swap(mine, "group", 1)
            by_z = swap(mine, "group", 2)
            cut = half // 2
            rest = [
                swap(after(by_z[:, :cut], *pins[0]), "group", 1),
                swap(after(by_x[:, cut:], *pins[0]), "group", 2),
            ]
            got = jnp.stack([mine, by_x, by_z, jnp.concatenate(rest, axis=1)], axis=1)
        else:
            got = [swap(after(piece(r, s), *pins[1]), "fsdp", bit) for r, s in order]
        for (r, s), part in zip(order, got):
            held[r ^ bit][s ^ bit] = part
        for r in going:
            del held[r]
        sources += [s ^ bit for s in sources]
    return [piece(0, s) for s in range(parts)]


def scattered(value):
    bit = 1
    while value.shape[0] > 1:
        pairs = value.reshape((value.shape[0] // 2, 2) + value.shape[1:])
        got = swap(pairs[:, 1].astype(BF16), "fsdp", bit)
        value = pairs[:, 0].astype(F32) + got.astype(F32)
        bit *= 2
    return value[0]


def summed(value, axis, kind=F32, far_first=False, steps=None):
    bits = bits_of(lax.axis_size(axis))
    for bit in bits if far_first else bits[::-1]:
        value = value + swap(value.astype(kind), axis, bit).astype(F32)
        if steps is not None:
            steps.append(value)
    return value


def lines():
    count = lax.axis_size("group")
    return [list(range(side, count, 2)) for side in (0, 1)]


class Lines:
    def __init__(self):
        self.last = None

    def order(self, value):
        return value if self.last is None else after(value, self.last)

    def scatter(self, value, among=None):
        self.last = lax.psum_scatter(
            self.order(value), "group", scatter_dimension=0, axis_index_groups=among
        )
        return self.last

    def gather(self, value, among=None):
        self.last = lax.all_gather(
            self.order(value), "group", axis=0, axis_index_groups=among
        )
        return self.last


def dot(a, b, contract=((1,), (0,)), precision=None):
    return lax.dot_general(a, b, (contract, ((), ())), precision=precision, preferred_element_type=F32)


def steps(dt_ref, head_ref, tri):
    raw = dt_ref[...] + head_ref[0:1, :]
    size = jnp.maximum(raw, 0.0) + jnp.log1p(jnp.exp(-jnp.abs(raw)))
    log_decay = size * head_ref[1:2, :]
    running = dot(tri, log_decay, precision=HIGHEST)
    return raw, size, log_decay, running


def columns(row, chunk):
    return jnp.broadcast_to(row, (LANES, chunk)).T


def squared(array, chunk):
    return array if chunk == LANES else array[:, :chunk]


def forward_kernel(
    chunk,
    own_ref,
    pre_ref,
    tail_ref,
    gate_ref,
    dt_ref,
    back_ref,
    row_ref,
    taps_ref,
    head_ref,
    skip_ref,
    gain_ref,
    act_ref,
    slope_ref,
    out_ref,
    gained_ref,
    enter_ref,
    stat_ref,
    state,
    window,
    carried,
    flown,
):
    where = pl.program_id(0)
    inner = gate_ref.shape[1]
    channels = act_ref.shape[1]

    @pl.when(where == 0)
    def _():
        state[...] = jnp.zeros_like(state)
        window[0:8, :] = jnp.zeros((8, channels), F32)

    start = (where * chunk).astype(F32)
    seg_row = row_ref[0:1, :]
    seg_col = columns(seg_row, chunk)
    time = lax.broadcasted_iota(jnp.int32, (chunk, LANES), 0).astype(F32) + start
    seen = [(seg_col <= time - back).astype(F32) for back in range(1, CONV)]
    window[8:, :inner] = pre_ref[...].astype(F32)
    window[8:, inner:] = tail_ref[...].astype(F32)
    for at in range(0, channels, LANES):
        lanes = slice(at, at + LANES)
        total = taps_ref[4:5, lanes] + taps_ref[3:4, lanes] * window[8 : 8 + chunk, lanes]
        for back in range(1, CONV):
            total += taps_ref[3 - back : 4 - back, lanes] * (
                window[8 - back : 8 - back + chunk, lanes] * seen[back - 1]
            )
        sig = jax.nn.sigmoid(total)
        act_ref[:, lanes] = (total * sig).astype(BF16)
        slope_ref[:, lanes] = (sig * (1.0 + total * (1.0 - sig))).astype(BF16)
    window[0:8, :] = window[chunk : chunk + 8, :]

    seg_last = seg_row[:, chunk - 1 : chunk]
    down = lax.broadcasted_iota(jnp.int32, (chunk, chunk), 0)
    across = lax.broadcasted_iota(jnp.int32, (chunk, chunk), 1)
    tri = (across <= down).astype(F32)
    _, size, _, running = steps(dt_ref, head_ref, tri)
    running_t = running.T
    size_t = size.T
    b_input = act_ref[:, inner : inner + STATE]
    c_output = act_ref[:, inner + STATE :]
    gram = dot(c_output, b_input, ((1,), (1,)))
    veil = jnp.where((squared(seg_col, chunk) == seg_row) & (across <= down), 0.0, FAR)
    crossing = (seg_col < start).astype(F32)
    ending = (seg_col == seg_last).astype(F32)
    passing = (seg_last < start).astype(F32)
    last = running[chunk - 1 : chunk, :]
    low = lax.broadcasted_iota(jnp.int32, (chunk, LANES), 1) < HEADDIM
    low_row = low[0:1, :]
    entering = state[...].astype(BF16)
    enter_ref[...] = entering
    carried[...] = dot(c_output, entering)
    squares = jnp.zeros((chunk, LANES), F32)
    products = jnp.zeros((chunk, LANES), F32)
    for pair in range(inner // LANES):
        lanes = slice(pair * LANES, (pair + 1) * LANES)
        heads = (2 * pair, 2 * pair + 1)
        x_pair = act_ref[:, lanes].astype(F32)
        run = [running[:, h : h + 1] for h in heads]
        mixing = [
            (jnp.exp(run[k] - running_t[h : h + 1, :] + veil) * gram * size_t[h : h + 1, :]).astype(
                BF16
            )
            for k, h in enumerate(heads)
        ]
        halves = [jnp.where(low, x_pair, 0.0).astype(BF16), jnp.where(low, 0.0, x_pair).astype(BF16)]
        inside = dot(jnp.concatenate(mixing, axis=1), jnp.concatenate(halves, axis=0))
        run_pair = jnp.where(low, run[0], run[1])
        size_pair = jnp.where(low, size[:, heads[0] : heads[0] + 1], size[:, heads[1] : heads[1] + 1])
        last_pair = jnp.where(
            low_row, last[:, heads[0] : heads[0] + 1], last[:, heads[1] : heads[1] + 1]
        )
        ssm = (
            inside
            + carried[:, lanes] * (jnp.exp(run_pair) * crossing)
            + skip_ref[:, lanes] * x_pair
        )
        outflow = jnp.exp(last_pair - run_pair) * ending * size_pair
        flown[:, lanes] = (x_pair * outflow).astype(BF16)
        state[:, lanes] = (jnp.exp(last_pair) * passing) * state[:, lanes]
        gate = gate_ref[:, lanes].astype(F32)
        gated = ssm * (gate * jax.nn.sigmoid(gate))
        out_ref[:, lanes] = ssm.astype(BF16)
        gained = gated * gain_ref[:, lanes]
        gained_ref[:, lanes] = gained.astype(BF16)
        squares += gated * gated
        products += gained * back_ref[:, lanes].astype(F32)
    state[...] += dot(b_input, flown[...], ((0,), (0,)))
    stat_ref[0:1, :] = jnp.sum(squares.T, axis=0, keepdims=True)
    stat_ref[1:2, :] = jnp.sum(products.T, axis=0, keepdims=True)
    stat_ref[2:8, :] = jnp.zeros((6, chunk), F32)


def backward_kernel(
    chunk,
    own_ref,
    act_ref,
    slope_ref,
    pre_ref,
    tail_ref,
    dt_ref,
    grad_ref,
    enter_ref,
    row_ref,
    taps_ref,
    head_ref,
    skip_ref,
    grad_pre_ref,
    grad_dt_ref,
    grad_taps_ref,
    grad_skip_ref,
    grad_head_ref,
    leaving,
    window,
    grad_act,
    row_sums,
    carried,
    fresh,
    into,
    flown,
):
    count = pl.num_programs(0)
    where = count - 1 - pl.program_id(0)
    inner = grad_ref.shape[1]
    channels = act_ref.shape[1]

    @pl.when(pl.program_id(0) == 0)
    def _():
        leaving[...] = jnp.zeros_like(leaving)
        window[chunk:, :] = jnp.zeros((8, channels), F32)
        grad_taps_ref[...] = jnp.zeros_like(grad_taps_ref)
        grad_skip_ref[...] = jnp.zeros_like(grad_skip_ref)
        grad_head_ref[...] = jnp.zeros_like(grad_head_ref)
        row_sums[...] = jnp.zeros_like(row_sums)

    start = (where * chunk).astype(F32)
    seg_row = row_ref[0:1, :]
    seg_col = columns(seg_row, chunk)
    seg_last = seg_row[:, chunk - 1 : chunk]
    down = lax.broadcasted_iota(jnp.int32, (chunk, chunk), 0)
    across = lax.broadcasted_iota(jnp.int32, (chunk, chunk), 1)
    tri = (across <= down).astype(F32)
    raw, size, log_decay, running = steps(dt_ref, head_ref, tri)
    running_t = running.T
    b_input = act_ref[:, inner : inner + STATE]
    c_output = act_ref[:, inner + STATE :]
    gram = dot(b_input, c_output, ((1,), (1,)))
    veil = jnp.where((squared(seg_col, chunk) == seg_row) & (down <= across), 0.0, FAR)
    crossing = (seg_col < start).astype(F32)
    ending = (seg_col == seg_last).astype(F32)
    passing = (seg_last < start).astype(F32)
    last = running[chunk - 1 : chunk, :]
    lane = lax.broadcasted_iota(jnp.int32, (chunk, LANES), 1)
    low = lane < HEADDIM
    low_row = low[0:1, :]
    lane_row = lane[0:1, :]
    left_low = leaving[...].astype(BF16)
    entering = enter_ref[...]
    carried[...] = dot(c_output, entering)
    fresh[...] = dot(b_input, left_low)
    grad_gram = jnp.zeros((chunk, chunk), F32)
    size_grad = jnp.zeros((chunk, LANES), F32)
    carry_grad = jnp.zeros((chunk, LANES), F32)
    total_grad = jnp.zeros((1, LANES), F32)
    for pair in range(inner // LANES):
        lanes = slice(pair * LANES, (pair + 1) * LANES)
        heads = (2 * pair, 2 * pair + 1)
        x_low = act_ref[:, lanes]
        x_pair = x_low.astype(F32)
        grad = grad_ref[:, lanes].astype(F32)
        halves = (low, jnp.logical_not(low))
        run = [running[:, h : h + 1] for h in heads]
        sizes = [size[:, h : h + 1] for h in heads]
        run_pair = jnp.where(low, run[0], run[1])
        size_pair = jnp.where(low, sizes[0], sizes[1])
        last_pair = jnp.where(
            low_row, last[:, heads[0] : heads[0] + 1], last[:, heads[1] : heads[1] + 1]
        )
        left = leaving[:, lanes]
        inflow = jnp.exp(run_pair) * crossing
        outflow = jnp.exp(last_pair - run_pair) * ending
        into_here = grad * inflow
        into[:, lanes] = into_here.astype(BF16)
        carry_here = into_here * carried[:, lanes]
        fresh_back = fresh[:, lanes] * outflow
        flown_here = x_pair * fresh_back
        flown[:, lanes] = (x_pair * outflow * size_pair).astype(BF16)
        whole = jnp.exp(last_pair) * passing
        kept = whole * jnp.sum(left * enter_ref[:, lanes].astype(F32), axis=0, keepdims=True)
        kept += jnp.sum(flown_here * size_pair, axis=0, keepdims=True)
        leaving[:, lanes] = whole * left
        both = jnp.concatenate(
            [jnp.where(low, grad, 0.0).astype(BF16), jnp.where(low, 0.0, grad).astype(BF16)], axis=0
        )
        back_both = dot(x_low, both, ((1,), (1,)))
        weights = []
        for k, h in enumerate(heads):
            mine = halves[k]
            decay = jnp.exp(running_t[h : h + 1, :] - run[k] + veil)
            weight = decay * gram
            weights.append((weight * sizes[k]).astype(BF16))
            back = back_both[:, k * chunk : (k + 1) * chunk]
            grad_gram += back * decay * sizes[k]
            straight = back * weight
            row_sums[h : h + 1, :] = jnp.sum(straight * sizes[k], axis=0, keepdims=True)
            flown_mine = jnp.where(mine, flown_here, 0.0)
            if chunk == LANES:
                size_here = jnp.sum(straight + flown_mine, axis=1, keepdims=True)
            else:
                size_here = jnp.sum(straight, axis=1, keepdims=True) + jnp.sum(
                    flown_mine, axis=1, keepdims=True
                )
            carry_mine = jnp.sum(jnp.where(mine, carry_here, 0.0), axis=1, keepdims=True)
            here = lane == h
            size_grad = jnp.where(here, size_here, size_grad)
            carry_grad = jnp.where(here, carry_mine, carry_grad)
            total_here = jnp.sum(jnp.where(mine[0:1, :], kept, 0.0), axis=1, keepdims=True)
            total_grad = jnp.where(lane_row == h, total_here, total_grad)
        grad_act[:, lanes] = (
            dot(jnp.concatenate(weights, axis=1), both)
            + fresh_back * size_pair
            + skip_ref[:, lanes] * grad
        )
        grad_skip_ref[0:1, lanes] += jnp.sum(grad * x_pair, axis=0, keepdims=True)
    grad_gram_low = grad_gram.astype(BF16)
    grad_act[:, inner : inner + STATE] = dot(grad_gram_low, c_output) + dot(
        flown[...], left_low, ((1,), (1,))
    )
    grad_act[:, inner + STATE :] = dot(grad_gram_low, b_input, ((0,), (0,))) + dot(
        into[...], entering, ((1,), (1,))
    )
    leaving[...] += dot(c_output, into[...], ((0,), (0,)))
    row_t = row_sums[...].T
    grad_run = row_t + carry_grad - size * size_grad
    upper = (across >= down).astype(F32)
    grad_decay = dot(upper, grad_run, precision=HIGHEST) + total_grad
    grad_size = grad_decay * head_ref[1:2, :] + size_grad
    grad_raw = jnp.where(lane < inner // HEADDIM, grad_size * jax.nn.sigmoid(raw), 0.0)
    grad_dt_ref[...] = grad_raw.astype(BF16)
    grad_head_ref[0:1, :] += jnp.sum(grad_raw, axis=0, keepdims=True)
    grad_head_ref[1:2, :] += jnp.sum(grad_decay * log_decay, axis=0, keepdims=True)

    same = [
        (columns(row_ref[ahead : ahead + 1, :], chunk) == seg_col).astype(F32)
        for ahead in range(1, CONV)
    ]
    for at in range(0, channels, LANES):
        lanes = slice(at, at + LANES)
        grad_sum = grad_act[:, lanes] * slope_ref[:, lanes].astype(F32)
        window[0:chunk, lanes] = grad_sum
        if at < inner:
            pre = pre_ref[:, lanes].astype(F32)
        else:
            pre = tail_ref[:, at - inner : at - inner + LANES].astype(F32)
        grad_pre = taps_ref[3:4, lanes] * grad_sum
        grad_taps_ref[3:4, lanes] += jnp.sum(pre * grad_sum, axis=0, keepdims=True)
        grad_taps_ref[4:5, lanes] += jnp.sum(grad_sum, axis=0, keepdims=True)
        for ahead in range(1, CONV):
            later = window[ahead : ahead + chunk, lanes] * same[ahead - 1]
            grad_pre += taps_ref[3 - ahead : 4 - ahead, lanes] * later
            grad_taps_ref[3 - ahead : 4 - ahead, lanes] += jnp.sum(
                pre * later, axis=0, keepdims=True
            )
        grad_pre_ref[:, lanes] = grad_pre.astype(BF16)
    window[chunk:, :] = window[0:8, :]


def scan_calls(parts, tok_count, inner):
    chunk = min(LANES, tok_count)
    per_part = tok_count // chunk
    count = parts * per_part
    channels = inner + 2 * STATE
    tokens = parts * tok_count

    def blocks(flip):
        def time(step):
            return count - 1 - step if flip else step

        def place(step, own):
            t = time(step)
            return lax.bitwise_xor(t // per_part, own[0]) * per_part + t % per_part

        def tok(width):
            return pl.BlockSpec((chunk, width), lambda step, own: (place(step, own), 0))

        row = pl.BlockSpec((None, 8, chunk), lambda step, own: (time(step), 0, 0))
        states = pl.BlockSpec((None, STATE, inner), lambda step, own: (time(step), 0, 0))

        def const(rows, width):
            return pl.BlockSpec((rows, width), lambda step, own: (0, 0))

        return tok, row, states, const

    def scan(kernel, ins, outs, shapes, scratch):
        return pl.pallas_call(
            partial(kernel, chunk),
            grid_spec=pltpu.PrefetchScalarGridSpec(
                num_scalar_prefetch=1,
                grid=(count,),
                in_specs=ins,
                out_specs=outs,
                scratch_shapes=scratch,
            ),
            out_shape=shapes,
            compiler_params=pltpu.CompilerParams(
                dimension_semantics=("arbitrary",), vmem_limit_bytes=VMEM
            ),
            cost_estimate=COST,
        )

    struct = jax.ShapeDtypeStruct
    tok, row, states, const = blocks(False)
    forward = scan(
        forward_kernel,
        [tok(inner), tok(2 * STATE), tok(inner), tok(LANES), tok(inner), row]
        + [const(8, channels), const(8, LANES), const(1, inner), const(1, inner)],
        [tok(channels), tok(channels), tok(inner), tok(inner), states, row],
        [
            struct((tokens, channels), BF16),
            struct((tokens, channels), BF16),
            struct((tokens, inner), BF16),
            struct((tokens, inner), BF16),
            struct((count, STATE, inner), BF16),
            struct((count, 8, chunk), F32),
        ],
        [
            pltpu.VMEM((STATE, inner), F32),
            pltpu.VMEM((chunk + 8, channels), F32),
            pltpu.VMEM((chunk, inner), F32),
            pltpu.VMEM((chunk, inner), BF16),
        ],
    )
    tok, row, states, const = blocks(True)
    backward = scan(
        backward_kernel,
        [tok(channels), tok(channels), tok(inner), tok(2 * STATE), tok(LANES)]
        + [tok(inner), states, row]
        + [const(8, channels), const(8, LANES), const(1, inner)],
        [tok(channels), tok(LANES), const(8, channels), const(8, inner), const(8, LANES)],
        [
            struct((tokens, channels), BF16),
            struct((tokens, LANES), BF16),
            struct((8, channels), F32),
            struct((8, inner), F32),
            struct((8, LANES), F32),
        ],
        [
            pltpu.VMEM((STATE, inner), F32),
            pltpu.VMEM((chunk + 8, channels), F32),
            pltpu.VMEM((chunk, channels), F32),
            pltpu.VMEM((LANES, chunk), F32),
            pltpu.VMEM((chunk, inner), F32),
            pltpu.VMEM((chunk, inner), F32),
            pltpu.VMEM((chunk, inner), BF16),
            pltpu.VMEM((chunk, inner), BF16),
        ],
    )
    return forward, backward


NN = ((1,), (0,))
NT = ((1,), (1,))
TN = ((0,), (0,))
COST = pl.CostEstimate(flops=1, bytes_accessed=1, transcendentals=0)


def call(kernel, grid, ins, outs, shapes, args, scratch=()):
    return pl.pallas_call(
        kernel,
        grid_spec=pltpu.PrefetchScalarGridSpec(
            num_scalar_prefetch=1,
            grid=grid,
            in_specs=ins,
            out_specs=outs,
            scratch_shapes=scratch,
        ),
        out_shape=shapes,
        compiler_params=pltpu.CompilerParams(
            dimension_semantics=("arbitrary",) * len(grid), vmem_limit_bytes=VMEM
        ),
        cost_estimate=COST,
    )(*args)


def fixed(shape):
    return pl.BlockSpec(shape, lambda i, own: (0,) * len(shape))


def own_heads(own, heads):
    head = lax.broadcasted_iota(jnp.int32, (HEADS, LANES), 0)
    lane = lax.broadcasted_iota(jnp.int32, (HEADS, LANES), 1)
    return ((head == own * heads + lane) & (lane < heads)).astype(F32)


def project_kernel(parts, own_ref, *refs):
    tok_refs, weights, tails = refs[:parts], refs[parts : 2 * parts], refs[2 * parts : 3 * parts]
    gain_ref, normed_ref, gate_ref, pre_ref, tail_ref, dt_ref, ordered = refs[3 * parts :]
    at = pl.program_id(0)
    rows = tails[0].shape[1]
    tok_count = tok_refs[0].shape[0]

    @pl.when(at == 0)
    def _():
        for r in range(parts):
            values = tok_refs[r][...].astype(F32)
            mean = jnp.mean(values * values, axis=-1, keepdims=True)
            normed_ref[r * tok_count : (r + 1) * tok_count, :] = (
                values * lax.rsqrt(mean + EPSILON) * gain_ref[...]
            ).astype(BF16)
        for s in range(parts):
            lanes = pl.ds(pl.multiple_of(lax.bitwise_xor(own_ref[0], s) * rows, LANES), rows)
            ordered[:, s * rows : (s + 1) * rows] = normed_ref[:, lanes]

    def total(refs):
        return dot(ordered[...], jnp.concatenate([ref[...] for ref in refs], axis=1), NT)

    @pl.when(at < 2)
    def _():
        gate_ref[...] = total(weights).astype(BF16)

    @pl.when((at >= 2) & (at < 4))
    def _():
        pre_ref[...] = total(weights).astype(BF16)

    @pl.when(at == 4)
    def _():
        rest = total(tails)
        tail_ref[...] = rest[:, : 2 * STATE].astype(BF16)
        pick = own_heads(own_ref[0], HEADS // parts)
        dt_ref[...] = dot(rest[:, 2 * STATE :], pick, precision=HIGHEST)


def project(own_arg, tok_parts, weights, tails, gain):
    parts, (tok_count, width) = len(tok_parts), tok_parts[0].shape
    half, rows = weights[0].shape[1:]
    tokens = parts * tok_count

    def near(i, own):
        return (jnp.minimum(i, 3), 0, 0)

    def far(i, own):
        return (lax.bitwise_xor(jnp.minimum(i, 3), own[1]), 0, 0)

    struct = jax.ShapeDtypeStruct
    return call(
        partial(project_kernel, parts),
        (5,),
        [fixed((tok_count, width))] * parts
        + [pl.BlockSpec((None, half, rows), far if s > 1 else near) for s in range(parts)]
        + [fixed(tails[0].shape)] * parts
        + [fixed((1, width))],
        [
            fixed((tokens, width)),
            pl.BlockSpec((tokens, half), lambda i, own: (0, jnp.minimum(i, 1))),
            pl.BlockSpec((tokens, half), lambda i, own: (0, jnp.clip(i - 2, 0, 1))),
            fixed((tokens, 2 * STATE)),
            fixed((tokens, LANES)),
        ],
        [
            struct((tokens, width), BF16),
            struct((tokens, 2 * half), BF16),
            struct((tokens, 2 * half), BF16),
            struct((tokens, 2 * STATE), BF16),
            struct((tokens, LANES), F32),
        ],
        (own_arg, *tok_parts, *weights, *tails, gain[None]),
        [pltpu.VMEM((tokens, width), BF16)],
    )


def back_kernel(parts, own_ref, *refs):
    weight_ref, all_ref, back_ref = refs[parts:]
    tok_count = refs[0].shape[0]

    @pl.when(pl.program_id(0) == 0)
    def _():
        for r in range(parts):
            all_ref[r * tok_count : (r + 1) * tok_count, :] = refs[r][...]

    back_ref[...] = dot(all_ref[...], weight_ref[...], NT).astype(BF16)


def project_back(own_arg, cot_parts, weight):
    parts, (tok_count, width) = len(cot_parts), cot_parts[0].shape
    inner = weight.shape[0]
    block = min(256, inner)
    tokens = parts * tok_count
    struct = jax.ShapeDtypeStruct
    return call(
        partial(back_kernel, parts),
        (inner // block,),
        [fixed((tok_count, width))] * parts
        + [pl.BlockSpec((block, width), lambda i, own: (i, 0))],
        [fixed((tokens, width)), pl.BlockSpec((tokens, block), lambda i, own: (0, i))],
        [struct((tokens, width), BF16), struct((tokens, inner), BF16)],
        (own_arg, *cot_parts, weight),
    )


def split_rows(value, even_ref, odd_ref):
    size = even_ref.shape[0]
    even_ref[...] = value[:size].astype(BF16)
    odd_ref[...] = value[size:].astype(BF16)


def split_outs(tok_count, parts, width):
    spec = pl.BlockSpec((None, tok_count, width), lambda i, own: (i, 0, 0))
    shape = jax.ShapeDtypeStruct((parts // 2, tok_count, width), BF16)
    return [spec, spec], [shape, shape]


def out_kernel(own_ref, a_ref, b_ref, even_ref, odd_ref):
    split_rows(dot(a_ref[...], b_ref[...]), even_ref, odd_ref)


def project_out(own_arg, gained, weight, parts):
    (tokens, inner), width = gained.shape, weight.shape[1]
    tok_count = tokens // parts
    specs, shapes = split_outs(tok_count, parts, width)
    return call(
        out_kernel,
        (parts // 2,),
        [pl.BlockSpec((2 * tok_count, inner), lambda i, own: (i, 0)), fixed((inner, width))],
        specs,
        shapes,
        (own_arg, gained, weight),
    )


def into_kernel(parts, own_ref, gate_ref, pre_ref, dt_ref, *refs):
    weights, tails = refs[:parts], refs[parts : 2 * parts]
    even_ref, odd_ref = refs[2 * parts :]
    half, rows = weights[0].shape[1:]
    pick = own_heads(own_ref[0], HEADS // parts).astype(BF16)
    grad_dt = dot(dt_ref[...], pick, NT).astype(BF16)
    left = jnp.concatenate([gate_ref[...], pre_ref[...], grad_dt], axis=1)
    for s in range(parts):
        order = [lax.bitwise_xor(q, own_ref[1]) if s > 1 else q for q in range(4)]
        right = jnp.concatenate([weights[s][q] for q in order] + [tails[s][...]], axis=0)
        lanes = pl.ds(pl.multiple_of(lax.bitwise_xor(own_ref[0], s) * rows, LANES), rows)
        split_rows(dot(left, right), even_ref.at[:, lanes], odd_ref.at[:, lanes])


def project_into(own_arg, grad_gate, grad_pre, grad_dt, weights, tails):
    parts = len(weights)
    (tokens, inner), channels = grad_gate.shape, grad_pre.shape[1]
    width = parts * weights[0].shape[2]
    tok_count = tokens // parts

    def tok(size):
        return pl.BlockSpec((2 * tok_count, size), lambda i, own: (i, 0))

    specs, shapes = split_outs(tok_count, parts, width)
    return call(
        partial(into_kernel, parts),
        (parts // 2,),
        [tok(inner), tok(channels), tok(LANES)]
        + [fixed(w.shape) for w in weights]
        + [fixed(r.shape) for r in tails],
        specs,
        shapes,
        (own_arg, grad_gate, grad_pre, grad_dt, *weights, *tails),
    )


def tail_kernel(count, parts, own_ref, *refs):
    pres, dts, normed = refs[:count], refs[count : 2 * count], refs[2 * count : 3 * count]
    even_ref, odd_ref = refs[3 * count :]
    pick = own_heads(own_ref[0], HEADS // parts)

    def total(lefts):
        terms = [dot(a[...], b[...], TN) for a, b in zip(lefts, normed)]
        return sum(terms[1:], terms[0])

    value = [total(pres), dot(pick.astype(BF16), total(dts).astype(BF16))]
    value = jnp.concatenate(value, axis=0).astype(BF16)

    @pl.when(pl.program_id(0) % 2 == 0)
    def _():
        even_ref[...] = value

    @pl.when(pl.program_id(0) % 2 == 1)
    def _():
        odd_ref[...] = value


def tail_grad(own_arg, grad_pres, grad_dts, normed, parts):
    (tokens, channels), width = grad_pres[0].shape, normed[0].shape[1]
    count, columns, rows = len(normed), 2 * STATE + HEADS, width // parts
    spec = pl.BlockSpec((None, columns, rows), lambda r, own: (r // 2, 0, 0))
    shape = jax.ShapeDtypeStruct((parts // 2, columns, rows), BF16)
    return call(
        partial(tail_kernel, count, parts),
        (parts,),
        [pl.BlockSpec((tokens, 2 * STATE), lambda r, own: (0, channels // (2 * STATE) - 1))] * count
        + [fixed((tokens, LANES))] * count
        + [pl.BlockSpec((tokens, rows), lambda r, own: (0, lax.bitwise_xor(own[0], r)))] * count,
        [spec, spec],
        [shape, shape],
        (own_arg, *grad_pres, *grad_dts, *normed),
    )


def add_kernel(own_ref, a_ref, b_ref, keep_ref, send_ref):
    keep_ref[...] = a_ref[0].astype(F32) + b_ref[0].astype(F32)
    send_ref[...] = (a_ref[1].astype(F32) + b_ref[1].astype(F32)).astype(BF16)


def add_parts(own_arg, even, got):
    _, size, width = even.shape
    block = size // 2
    both = pl.BlockSpec((2, block, width), lambda i, own: (0, i, 0))
    one = pl.BlockSpec((block, width), lambda i, own: (i, 0))
    struct = jax.ShapeDtypeStruct
    return call(
        add_kernel,
        (2,),
        [both, both],
        [one, one],
        [struct((size, width), F32), struct((size, width), BF16)],
        (own_arg, even, got),
    )


class Split:
    def __init__(self, own_arg, parts):
        self.own_arg = own_arg
        self.even, self.odd = parts
        self.plain = self.even.shape[0] != 2
        self.sent = self.even
        if not self.plain:
            self.got = swap(self.odd, "fsdp", 1)

    def middle(self, *earlier):
        if not self.plain:
            got = after(self.got, *earlier)
            self.keep, self.sent = add_parts(self.own_arg, self.even, got)
            self.got = swap(self.sent, "fsdp", 2)
        return self.sent

    def final(self, *earlier):
        if not self.plain:
            return self.keep, after(self.got, *earlier)
        every = jnp.stack([self.even, self.odd], axis=1)
        every = every.reshape((-1,) + self.even.shape[1:])
        total = scattered(after(every, *earlier))
        return total, jnp.zeros(total.shape, BF16)


def mixed_kernel(own_ref, tok_ref, scale_ref, keep_ref, got_ref, out_ref):
    total = keep_ref[...] + got_ref[...].astype(F32)
    out_ref[...] = (tok_ref[...].astype(F32) + total * scale_ref[...]).astype(BF16)


def mixed_rows(own_arg, tok, scale, terms):
    size, width = tok.shape
    block = min(128, size)
    one = pl.BlockSpec((block, width), lambda i, own: (i, 0))
    return call(
        mixed_kernel,
        (size // block,),
        [one, pl.BlockSpec((block, 1), lambda i, own: (i, 0)), one, one],
        [one],
        [jax.ShapeDtypeStruct((size, width), BF16)],
        (own_arg, tok, scale, *terms),
    )[0]


def norm_kernel(own_ref, tok_ref, cot_ref, gain_ref, keep_ref, got_ref, out_ref, sum_ref):
    @pl.when(pl.program_id(0) == 0)
    def _():
        sum_ref[...] = jnp.zeros_like(sum_ref)

    tok = tok_ref[...].astype(F32)
    inverse = lax.rsqrt(jnp.mean(tok * tok, axis=-1, keepdims=True) + EPSILON)
    hat = tok * inverse
    part = keep_ref[...] + got_ref[...].astype(F32)
    through = part * gain_ref[...]
    here = inverse * (through - hat * jnp.mean(hat * through, axis=-1, keepdims=True))
    out_ref[...] = (cot_ref[...].astype(F32) + here).astype(BF16)
    sum_ref[0:1, :] += jnp.sum(part * hat, axis=0, keepdims=True)


def norm_rows(own_arg, tok, cot, gain, terms):
    size, width = tok.shape
    block = min(128, size)
    one = pl.BlockSpec((block, width), lambda i, own: (i, 0))
    return call(
        norm_kernel,
        (size // block,),
        [one, one, fixed((1, width)), one, one],
        [one, fixed((8, width))],
        [jax.ShapeDtypeStruct((size, width), BF16), jax.ShapeDtypeStruct((8, width), F32)],
        (own_arg, tok, cot, gain[None], *terms),
    )


def join_kernel(own_ref, a_ref, b_ref, out_ref):
    out_ref[...] = (a_ref[...].astype(F32) + b_ref[...].astype(F32)).astype(BF16)


def join(own_arg, keep, got):
    size, width = keep.shape
    one = pl.BlockSpec((size // 4, width), lambda i, own: (i, 0))
    return call(
        join_kernel,
        (4,),
        [one, one],
        [one],
        [jax.ShapeDtypeStruct((size, width), BF16)],
        (own_arg, keep, got),
    )[0]


def pick_kernel(order, own_ref, *refs):
    out_ref = refs[-1]
    rows = out_ref.shape[-1]
    for i, (ref, block, lane) in enumerate(order):
        if lane:
            lanes = pl.ds(pl.multiple_of(lax.bitwise_xor(own_ref[0], block) * rows, LANES), rows)
            out_ref[i] = refs[ref][:, lanes]
        else:
            out_ref[i] = refs[ref][block]


def picked(own_arg, order, args, rows):
    shape = (len(order), args[0].shape[0], rows)
    return call(
        partial(pick_kernel, order),
        (1,),
        [fixed(arg.shape) for arg in args],
        [fixed(shape)],
        [jax.ShapeDtypeStruct(shape, BF16)],
        (own_arg, *args),
    )[0]


def place_kernel(own_ref, half_ref, far_ref, near_ref, out_ref):
    rows = out_ref.shape[-1]
    own = own_ref[0]
    lanes = pl.ds(pl.multiple_of(own * rows, LANES), rows)
    out_ref[own] = half_ref[:, lanes]
    out_ref[lax.bitwise_xor(own, 2)] = far_ref[0]
    out_ref[lax.bitwise_xor(own, 1)] = near_ref[0]
    out_ref[lax.bitwise_xor(own, 3)] = near_ref[1]


class Trade:
    def __init__(self, own_arg, half, parts):
        self.own_arg, self.half, self.parts = own_arg, half, parts
        self.rows = half.shape[1] // parts
        self.sent = half
        self.plain = parts != 4
        if not self.plain:
            self.sent = picked(own_arg, [(0, 2, True), (0, 3, True)], [half], self.rows)
            self.far = swap(self.sent, "fsdp", 2)

    def middle(self, *earlier):
        if not self.plain:
            self.far = after(self.far, *earlier)
            order = [(0, 1, True), (1, 1, False)]
            self.sent = picked(self.own_arg, order, [self.half, self.far], self.rows)
            self.near = swap(self.sent, "fsdp", 1)
        return self.sent

    def final(self, *earlier):
        if self.plain:
            own = lax.axis_index("fsdp")
            here = [
                lax.dynamic_slice_in_dim(self.half, (own ^ r) * self.rows, self.rows, 1)
                for r in range(self.parts)
            ]
            here = traded(here, lambda value, bit: swap(value, "fsdp", bit))
            return jnp.stack(absolute(here))
        near = after(self.near, *earlier)
        shape = (self.parts, self.half.shape[0], self.rows)
        return call(
            place_kernel,
            (1,),
            [fixed(self.half.shape), fixed(self.far.shape), fixed(near.shape)],
            [fixed(shape)],
            [jax.ShapeDtypeStruct(shape, BF16)],
            (self.own_arg, self.half, self.far, near),
        )[0]


def weight_kernel(count, own_ref, *refs):
    out_ref = refs[-1]
    total = dot(refs[0][...], refs[count][...], TN)
    for m in range(1, count):
        total += dot(refs[m][...], refs[count + m][...], TN)
    out_ref[...] = total.astype(out_ref.dtype)


def half_of(own, kept):
    return lax.bitwise_xor(own[1] & 1, 0 if kept else 1)


def weight_grad(own_arg, lefts, rights, inner, kept):
    tokens, width = rights[0].shape
    half, block = inner // 2, 512
    return call(
        partial(weight_kernel, len(lefts)),
        (width // block,),
        [pl.BlockSpec((tokens, half), lambda i, own: (0, half_of(own, kept)))] * len(lefts)
        + [pl.BlockSpec((tokens, block), lambda i, own: (0, i))] * len(rights),
        [pl.BlockSpec((half, block), lambda i, own: (0, i))],
        [jax.ShapeDtypeStruct((half, width), BF16)],
        (own_arg, *lefts, *rights),
    )[0]


def gate_kernel(micro, chunk, per_part, own_ref, *refs):
    gain_ref, refs = refs[0], refs[1:]
    ssm, gate, back, stat, normed = (refs[k * micro : (k + 1) * micro] for k in range(5))
    outs = refs[5 * micro :]
    grad_ssm, grad_gate, gated_all = (outs[k * micro : (k + 1) * micro] for k in range(3))
    grad_gain_ref, out_ref = outs[3 * micro :]
    count = stat[0].shape[0]
    half = gain_ref.shape[1]

    grad_gain_ref[...] = jnp.zeros_like(grad_gain_ref)

    def step(t):
        place = lax.bitwise_xor(t // per_part, own_ref[0]) * per_part + t % per_part
        rows = pl.ds(pl.multiple_of(place * chunk, chunk), chunk)
        for m in range(micro):
            sums = stat[m][t]
            scale = lax.rsqrt(sums[0:1, :] * (1.0 / INNER) + EPSILON)
            shift = scale * scale * scale * sums[1:2, :] * (1.0 / INNER)
            scale = columns(scale, chunk)
            shift = columns(shift, chunk)
            for at in range(0, half, LANES):
                lanes = slice(at, at + LANES)
                out = ssm[m][rows, lanes].astype(F32)
                branch = gate[m][rows, lanes].astype(F32)
                grad = back[m][rows, lanes].astype(F32)
                sig = jax.nn.sigmoid(branch)
                silu = branch * sig
                gated = out * silu
                scaled = gated * scale
                gain = gain_ref[:, lanes]
                grad_gated = scale * (gain * grad) - gated * shift
                grad_ssm[m][rows, lanes] = (grad_gated * silu).astype(BF16)
                grad_gate[m][rows, lanes] = (
                    grad_gated * out * (sig * (1.0 + branch * (1.0 - sig)))
                ).astype(BF16)
                gated_all[m][rows, lanes] = (scaled * gain).astype(BF16)
                grad_gain_ref[0:1, lanes] += jnp.sum(scaled * grad, axis=0, keepdims=True)

    for t in range(count):
        step(t)

    terms = [dot(a[...], b[...], TN) for a, b in zip(grad_gate, normed)]
    out_ref[...] = sum(terms[1:], terms[0]).astype(BF16).reshape(out_ref.shape)


def gate_grads(own_arg, scans, stats, normed, gain, per_part, lines):
    micro = len(scans)
    (tokens, inner), width = scans[0][0].shape, normed[0].shape[1]
    share = inner // 2 // lines
    taken = max(1, min(lines, 256 // share))
    block = taken * share
    chunk = stats[0].shape[2]
    cols = pl.BlockSpec((tokens, block), lambda i, own: (0, i))
    row = pl.BlockSpec((1, block), lambda i, own: (0, i))
    sums = pl.BlockSpec((8, block), lambda i, own: (0, i))
    struct = jax.ShapeDtypeStruct
    outs = call(
        partial(gate_kernel, micro, chunk, per_part),
        (inner // block,),
        [row] + [cols] * (3 * micro) + [fixed(stats[0].shape)] * micro + [fixed((tokens, width))] * micro,
        [cols] * (3 * micro)
        + [sums]
        + [
            pl.BlockSpec(
                (taken, None, share, width),
                lambda i, own: (i % (lines // taken), i // (lines // taken), 0, 0),
            )
        ],
        [struct((tokens, inner), BF16)] * (3 * micro)
        + [struct((8, inner), F32), struct((lines, 2, share, width), BF16)],
        (own_arg, gain, *[scan[k] for k in range(3) for scan in scans], *stats, *normed),
    )
    split = [outs[k * micro : (k + 1) * micro] for k in range(3)]
    return split + list(outs[3 * micro :])


def fill_kernel(own_ref, part_ref, *refs):
    out_ref = refs[-1]
    out_ref[...] = part_ref[...].reshape(out_ref.shape).astype(F32)


def fill(own_arg, whole, rows, part, grid, part_spec, out_spec):
    width = part.shape[-1]
    return pl.pallas_call(
        fill_kernel,
        grid_spec=pltpu.PrefetchScalarGridSpec(
            num_scalar_prefetch=1,
            grid=grid,
            in_specs=[part_spec] + [pl.BlockSpec(memory_space=pl.ANY)] * (whole is not None),
            out_specs=out_spec,
        ),
        out_shape=jax.ShapeDtypeStruct((rows, width), F32),
        input_output_aliases={} if whole is None else {2: 0},
        compiler_params=pltpu.CompilerParams(
            dimension_semantics=("arbitrary",) * len(grid), vmem_limit_bytes=VMEM
        ),
        cost_estimate=COST,
    )(*([own_arg, part] + ([] if whole is None else [whole])))


IN_ROWS = 2 * INNER + 2 * STATE + HEADS


def fill_lines(own_arg, whole, part, kept):
    lines, parts, share, rows = part.shape
    return fill(
        own_arg,
        whole,
        IN_ROWS,
        part,
        (parts,),
        pl.BlockSpec((lines, None, share, rows), lambda f, own: (0, f, 0, 0)),
        pl.BlockSpec((lines * share, rows), lambda f, own: (2 * f + half_of(own, kept), 0)),
    )


def fill_tail(own_arg, whole, part):
    return fill(
        own_arg,
        whole,
        IN_ROWS,
        part,
        (part.shape[0] // HEADS,),
        pl.BlockSpec((HEADS, part.shape[1]), lambda i, own: (i, 0)),
        pl.BlockSpec((HEADS, part.shape[1]), lambda i, own: (2 * INNER // HEADS + i, 0)),
    )


def fill_heads(own_arg, whole, part, first):
    lines, _, parts, share, rows = part.shape
    size = lines * share
    return fill(
        own_arg,
        whole,
        IN_ROWS,
        part,
        (parts, 2),
        pl.BlockSpec((lines, None, None, share, rows), lambda f, k, own: (0, k, f, 0, 0)),
        pl.BlockSpec((size, rows), lambda f, k, own: (first // size + 2 * f + k, 0)),
    )


def on_device(
    tokens,
    segment_ids,
    cotangent,
    norm_gain,
    in_weight,
    conv_weight,
    conv_bias,
    dt_bias,
    a_log,
    skip_d,
    inner_gain,
    out_weight,
):
    micro, _, tok_count, width = tokens.shape
    parts = lax.axis_size("fsdp")
    groups = lax.axis_size("group")
    own = lax.axis_index("fsdp")
    inner = INNER // parts
    heads = HEADS // parts
    channels = inner + 2 * STATE
    rows = width // parts
    seq = tok_count * parts
    chunk = min(LANES, tok_count)
    forward, backward = scan_calls(parts, tok_count, inner)
    side = lax.axis_index("group") & 3
    own_arg = jnp.stack([own, side]).astype(jnp.int32)
    along = Lines()

    def small(sent):
        taps_here = jnp.concatenate([conv_weight, conv_bias[None]], axis=0).astype(F32)
        packed = jnp.concatenate(
            [
                norm_gain.astype(F32),
                taps_here.reshape(-1),
                segment_ids.astype(F32).reshape(-1),
            ]
        )
        held = gather_far(after(packed, sent))
        packed = jnp.stack(absolute(gather_near(held)))
        cut = norm_gain.shape[0]
        gain_norm = packed[:, :cut].reshape(-1)
        taps_size = taps_here.size
        taps = packed[:, cut : cut + taps_size].reshape(parts, CONV + 1, -1)
        taps = taps.transpose(1, 0, 2).reshape(CONV + 1, XBC)
        seg = packed[:, cut + taps_size :].reshape(parts, micro, tok_count)
        seg = seg.transpose(1, 0, 2).reshape(micro, seq)
        taps = jnp.concatenate(
            [lax.dynamic_slice_in_dim(taps, own * inner, inner, 1), taps[:, INNER:]], axis=1
        )
        taps = jnp.pad(taps, ((0, 8 - CONV - 1), (0, 0)))
        seg_rows = [seg] + [
            jnp.pad(seg[:, ahead:], ((0, 0), (0, ahead)), constant_values=-1.0)
            for ahead in range(1, CONV)
        ]
        seg_rows = jnp.stack([part.reshape(micro, -1, chunk) for part in seg_rows], axis=2)
        seg_rows = jnp.pad(seg_rows, ((0, 0), (0, 0), (0, 8 - CONV), (0, 0)))
        head_row = jnp.concatenate(
            [dt_bias.astype(F32)[None], -jnp.exp(a_log.astype(F32))[None]], axis=0
        )
        head_row = jnp.pad(head_row, ((0, 6), (0, LANES - heads)))
        skip_row = jnp.repeat(skip_d.astype(F32), HEADDIM)[None]
        gain_row = inner_gain.astype(F32)[None]
        return held[parts // 2], (gain_norm, taps, seg_rows, head_row, skip_row, gain_row)

    in_rows = in_weight.T
    started = {}

    def between(sent, got):
        packed, started["small"] = small(sent)
        started["tok"] = [gather_far(after(tokens[0, 0], got))]
        started["tail"] = gather_far(after(in_rows[2 * INNER :], got))
        first = started["tok"][0][parts // 2]
        started["tok"] += [gather_far(after(tokens[m, 0], first)) for m in range(1, micro)]
        started["cot"] = [gather_far(after(cotangent[0, 0], first))]
        return [first, packed], [started["tail"][parts // 2], *started["small"]]

    with jax.named_scope("weights"):
        weights = traded_weights(in_rows, inner, between)
    gain_norm, taps, seg_rows, head_row, skip_row, gain_row = started["small"]
    tails = gather_near(started["tail"], weights[1])

    projected = []
    for m in range(micro):
        tok_here = gather_near(started["tok"][m], weights[1], *[p[0] for p in projected[-1:]])
        projected.append(project(own_arg, tok_here, weights, tails, gain_norm))
    normed_all = [p[0] for p in projected]
    for m in range(1, micro):
        started["cot"].append(
            gather_far(after(cotangent[m, 0], started["tok"][m][parts // 2], normed_all[0]))
        )
    scans = []
    cot_all = []
    for m in range(micro):
        parts_here = gather_near(started["cot"][m], *(scans[m - 1][-1:] if m else normed_all[-1:]))
        cot, back = project_back(own_arg, parts_here, out_weight)
        _, gate, pre, tail, dt_raw = projected[m]
        outs = forward(
            own_arg, pre, tail, gate, dt_raw, back, seg_rows[m], taps, head_row, skip_row, gain_row
        )
        cot_all.append(cot)
        scans.append((gate, pre, tail, dt_raw, back) + tuple(outs))
    stats = [
        jnp.pad(summed(scan[-1][:, :2], "fsdp"), ((0, 0), (0, 6), (0, 0))) for scan in scans
    ]

    def scan_back(m, *earlier):
        _, pre, tail, dt_raw, _, act, slope, _, _, entering, _ = scans[m]
        return backward(
            own_arg,
            act,
            slope,
            pre,
            tail,
            dt_raw,
            after(grad_ssm[m], *earlier),
            entering,
            seg_rows[m],
            taps,
            head_row,
            skip_row,
        )

    def across(away):
        return swap(away, "group", 1)

    lines_count = groups // 2
    lane = lax.axis_index("group") & 1

    def joined(keep, got):
        return join(own_arg, keep, got).reshape(lines_count, -1, width)

    grad_ssm, grad_gates, gated, grad_inner, gate_out = gate_grads(
        own_arg,
        [(scan[7], scan[0], scan[4]) for scan in scans],
        stats,
        normed_all,
        gain_row,
        tok_count // chunk,
        lines_count,
    )
    half_gate = along.scatter(gate_out.reshape(groups, -1, width))
    gated = [after(g, gate_out) for g in gated]
    away_out = weight_grad(own_arg, gated, cot_all, inner, False)
    with jax.named_scope("away_out"):
        got_out = across(away_out)
    gated = [after(g, away_out) for g in gated]
    keep_out = weight_grad(own_arg, gated, cot_all, inner, True)
    backs = [scan_back(0, keep_out)]
    half_out = joined(keep_out, after(got_out, backs[0][0]))
    with jax.named_scope("trade_gate"):
        trade = Trade(own_arg, after(half_gate, half_out), parts)
    for m in range(1, micro):
        backs.append(scan_back(m, half_out, trade.sent))
    with jax.named_scope("trade_gate"):
        trade.middle(backs[-1][0])
        gate_cols = trade.final()
    left = [after(b[0], gate_cols) for b in backs]
    away_x = weight_grad(own_arg, left, normed_all, inner, False)
    with jax.named_scope("away_heads"):
        got_x = across(away_x)
    left = [after(b[0], away_x) for b in backs]
    keep_x = weight_grad(own_arg, left, normed_all, inner, True)
    half_out = along.scatter(half_out, lines())
    gate_lines = along.gather(after(gate_cols, away_x), lines())

    into = []
    for m in range(micro):
        grad_gate = after(grad_gates[m], keep_x, *(part[0] for part in into[-1:]))
        into.append(project_into(own_arg, grad_gate, *backs[m][:2], weights, tails))
    half_x = joined(keep_x, after(got_x, into[-1][0]))
    with jax.named_scope("gate_lines"):
        got_lines = across(after(gate_lines, half_x))
    rights = [after(n, half_x) for n in normed_all]
    tail_part = tail_grad(own_arg, [b[0] for b in backs], [b[1] for b in backs], rights, parts)

    def split(pair, name):
        with jax.named_scope(name):
            return Split(own_arg, [after(part, half_x) for part in pair])

    into = [split(pair, "into") for pair in into]
    tail_part = split(tail_part, "tail")
    with jax.named_scope("into"):
        sent = [part.middle() for part in into]
    with jax.named_scope("tail"):
        sent.append(tail_part.middle())
    keep, got = tail_part.final(*sent)
    steps = [keep + got.astype(F32)]
    with jax.named_scope("tail"):
        grad_tail = summed(steps[0], "group", BF16, True, steps)
    mixed = []
    for m in range(micro):
        gained = after(scans[m][8], steps[0], *sent, *(pair[0] for pair in mixed[-1:]))
        mixed.append(project_out(own_arg, gained, out_weight, parts))
    half_x = along.scatter(half_x, lines())
    with jax.named_scope("trade_heads"):
        trade = Trade(own_arg, after(half_x, mixed[-1][0]), parts)
    out_pin = mixed[-1][0]
    sent = trade.sent
    grad_tok = []
    grad_norm = jnp.zeros((width,), F32)
    for m in range(micro):
        terms = into[m].final(sent, got_lines, *(steps[2:3] if m else []))
        tok, gain = norm_rows(own_arg, tokens[m, 0], cotangent[m, 0], gain_norm, terms)
        grad_tok.append(tok)
        grad_norm += gain[0]
        if m == 0:
            with jax.named_scope("trade_heads"):
                sent = trade.middle(tok)
    with jax.named_scope("trade_heads"):
        x_cols = trade.final(tok)
    grad_taps = sum(b[2] for b in backs)[: CONV + 1]
    grad_skip = sum(b[3] for b in backs)[0]
    grad_head = sum(b[4] for b in backs)
    taps_all = lax.dynamic_update_slice_in_dim(
        jnp.zeros((CONV + 1, XBC), F32), grad_taps[:, :inner], own * inner, 1
    )
    taps_all = taps_all.at[:, INNER:].set(grad_taps[:, inner:])
    with jax.named_scope("small"):
        joint = summed(jnp.concatenate([taps_all.reshape(-1), grad_norm]), "fsdp")
    skip_sum = jnp.sum(grad_skip.reshape(heads, HEADDIM), axis=1)
    joint = jnp.concatenate(
        [joint, grad_inner[0], grad_head[0, :heads], grad_head[1, :heads], skip_sum]
    )

    with jax.named_scope("small"):
        joint = summed(joint, "group")
    out_lines = along.gather(after(half_out, out_pin), lines())
    with jax.named_scope("out_lines"):
        got_out = across(after(out_lines, joint, grad_tail))
    x_all = along.gather(after(x_cols, joint, grad_tail))
    with jax.named_scope("mixed"):
        mixed = [Split(own_arg, [after(part, x_cols) for part in pair]) for pair in mixed]
        for part in mixed:
            part.middle()

    def all_lines(value):
        return value.reshape(lines_count, 2, parts, -1, rows)

    whole = fill_lines(own_arg, None, after(gate_lines, x_cols), True)
    whole = fill_lines(own_arg, whole, after(got_lines, x_cols), False)
    whole = fill_tail(own_arg, whole, grad_tail)
    grad_out = jnp.stack(
        [
            jnp.where(lane == 0, out_lines, got_out),
            jnp.where(lane == 0, got_out, out_lines),
        ]
    )
    grad_out = grad_out.reshape(inner, width).astype(F32)

    for m in range(micro):
        stat = lax.dynamic_slice_in_dim(
            stats[m][:, 0].reshape(seq), own * tok_count, tok_count, 0
        )
        scale = lax.rsqrt(stat * (1.0 / INNER) + EPSILON)[:, None]
        mixed[m] = mixed_rows(own_arg, tokens[m, 0], scale, mixed[m].final(whole))

    at = (CONV + 1) * XBC
    share = XBC // parts
    taps_all = lax.dynamic_slice_in_dim(joint[:at].reshape(CONV + 1, XBC), own * share, share, 1)
    grad_norm = lax.dynamic_slice_in_dim(joint, at + own * rows, rows, 0)
    at += width
    grad_inner = joint[at : at + inner]
    at += inner
    grad_bias, grad_rate, grad_skip = (
        joint[at + k * heads : at + (k + 1) * heads] for k in range(3)
    )
    mixed = jnp.stack(mixed)[:, None]
    grad_tok = jnp.stack(grad_tok)[:, None]
    x_all = after(x_all, whole, grad_out, grad_norm, mixed, grad_tok)
    grad_in = fill_heads(own_arg, whole, all_lines(x_all), INNER).T
    return (
        mixed,
        grad_tok,
        grad_norm,
        grad_in,
        taps_all[:CONV],
        taps_all[CONV],
        grad_bias,
        grad_rate,
        grad_skip,
        grad_inner,
        grad_out,
    )


def solution(mesh):
    rows = P(None, "group", "fsdp", None)
    shard = P("fsdp")
    in_specs = (rows, P(None, "group", "fsdp"), rows, shard, P("fsdp", None), P(None, "fsdp"))
    in_specs += (shard,) * 5 + (P("fsdp", None),)
    out_specs = (rows, rows, shard, P("fsdp", None), P(None, "fsdp")) + (shard,) * 5
    out_specs += (P("fsdp", None),)
    return jax.shard_map(
        on_device, mesh=mesh, in_specs=in_specs, out_specs=out_specs, check_vma=False
    )
```
